32 devices in a mesh: grp: 2 (over y), seq: 4 (over z), head: 4 (over x, core).
Axes of the slice: x: 2, y: 2, z: 4, core: 2. Of those that a mesh axis runs over, the one named last changes fastest.
Arguments:
- q_heads: bfloat16 [8, 64, 16384], P('head', None, ('grp', 'seq')), parts along dimension 2, may hold values from -12 to 12
- k_heads: bfloat16 [8, 64, 16384], P('head', None, ('grp', 'seq')), parts along dimension 2, may hold values from -10 to 10
- v_heads: bfloat16 [8, 64, 16384], P('head', None, ('grp', 'seq')), parts along dimension 2, may hold values from -10 to 10
- morton_order: int32 [8, 2048], P(('grp', 'seq')), parts along dimension 0, may hold values from 0 to 2047, each once within a row
- leaf_counts: int32 [64], P('grp'), parts along dimension 0, may hold values from 64 to 256, as said below
Outputs:
- attended: bfloat16 [8, 64, 16384], P('head', None, ('grp', 'seq')), parts along dimension 2
The draws below stay inside these ranges and needn't reach their ends.
There are 2 independent parts, one for each index of `grp`. The reference program is written for one: setup_inputs(seed, part) draws one part's arguments, and reference() takes and returns one part's arrays. A program takes and returns all parts, laid end to end along the dimension named above; each array names one. Nothing has to cross between parts.
Inputs may be any that keep to these rules, and one draw needn't show every extreme that they name: `morton_order`: each row holds every number of 0 .. 2047 once. `leaf_counts`: the valid points of a leaf are its first ones.
All inputs are finite; a program needn't handle non-finite values.
Results may differ from the reference program's by a relative error of at most 0.0021.
Values may be sent and summed in bfloat16 or wider, within the bound.
No kernel may reach another device: no remote copies, remote signals or barrier semaphores. Data moves between devices by JAX's collectives and lax.ppermute only.
A program may use at most 64 MiB of HBM per device.

```python
import math
import jax
import jax.numpy as jnp
from jax import lax

HEADS = 8
HEAD_SIZE = 64
LEAF_POINTS = 256
TOK_DEV = 2048
TOKENS = 8192
BLOCKS = 4


def multiscale(key):
    leaves = TOKENS // LEAF_POINTS
    scale_count = leaves.bit_length()
    field = jnp.zeros((HEADS, HEAD_SIZE, TOKENS), jnp.float32)
    for level_index in range(scale_count):
        pieces = max(leaves >> level_index, 1)
        coarse = jax.random.normal(jax.random.fold_in(key, 100 + level_index), (HEADS, HEAD_SIZE, pieces), jnp.float32)
        field = field + jnp.repeat(coarse, TOKENS // pieces, axis=2)
    return field / math.sqrt(scale_count)


def draw_q_heads(key, part):
    shape = (HEADS, HEAD_SIZE, TOKENS)
    smooth = multiscale(jax.random.fold_in(key, 15))
    rough = jax.random.normal(jax.random.fold_in(key, 13), shape, jnp.float32)
    values = 1.4 * rough + 0.9 * smooth
    return jnp.clip(values, -12.0, 12.0).astype(jnp.bfloat16)


def draw_k_heads(key, part):
    shape = (HEADS, HEAD_SIZE, TOKENS)
    smooth = multiscale(jax.random.fold_in(key, 16))
    rough = jax.random.normal(jax.random.fold_in(key, 12), shape, jnp.float32)
    values = 1.4 * rough + 0.9 * smooth
    return jnp.clip(values, -10.0, 10.0).astype(jnp.bfloat16)


def draw_v_heads(key, part):
    shape = (HEADS, HEAD_SIZE, TOKENS)
    smooth = multiscale(jax.random.fold_in(key, 32))
    rough = jax.random.normal(jax.random.fold_in(key, 31), shape, jnp.float32)
    values = 1.5 * rough + 1.5 * smooth
    return jnp.clip(values, -10.0, 10.0).astype(jnp.bfloat16)


def draw_leaf_counts(key, part):
    raw_counts = jax.random.randint(jax.random.fold_in(key, 41), (TOKENS // LEAF_POINTS,), LEAF_POINTS // 4, 2 * LEAF_POINTS, jnp.int32)
    return jnp.minimum(raw_counts, LEAF_POINTS).astype(jnp.int32)


def setup_inputs(seed: int = 0, part: int = 0) -> dict:
    streams_of = jax.random.split(jax.random.key(seed), 6)
    own_keys = jax.random.split(jax.random.fold_in(streams_of[5], part), 6)
    return {
        "q_heads": draw_q_heads(jax.random.fold_in(jax.random.fold_in(streams_of[5], part), 71), part),
        "k_heads": draw_k_heads(jax.random.fold_in(jax.random.fold_in(streams_of[5], part), 71), part),
        "v_heads": draw_v_heads(jax.random.fold_in(jax.random.fold_in(streams_of[5], part), 71), part),
        "morton_order": jax.vmap(lambda own: jax.random.permutation(own, TOK_DEV))(jax.random.split(own_keys[3], BLOCKS)).reshape((BLOCKS, TOK_DEV)).astype(jnp.int32),
        "leaf_counts": draw_leaf_counts(jax.random.fold_in(jax.random.fold_in(streams_of[5], part), 71), part),
    }


NEG_FILL = -1e+30

def valid_points(leaf_counts):
    slots = jnp.arange(LEAF_POINTS, dtype=jnp.int32)
    return (slots[None, :] < leaf_counts[:, None]).astype(jnp.float32).reshape(-1)

def pooled(values, group_len):
    new_shape = values.shape[:-1] + (values.shape[-1] // group_len, group_len)
    return lax.optimization_barrier(jnp.sum(values.reshape(new_shape), axis=-1, dtype=jnp.float32))

def sibling_rows(values, block_rows):
    new_shape = values.shape[:-1] + (values.shape[-1] // (2 * block_rows), 2, block_rows)
    return jnp.flip(values.reshape(new_shape), axis=-2).reshape(values.shape)

def near_field(query_rows, key_rows, value_rows, valid):
    leaves = TOKENS // LEAF_POINTS
    scale_multiplier = 1.0 / math.sqrt(HEAD_SIZE)
    key_pad = jnp.pad(key_rows, ((0, 0), (LEAF_POINTS, LEAF_POINTS))).reshape(HEAD_SIZE, leaves + 2, LEAF_POINTS)
    value_pad = jnp.pad(value_rows, ((0, 0), (LEAF_POINTS, LEAF_POINTS))).reshape(HEAD_SIZE, leaves + 2, LEAF_POINTS)
    valid_pad = jnp.pad(valid, (LEAF_POINTS, LEAF_POINTS)).reshape(leaves + 2, LEAF_POINTS)
    key_win = jnp.concatenate([key_pad[:, offset:offset + leaves] for offset in range(3)], axis=-1)
    value_win = jnp.concatenate([value_pad[:, offset:offset + leaves] for offset in range(3)], axis=-1)
    valid_win = jnp.concatenate([valid_pad[offset:offset + leaves] for offset in range(3)], axis=-1)
    group = math.gcd(leaves, 64)
    batches = leaves // group
    query_grp = jnp.moveaxis(query_rows.reshape(HEAD_SIZE, batches, group, LEAF_POINTS), 1, 0)
    key_grp = jnp.moveaxis(key_win.reshape(HEAD_SIZE, batches, group, 3 * LEAF_POINTS), 1, 0)
    value_grp = jnp.moveaxis(value_win.reshape(HEAD_SIZE, batches, group, 3 * LEAF_POINTS), 1, 0)
    valid_grp = valid_win.reshape(batches, group, 3 * LEAF_POINTS)

    def one_batch(pieces):
        query_piece, key_piece, value_piece, mask_piece = pieces
        logit_scores = jnp.einsum('dnq,dnk->nqk', query_piece.astype(jnp.float32), key_piece.astype(jnp.float32)) * scale_multiplier
        logit_scores = jnp.where(mask_piece[:, None, :] > 0, logit_scores, NEG_FILL)
        best_score = lax.optimization_barrier(jnp.max(logit_scores, axis=-1))
        weight_probs = jnp.exp(logit_scores - best_score[..., None])
        weight_sum = lax.optimization_barrier(jnp.sum(weight_probs, axis=-1))
        probabilities = weight_probs.astype(jnp.bfloat16)
        blended_sum = jnp.einsum('nqk,dnk->dnq', probabilities.astype(jnp.float32), value_piece.astype(jnp.float32))
        return (best_score, blended_sum, weight_sum)
    best_all, mixed_all, total_all = lax.map(one_batch, (query_grp, key_grp, value_grp, valid_grp))
    mixed_all = jnp.moveaxis(mixed_all, 0, 1).reshape(HEAD_SIZE, TOKENS)
    return (best_all.reshape(-1), mixed_all, total_all.reshape(-1))

def far_field(query_rows, key_rows, value_rows, valid, level_index):
    group_len = 2 ** level_index
    scale_multiplier = 1.0 / math.sqrt(HEAD_SIZE)
    mean_query = pooled(query_rows.astype(jnp.float32), group_len) / group_len
    key_sums = pooled(key_rows.astype(jnp.float32) * valid, group_len)
    value_sums = pooled(value_rows.astype(jnp.float32) * valid, group_len)
    masses = pooled(valid, group_len)
    block_groups = TOKENS // (group_len * LEAF_POINTS)
    far_mass = sibling_rows(masses, LEAF_POINTS)
    mean_keys = sibling_rows(key_sums, LEAF_POINTS) / jnp.maximum(far_mass, 1.0)
    distant_values = sibling_rows(value_sums, LEAF_POINTS)
    mass_rows = far_mass.reshape(block_groups, LEAF_POINTS)
    logit_scores = jnp.einsum('swj,swg->wjg', mean_query.reshape(HEAD_SIZE, block_groups, LEAF_POINTS), mean_keys.reshape(HEAD_SIZE, block_groups, LEAF_POINTS), precision=lax.Precision.HIGHEST) * scale_multiplier
    logit_scores = jnp.where(mass_rows[:, None, :] > 0, logit_scores, NEG_FILL)
    best_score = lax.optimization_barrier(jnp.max(logit_scores, axis=-1))
    weight_probs = jnp.exp(logit_scores - best_score[..., None])
    weight_sum = lax.optimization_barrier(jnp.sum(weight_probs * mass_rows[:, None, :], axis=-1))
    blended_sum = jnp.einsum('rto,pro->prt', weight_probs, distant_values.reshape(HEAD_SIZE, block_groups, LEAF_POINTS), precision=lax.Precision.HIGHEST)
    return (best_score.reshape(-1), blended_sum.reshape(HEAD_SIZE, -1), weight_sum.reshape(-1))

def reference(q_heads, k_heads, v_heads, morton_order, leaf_counts):
    offsets = (jnp.arange(morton_order.shape[0], dtype=jnp.int32) * TOK_DEV)[:, None]
    gather_index = (morton_order + offsets).reshape(-1).astype(jnp.int32)
    query_all = jnp.take(q_heads, gather_index, axis=2)
    key_all = jnp.take(k_heads, gather_index, axis=2)
    value_all = jnp.take(v_heads, gather_index, axis=2)
    valid = valid_points(leaf_counts)
    depth_all = (TOKENS // LEAF_POINTS).bit_length() - 1

    def one_head(pieces):
        query_rows, key_rows, value_rows = pieces
        near_best, near_mixed, near_total = near_field(query_rows, key_rows, value_rows, valid)
        far_terms = []
        for level_index in range(1, depth_all):
            far_terms.append((2 ** level_index, far_field(query_rows, key_rows, value_rows, valid, level_index)))
        best_score = near_best
        for group_len, term in far_terms:
            best_score = jnp.maximum(best_score, jnp.repeat(term[0], group_len))
        factor = jnp.exp(near_best - best_score)
        blended_sum = near_mixed * factor[None, :]
        weight_sum = near_total * factor
        for group_len, term in far_terms:
            factor = jnp.exp(jnp.repeat(term[0], group_len) - best_score)
            blended_sum = blended_sum + jnp.repeat(term[1], group_len, axis=-1) * factor[None, :]
            weight_sum = weight_sum + jnp.repeat(term[2], group_len) * factor
        return (blended_sum / weight_sum[None, :]).astype(jnp.bfloat16)
    return lax.map(one_head, (query_all, key_all, value_all))
```

```python
import functools
import math

import jax
import jax.numpy as jnp
from jax import lax
from jax.experimental import pallas as pl
from jax.experimental.pallas import tpu as pltpu
from jax.sharding import PartitionSpec as P

LEAF = 256
HEAD = 64
LANES = 128
MASKED = -1e30
F32 = jnp.float32
BF16 = jnp.bfloat16
LOG2E = math.log2(math.e)


def dot(a, b):
    return lax.dot_general(a, b, (((1,), (0,)), ((), ())), preferred_element_type=F32)


def iota(shape, dim):
    return lax.broadcasted_iota(jnp.int32, shape, dim)


def bits(cond):
    return jnp.where(cond, 1.0, 0.0).astype(BF16)


def split(x):
    hi = x.astype(BF16)
    return hi, (x - hi.astype(F32)).astype(BF16)


def one_hot(order_row, tokens):
    slots = iota((LEAF, LEAF), 0).astype(F32).astype(BF16)
    tiles = []
    for j in range(tokens // LEAF):
        rel = (order_row - j * LEAF).astype(F32).astype(BF16)
        tiles.append(jnp.where(slots == rel, jnp.ones((), BF16), jnp.zeros((), BF16)))
    return jnp.concatenate(tiles, axis=0)


def pool_matrix(group, first_row, rows):
    token = iota((LEAF, rows), 0)
    row = iota((LEAF, rows), 1)
    return bits(token // group + first_row == row)


def spread_matrix(group, first_row, rows):
    row = iota((rows, LEAF), 0)
    token = iota((rows, LEAF), 1)
    return bits(token // group + first_row == row)


def level_shape(level, tokens):
    group = 2**level
    rows = tokens // group
    return group, rows, max(min(rows, LEAF), LANES), max(rows // LEAF, 1)


def place(level, leaf, tokens):
    group, rows, block_rows, _ = level_shape(level, tokens)
    per_leaf = LEAF // group
    return (leaf * per_leaf) // block_rows, (leaf * per_leaf) % block_rows


def pooled(level, leaf_values, tokens):
    group, _, block_rows, blocks = level_shape(level, tokens)
    sums = [None] * blocks
    for leaf, values in enumerate(leaf_values):
        block, first = place(level, leaf, tokens)
        if LEAF // group == LANES:
            piece = dot(values, pool_matrix(group, 0, LANES))
            sums[block] = (
                piece if sums[block] is None else jnp.concatenate([sums[block], piece], axis=1)
            )
        else:
            piece = dot(values, pool_matrix(group, first, block_rows))
            sums[block] = piece if sums[block] is None else sums[block] + piece
    return sums


def coarse_pair(sums):
    keys, values, mass = sums[:LANES], sums[LANES : 2 * LANES], sums[2 * LANES :]
    means = keys / jnp.maximum(mass[:1], 1.0)
    hi, lo = split(means)
    pair_k = []
    pair_v = []
    v_hi, v_lo = split(values)
    for h in range(2):
        here = slice(h * HEAD, (h + 1) * HEAD)
        both = jnp.concatenate([hi[here], lo[here]], axis=0)
        pair_k.append(both.astype(F32).T.astype(BF16))
        pair_v += [v_hi[here], v_lo[here]]
    return pair_k, jnp.concatenate(pair_v + [mass.astype(BF16)], axis=0)


def kv_kernel(tokens, remote_levels, counts, order, k, v, k_rows, v_cols, kf1, vf1, kf2, vf2, *packs):
    rank = lax.axis_index("seq")
    leaves = tokens // LEAF
    joint = jnp.concatenate([k[...], v[...]], axis=0)
    lane = iota((2 * LANES, LEAF), 1)
    ones = jnp.ones((16, LEAF), BF16)
    masked = []
    for n in range(leaves):
        cols = slice(n * LEAF, (n + 1) * LEAF)
        got = dot(joint, one_hot(order[:, cols], tokens))
        got16 = got.astype(BF16)
        k_rows[cols, :] = got[:LANES].T.astype(BF16)
        v_cols[:, cols] = got16[LANES:]
        lane = iota((2 * LANES + 16, LEAF), 1)
        full = jnp.concatenate([got16, ones], axis=0)
        masked.append(
            jnp.where(lane < counts[rank * leaves + n], full.astype(F32), 0.0).astype(BF16)
        )
    for level, kf, vf in ((1, kf1, vf1), (2, kf2, vf2)):
        for block, sums in enumerate(pooled(level, masked, tokens)):
            pair_k, value = coarse_pair(sums)
            rows = slice(block * LEAF, (block + 1) * LEAF)
            for h in range(2):
                kf[h, rows, :] = pair_k[h]
            vf[:, rows] = value
    odd = rank % 2 == 1

    def halo(ref, leaf):
        rows = slice(leaf * LEAF, (leaf + 1) * LEAF)
        ref[0:LEAF, :] = k_rows[rows, :]
        for half in range(2):
            ref[LEAF + half * LANES : LEAF + (half + 1) * LANES, :] = v_cols[
                :, leaf * LEAF + half * LANES : leaf * LEAF + (half + 1) * LANES
            ]

    pair_ref, step_ref = packs[0], packs[1]

    @pl.when(odd)
    def _():
        halo(pair_ref, 0)
        halo(step_ref, leaves - 1)

    @pl.when(jnp.logical_not(odd))
    def _():
        halo(pair_ref, leaves - 1)
        halo(step_ref, 0)

    for index, level in enumerate(remote_levels):
        ref = pair_ref if index == 0 else packs[index + 1]
        at = 2 * LEAF if index == 0 else 0
        (sums,) = pooled(level, masked, tokens)
        pair_k, value = coarse_pair(sums)
        width = value.shape[1]
        for h in range(2):
            ref[at : at + width, :] = pair_k[h]
            at += width
        for piece in range(width // LANES):
            ref[at : at + value.shape[0], :] = value[:, piece * LANES : (piece + 1) * LANES]
            at += value.shape[0]


VALUE_ROWS = 4 * HEAD + 16


def pack_rows(index, tokens, level):
    width = level_shape(level, tokens)[2]
    rows = 2 * width + VALUE_ROWS * (width // LANES)
    return rows + (2 * LEAF if index == 0 else 0)


def key_counts(counts, first_leaf, leaves, per_leaf, rows):
    leaf = iota((rows, LANES), 0) // per_leaf
    out = jnp.zeros((rows, LANES), jnp.int32)
    for n in range(leaves):
        out = jnp.where(leaf == n, counts[first_leaf + n], out)
    return out


def empty_rows(counts, first_leaf, leaves, group, rows):
    per_leaf = LEAF // group
    start = (iota((rows, LANES), 0) % per_leaf) * group
    return start >= key_counts(counts, first_leaf, leaves, per_leaf, rows)


def far(kf, empty, value, query):
    count = query.shape[1]
    lane = iota(kf.shape, 1)
    mark = jnp.where((lane == HEAD) & empty, MASKED, 0.0)
    second = jnp.where(lane < HEAD, kf.astype(F32), mark).astype(BF16)
    left = jnp.concatenate([kf, second], axis=1)
    hi, lo = query[:HEAD], query[HEAD:]
    flag = bits(iota((HEAD, count), 0) == 0)
    scores = dot(left, jnp.concatenate([hi, hi, lo, flag], axis=0))
    top = jnp.max(scores, axis=0, keepdims=True).astype(BF16).astype(F32)
    w_hi, w_lo = split(jnp.exp2(scores - top))
    out = dot(
        jnp.concatenate([value, value], axis=1), jnp.concatenate([w_hi, w_lo], axis=0)
    )
    return top, out[:HEAD] + out[HEAD : 2 * HEAD], out[2 * HEAD :]


def to_spread(term):
    top, sums, totals = term
    count = sums.shape[1]
    row = iota((16, count), 0)
    t_hi, t_lo = split(totals)
    tail = jnp.where(
        row == 0, t_hi.astype(F32), jnp.where(row == 1, t_lo.astype(F32), jnp.broadcast_to(top, (16, count)))
    )
    hi, lo = split(sums)
    return jnp.concatenate([hi, lo, tail.astype(BF16)], axis=0)


def from_spread(x):
    tail = x[2 * HEAD :]
    return tail[2:3], x[:HEAD] + x[HEAD : 2 * HEAD], tail[0:1] + tail[1:2]


def near(q_cols, k_window, empty, v_window):
    keys = k_window.shape[0]
    lane = iota((keys, LANES), 1)
    mark = jnp.where((lane == 0) & empty, MASKED, 0.0).astype(BF16)
    left = jnp.concatenate([k_window, mark], axis=1)
    none = jnp.zeros((HEAD, LEAF), BF16)
    flag = bits(iota((LANES, 2 * LEAF), 0) == 0)
    right = jnp.concatenate(
        [
            jnp.concatenate([q_cols[:HEAD], none], axis=1),
            jnp.concatenate([none, q_cols[HEAD:]], axis=1),
            flag,
        ],
        axis=0,
    )
    scores = dot(left, right)
    top = jnp.max(scores, axis=0, keepdims=True)
    scale = LOG2E / math.sqrt(HEAD)
    weights = jnp.exp2((scores - top) * scale)
    totals = jnp.sum(weights, axis=0, keepdims=True)
    probs = weights.astype(BF16)
    out = []
    for h in range(2):
        cols = slice(h * LEAF, (h + 1) * LEAF)
        sums = dot(v_window[h * HEAD : (h + 1) * HEAD], probs[:, cols])
        out.append((top[:, cols] * scale, sums, totals[:, cols]))
    return out


def merge(terms):
    top = functools.reduce(jnp.maximum, [t[0] for t in terms])
    sums = totals = 0.0
    for t in terms:
        factor = jnp.exp2(t[0] - top)
        sums = sums + t[1] * factor
        totals = totals + t[2] * factor
    return top, sums, totals


def head_value(value, h):
    return jnp.concatenate(
        [value[h * 2 * HEAD : (h + 1) * 2 * HEAD], value[4 * HEAD :]], axis=0
    )


def leaf_empty(counts, leaf):
    return iota((LEAF, LANES), 0) >= counts[leaf]


def local_kernel(
    tokens, remote_levels, counts, order, q, k_rows, v_cols, kf1, vf1, kf2, vf2,
    sums_out, stat_out, q_ends, *rest
):
    queries_out, q_all = rest[:-1], rest[-1]
    rank = lax.axis_index("seq")
    leaves = tokens // LEAF
    first_leaf = rank * leaves
    joint = q[...]
    leaf_q = []
    for n in range(leaves):
        cols = slice(n * LEAF, (n + 1) * LEAF)
        got = dot(joint, one_hot(order[:, cols], tokens)).astype(BF16)
        q_all[:, cols] = got
        leaf_q.append(got)
    q_ends[:, :LEAF] = leaf_q[0]
    q_ends[:, LEAF:] = leaf_q[-1]

    def queries(level):
        factor = LOG2E / math.sqrt(HEAD) / 2**level
        out = []
        for sums in pooled(level, leaf_q, tokens):
            hi, lo = split(sums * factor)
            out.append(
                [
                    jnp.concatenate(
                        [hi[h * HEAD : (h + 1) * HEAD], lo[h * HEAD : (h + 1) * HEAD]], axis=0
                    )
                    for h in range(2)
                ]
            )
        return out

    for index, level in enumerate(remote_levels):
        (block,) = queries(level)
        for h in range(2):
            queries_out[index][h] = block[h]

    spread = {}
    for level, kf, vf in ((1, kf1, vf1), (2, kf2, vf2)):
        group, _, block_rows, blocks = level_shape(level, tokens)
        level_queries = queries(level)
        per_block = block_rows * group // LEAF
        for block in range(blocks):
            other = block ^ 1
            rows = slice(other * block_rows, (other + 1) * block_rows)
            empty = empty_rows(counts, first_leaf + other * per_block, per_block, group, block_rows)
            value = vf[:, rows]
            for h in range(2):
                spread[level, block, h] = to_spread(
                    far(kf[h, rows, :], empty, head_value(value, h), level_queries[block][h])
                )
    for n in range(leaves):
        cols = slice(n * LEAF, (n + 1) * LEAF)
        own = None
        if 0 < n < leaves - 1:
            window = slice((n - 1) * LEAF, (n + 2) * LEAF)
            empty = jnp.concatenate(
                [leaf_empty(counts, first_leaf + n + step) for step in (-1, 0, 1)], axis=0
            )
            own = near(q_all[:, cols], k_rows[window, :], empty, v_cols[:, window])
        for h in range(2):
            terms = []
            for level in (1, 2):
                block, first = place(level, n, tokens)
                group, _, block_rows, _ = level_shape(level, tokens)
                terms.append(
                    from_spread(dot(spread[level, block, h], spread_matrix(group, first, block_rows)))
                )
            if own is not None:
                terms.append(own[h])
            top, sums, totals = merge(terms)
            sums_out[h, :, cols] = sums
            stat_out[h, 0:1, cols] = top
            stat_out[h, 1:2, cols] = totals


def last_kernel(
    tokens, remote_levels, count, counts, sums_in, stat_in, q_ends, k_rows, v_cols, *rest
):
    levels = len(remote_levels)
    queries = rest[:levels]
    pair, step = rest[levels], rest[levels + 1]
    packs = rest[levels + 2 : -1]
    out = rest[-1]
    rank = lax.axis_index("seq")
    leaves = tokens // LEAF
    odd = rank % 2 == 1

    def halo(ref):
        return ref[0:LEAF, :], jnp.concatenate(
            [ref[LEAF : LEAF + LANES, :], ref[LEAF + LANES : 2 * LEAF, :]], axis=1
        )

    pair_k, pair_v = halo(pair)
    step_k, step_v = halo(step)
    ends = {}
    for side, leaf, reach, shown in ((0, 0, -1, odd), (1, leaves - 1, 1, jnp.logical_not(odd))):
        flag = jnp.where(shown, 1, 0)
        out_k = jnp.where(flag == 1, pair_k.astype(F32), step_k.astype(F32)).astype(BF16)
        out_v = jnp.where(flag == 1, pair_v.astype(F32), step_v.astype(F32)).astype(BF16)
        inner = leaf - reach
        far_leaf = rank * leaves + leaf + reach
        there = jnp.logical_and(far_leaf >= 0, far_leaf < count * leaves)
        held = jnp.where(there, counts[jnp.clip(far_leaf, 0, count * leaves - 1)], 0)
        row = iota((LEAF, LANES), 0)
        ends[leaf] = near(
            q_ends[:, side * LEAF : (side + 1) * LEAF],
            jnp.concatenate(
                [out_k, k_rows[leaf * LEAF : (leaf + 1) * LEAF, :], k_rows[inner * LEAF : (inner + 1) * LEAF, :]],
                axis=0,
            ),
            jnp.concatenate(
                [
                    row >= held,
                    leaf_empty(counts, rank * leaves + leaf),
                    leaf_empty(counts, rank * leaves + inner),
                ],
                axis=0,
            ),
            jnp.concatenate(
                [out_v, v_cols[:, leaf * LEAF : (leaf + 1) * LEAF], v_cols[:, inner * LEAF : (inner + 1) * LEAF]],
                axis=1,
            ),
        )

    spread = {}
    used = 0
    for index, level in enumerate(remote_levels):
        group, _, width, _ = level_shape(level, tokens)
        kf = [[], []]
        empty = []
        values = []
        for partner in range(2**index, 2 ** (index + 1)):
            ref = pair if index == 0 else packs[used]
            used += 0 if index == 0 else 1
            at = 2 * LEAF if index == 0 else 0
            for h in range(2):
                kf[h].append(ref[at : at + width, :])
                at += width
            for piece in range(width // LANES):
                values.append(ref[at : at + VALUE_ROWS, :])
                at += VALUE_ROWS
            empty.append(empty_rows(counts, (rank ^ partner) * leaves, leaves, group, width))
        value = jnp.concatenate(values, axis=1)
        none = jnp.concatenate(empty, axis=0)
        for h in range(2):
            spread[index, h] = to_spread(
                far(jnp.concatenate(kf[h], axis=0), none, head_value(value, h), queries[index][h])
            )
    for n in range(leaves):
        cols = slice(n * LEAF, (n + 1) * LEAF)
        for h in range(2):
            terms = [(stat_in[h, 0:1, cols], sums_in[h, :, cols], stat_in[h, 1:2, cols])]
            for index, level in enumerate(remote_levels):
                group, _, width, _ = level_shape(level, tokens)
                _, first = place(level, n, tokens)
                terms.append(from_spread(dot(spread[index, h], spread_matrix(group, first, width))))
            if n in ends:
                terms.append(ends[n][h])
            _, sums, totals = merge(terms)
            out[h, :, cols] = (sums / totals).astype(BF16)


VMEM = pl.BlockSpec(memory_space=pltpu.VMEM)
SMEM = pl.BlockSpec(memory_space=pltpu.SMEM)


def params():
    return pltpu.CompilerParams(vmem_limit_bytes=48 * 2**20)


def head_pair(q, k, v, order, counts):
    tokens = q.shape[2]
    count = lax.axis_size("seq")
    local_depth = (tokens // LEAF).bit_length() - 1
    depth = (tokens * count // LEAF).bit_length() - 1
    remote = tuple(range(local_depth, depth))
    flat = (2 * HEAD, tokens)
    shape = jax.ShapeDtypeStruct
    pack_shapes = [shape((pack_rows(i, tokens, level), LANES), BF16) for i, level in enumerate(remote)]
    step_shape = shape((2 * LEAF, LANES), BF16)
    coarse_shapes = []
    for level in (1, 2):
        rows = tokens // 2**level
        coarse_shapes += [shape((2, rows, LANES), BF16), shape((VALUE_ROWS, rows), BF16)]
    outs = [shape((tokens, 2 * HEAD), BF16), shape(flat, BF16)] + coarse_shapes
    outs += [pack_shapes[0], step_shape] + pack_shapes[1:]
    made = pl.pallas_call(
        functools.partial(kv_kernel, tokens, remote),
        out_shape=outs,
        in_specs=[SMEM, VMEM, VMEM, VMEM],
        out_specs=[VMEM] * len(outs),
        compiler_params=params(),
        cost_estimate=pl.CostEstimate(flops=2 * 256 * tokens * tokens, bytes_accessed=4 * 2**20, transcendentals=0),
        name="gather_keys",
    )(counts, order, k.reshape(flat), v.reshape(flat))
    k_rows, v_cols = made[:2]
    coarse = made[2:6]
    pair, step = made[6:8]
    packs = made[8:]

    got_pair = lax.ppermute(pair, "seq", [(i, i ^ 1) for i in range(count)])
    swaps = []
    for i in range(1, count - 1, 2):
        swaps += [(i, i + 1), (i + 1, i)]
    got_step = lax.ppermute(step, "seq", swaps) if swaps else jnp.zeros_like(step)
    got = []
    for index in range(1, len(remote)):
        for partner in range(2**index, 2 ** (index + 1)):
            got.append(
                lax.ppermute(packs[index - 1], "seq", [(i, i ^ partner) for i in range(count)])
            )

    query_shapes = [shape((2, 2 * HEAD, level_shape(level, tokens)[2]), BF16) for level in remote]
    local_outs = [
        shape((2, HEAD, tokens), F32),
        shape((2, 2, tokens), F32),
        shape((2 * HEAD, 2 * LEAF), BF16),
    ] + query_shapes
    local = pl.pallas_call(
        functools.partial(local_kernel, tokens, remote),
        out_shape=local_outs,
        in_specs=[SMEM] + [VMEM] * 8,
        out_specs=[VMEM] * len(local_outs),
        scratch_shapes=[pltpu.VMEM(flat, BF16)],
        compiler_params=params(),
        cost_estimate=pl.CostEstimate(
            flops=2 * 128 * tokens * tokens + 2**31, bytes_accessed=8 * 2**20, transcendentals=2**22
        ),
        name="local_attention",
    )(counts, order, q.reshape(flat), k_rows, v_cols, *coarse)
    sums, stats, q_ends = local[:3]
    queries = local[3:]
    return pl.pallas_call(
        functools.partial(last_kernel, tokens, remote, count),
        out_shape=shape((2, HEAD, tokens), BF16),
        in_specs=[SMEM] + [VMEM] * (7 + len(queries) + len(got)),
        out_specs=VMEM,
        compiler_params=params(),
        cost_estimate=pl.CostEstimate(flops=2**30, bytes_accessed=4 * 2**20, transcendentals=2**20),
        name="remote_attention",
    )(counts, sums, stats, q_ends, k_rows, v_cols, *queries, got_pair, got_step, *got)


def shards(q, k, v, order, counts):
    heads = q.shape[0]
    if heads % 2:
        q, k, v = (jnp.concatenate([x, jnp.zeros_like(x[:1])], axis=0) for x in (q, k, v))
    out = [
        head_pair(q[h : h + 2], k[h : h + 2], v[h : h + 2], order, counts)
        for h in range(0, q.shape[0], 2)
    ]
    out = out[0] if len(out) == 1 else jnp.concatenate(out, axis=0)
    return out[:heads] if heads % 2 else out


def solution(mesh):
    placed = (
        P("head", None, ("grp", "seq")),
        P("head", None, ("grp", "seq")),
        P("head", None, ("grp", "seq")),
        P(("grp", "seq"), None),
        P("grp"),
    )
    return jax.shard_map(
        shards,
        mesh=mesh,
        in_specs=placed,
        out_specs=P("head", None, ("grp", "seq")),
        check_vma=False,
    )
```

```python
import functools
import math

import jax
import jax.numpy as jnp
from jax import lax
from jax.experimental import pallas as pl
from jax.experimental.pallas import tpu as pltpu
from jax.sharding import PartitionSpec as P

LEAF = 256
HEAD = 64
LANES = 128
MASKED = -1e30
F32 = jnp.float32
BF16 = jnp.bfloat16
SCALE = math.log2(math.e) / math.sqrt(HEAD)
SENT = BF16
TERMS = 2


def dot(a, b):
    return lax.dot_general(a, b, (((1,), (0,)), ((), ())), preferred_element_type=F32)


def iota(shape, dim):
    return lax.broadcasted_iota(jnp.int32, shape, dim)


def bits(cond):
    return jnp.where(cond, 1.0, 0.0).astype(BF16)


def split(x, terms=2):
    out = []
    for _ in range(terms - 1):
        out.append(x.astype(BF16))
        x = x - out[-1].astype(F32)
    return out + [x.astype(BF16)]


def encode(x):
    return split(x, TERMS)


def decode(terms):
    return functools.reduce(jnp.add, [t.astype(F32) for t in terms])


def one_hot(order_row, tokens):
    high = order_row // LEAF
    low = (order_row - high * LEAF).astype(F32).astype(BF16)
    slots = iota((LEAF, LEAF), 0).astype(F32).astype(BF16)
    base = jnp.where(slots == low, jnp.ones((), BF16), jnp.zeros((), BF16))
    return jnp.concatenate([base * bits(high == j) for j in range(tokens // LEAF)], axis=0)


def pool_matrix(group, first_row, rows):
    return bits(iota((LEAF, rows), 0) // group + first_row == iota((LEAF, rows), 1))


def pool_rows(group, first_row, rows):
    return bits(iota((rows, LEAF), 1) // group + first_row == iota((rows, LEAF), 0))


def level_shape(level, tokens):
    group = 2**level
    rows = tokens // group
    return group, max(min(rows, LEAF), LANES), max(rows // LEAF, 1)


def place(level, leaf, tokens):
    group, rows, _ = level_shape(level, tokens)
    per_leaf = LEAF // group
    return (leaf * per_leaf) // rows, (leaf * per_leaf) % rows


def pooled_cols(level, leaf_values, tokens):
    group, rows, blocks = level_shape(level, tokens)
    sums = [None] * blocks
    for leaf, values in enumerate(leaf_values):
        block, first = place(level, leaf, tokens)
        if LEAF // group == LANES:
            piece = dot(values, pool_matrix(group, 0, LANES))
            old = sums[block]
            sums[block] = piece if old is None else jnp.concatenate([old, piece], axis=1)
        else:
            piece = dot(values, pool_matrix(group, first, rows))
            sums[block] = piece if sums[block] is None else sums[block] + piece
    return sums


def pooled_rows(level, leaf_values, tokens):
    group, rows, blocks = level_shape(level, tokens)
    per_leaf = LEAF // group
    sums = [None] * blocks
    for leaf, values in enumerate(leaf_values):
        block, first = place(level, leaf, tokens)
        old = sums[block]
        if per_leaf % 16 == 0:
            piece = dot(pool_rows(group, 0, per_leaf), values)
            sums[block] = piece if old is None else jnp.concatenate([old, piece], axis=0)
        else:
            piece = dot(pool_rows(group, first, rows), values)
            sums[block] = piece if old is None else old + piece
    return sums


def mass(counts, first_leaf, leaves, group, shape, dim):
    row = iota(shape, dim)
    per_leaf = LEAF // group
    leaf = row // per_leaf
    held = jnp.zeros(shape, jnp.int32)
    for n in range(leaves):
        held = jnp.where(leaf == n, counts[first_leaf + n], held)
    return jnp.clip(held - (row % per_leaf) * group, 0, group)


def near_marks(empty):
    return jnp.where((iota(empty.shape, 1) == 0) & empty, MASKED, 0.0).astype(BF16)


def far_marks(empty):
    return jnp.where((iota(empty.shape, 1) == HEAD) & empty, MASKED, 0.0)


def by_head(both):
    turned = pltpu.roll(both, HEAD, 1)
    return (both, turned), (turned, both)


def far_keys(means, mark):
    hi, lo = split(means)
    hi_left, _ = by_head(hi.astype(F32))
    _, lo_right = by_head(lo.astype(F32))
    lane = iota(mark.shape, 1) < HEAD
    out = []
    for h in range(2):
        both = jnp.where(lane, hi_left[h], lo_right[h]).astype(BF16)
        once = jnp.where(lane, hi_left[h], mark).astype(BF16)
        out.append(jnp.concatenate([both, once], axis=1))
    return out


def far_values(sums, mass_rows):
    hi, lo = split(sums.T)
    return [
        jnp.concatenate([hi[h * HEAD : (h + 1) * HEAD], lo[h * HEAD : (h + 1) * HEAD], mass_rows], axis=0)
        for h in range(2)
    ]


def near_scores(k_window, mark, query):
    none = jnp.zeros((HEAD, LEAF), BF16)
    right = jnp.concatenate(
        [
            jnp.concatenate([query[:HEAD], none], axis=1),
            jnp.concatenate([none, query[HEAD:]], axis=1),
            bits(iota((LANES, 2 * LEAF), 0) == 0),
        ],
        axis=0,
    )
    left = jnp.concatenate([k_window, mark], axis=1)
    return [dot(left[i * LEAF : (i + 1) * LEAF], right) for i in range(3)]


def near(scores, v_window, h):
    scores = [piece[:, h * LEAF : (h + 1) * LEAF] for piece in scores]
    top = functools.reduce(jnp.maximum, [jnp.max(x, axis=0, keepdims=True) for x in scores])
    sums = totals = 0.0
    for i, piece in enumerate(scores):
        weights = jnp.exp2((piece - top) * SCALE)
        totals = totals + jnp.sum(weights, axis=0, keepdims=True)
        value = v_window[h * HEAD : (h + 1) * HEAD, i * LEAF : (i + 1) * LEAF]
        sums = sums + dot(value, weights.astype(BF16))
    return top * SCALE, sums, totals


def far_scores(keys, query):
    hi, lo = query[:HEAD], query[HEAD:]
    flag = bits(iota((HEAD, query.shape[1]), 0) == 0)
    return dot(keys, jnp.concatenate([hi, hi, lo, flag], axis=0))


def far(scores, value):
    top = jnp.max(scores, axis=0, keepdims=True).astype(BF16).astype(F32)
    w_hi, w_lo = split(jnp.exp2(scores - top))
    out = dot(jnp.concatenate([value, value], axis=1), jnp.concatenate([w_hi, w_lo], axis=0))
    return top, out[:HEAD] + out[HEAD : 2 * HEAD], out[2 * HEAD : 2 * HEAD + 1]


def staggered(units):
    held = None
    for first, second in units:
        scores = first()
        if held is not None:
            held[0](held[1])
        held = (second, scores)
    held[0](held[1])


def to_spread(term):
    top, sums, totals = term
    row = iota((16, sums.shape[1]), 0)
    t_hi, t_lo = split(totals)
    tail = jnp.where(row == 0, t_hi.astype(F32), jnp.where(row == 1, t_lo.astype(F32), top))
    hi, lo = split(sums)
    return jnp.concatenate([hi, lo, tail.astype(BF16)], axis=0)


def spread(rows, times, first, width):
    size = (rows.shape[1], width)
    x = dot(rows, bits(iota(size, 0) == iota(size, 1) // times + first))
    tail = x[2 * HEAD :]
    return tail[2:3], x[:HEAD] + x[HEAD : 2 * HEAD], tail[0:1] + tail[1:2]


def merge(terms):
    top = functools.reduce(jnp.maximum, [t[0] for t in terms])
    sums = totals = 0.0
    for t in terms:
        factor = jnp.exp2(t[0] - top)
        sums = sums + t[1] * factor
        totals = totals + t[2] * factor
    return top, sums, totals


def halo_rows():
    return 2 * LEAF


def pack_rows(index, tokens, level):
    rows = 2 * TERMS * level_shape(level, tokens)[1]
    return rows + (halo_rows() if index == 0 else 0)


def kv_kernel(
    tokens, remote, counts_in, order_in, k_in, v_in, kv_rows, v_cols, order, *rest
):
    packs, (counts, k, v, sems) = rest[: len(remote) + 1], rest[len(remote) + 1 :]
    copies = [
        pltpu.make_async_copy(source, target, sems.at[i])
        for i, (source, target) in enumerate(
            ((order_in, order), (k_in, k), (v_in, v), (counts_in, counts))
        )
    ]
    for copy in copies:
        copy.start()
    for copy in copies:
        copy.wait()
    rank = lax.axis_index("seq")
    leaves = tokens // LEAF
    joint = jnp.concatenate([k[...], v[...]], axis=0)
    masked = []
    for n in range(leaves):
        cols = slice(n * LEAF, (n + 1) * LEAF)
        got = dot(joint, one_hot(order[:, cols], tokens)).astype(BF16)
        rows = got.T
        kv_rows[cols, :] = rows
        v_cols[:, cols] = got[LANES:]
        held = iota((LEAF, 2 * LANES), 0) < counts[rank * leaves + n]
        masked.append(jnp.where(held, rows.astype(F32), 0.0).astype(BF16))
    odd = rank % 2 == 1
    pair, step = packs[:2]

    def halo(ref, leaf):
        rows = slice(leaf * LEAF, (leaf + 1) * LEAF)
        ref[0:LEAF, :] = kv_rows[rows, :LANES]
        for half in range(2):
            at = leaf * LEAF + half * LANES
            ref[LEAF + half * LANES : LEAF + (half + 1) * LANES, :] = v_cols[:, at : at + LANES]

    @pl.when(odd)
    def _():
        halo(pair, 0)
        halo(step, leaves - 1)

    @pl.when(jnp.logical_not(odd))
    def _():
        halo(pair, leaves - 1)
        halo(step, 0)

    for index, level in enumerate(remote):
        ref = pair if index == 0 else packs[index + 1]
        at = halo_rows() if index == 0 else 0
        group, rows, _ = level_shape(level, tokens)
        (sums,) = pooled_rows(level, masked, tokens)
        weight = mass(counts, rank * leaves, leaves, group, (rows, LANES), 0).astype(F32)
        means = sums[:, :LANES] / jnp.maximum(weight, 1.0)
        for term in encode(means) + encode(sums[:, LANES:] * (1.0 / group)):
            ref[at : at + rows, :] = term
            at += rows


def local_kernel(tokens, remote, counts_in, q, order, kv_rows, v_cols, *rest):
    levels = len(remote)
    near_out, near_stat, far_out, far_stat, q_ends, end_marks = rest[:6]
    rest = rest[6:]
    queries_out, marks_out, mass_out = rest[:levels], rest[levels : 2 * levels], rest[2 * levels : 3 * levels]
    counts, sem, mark = rest[3 * levels :]
    copy = pltpu.make_async_copy(counts_in, counts, sem)
    copy.start()
    rank = lax.axis_index("seq")
    count = lax.axis_size("seq")
    leaves = tokens // LEAF
    first_leaf = rank * leaves
    joint = q[...]
    copy.wait()
    masked = []
    for n in range(leaves):
        rows = slice(n * LEAF, (n + 1) * LEAF)
        mark[rows, :] = near_marks(iota((LEAF, LANES), 0) >= counts[first_leaf + n])
        held = iota((LEAF, 2 * LANES), 0) < counts[first_leaf + n]
        masked.append(jnp.where(held, kv_rows[rows, :].astype(F32), 0.0).astype(BF16))
    leaf_q = [None] * leaves

    def gather(n):
        cols = slice(n * LEAF, (n + 1) * LEAF)
        leaf_q[n] = dot(joint, one_hot(order[:, cols], tokens)).astype(BF16)

    def near_unit(n):
        cols = slice(n * LEAF, (n + 1) * LEAF)
        window = slice((n - 1) * LEAF, (n + 2) * LEAF)

        def first():
            gather(n)
            return near_scores(kv_rows[window, :LANES], mark[window, :], leaf_q[n])

        def second(scores):
            for h in range(2):
                top, sums, totals = near(scores, v_cols[:, window], h)
                near_out[h, :, cols] = sums
                near_stat[h, 0:1, cols] = top
                near_stat[h, 1:2, cols] = totals

        return first, second

    gather(0)
    gather(leaves - 1)
    staggered([near_unit(n) for n in range(1, leaves - 1)])
    q_ends[:, :LEAF] = leaf_q[0]
    q_ends[:, LEAF:] = leaf_q[-1]

    def queries(level):
        out = []
        for sums in pooled_cols(level, leaf_q, tokens):
            hi, lo = split(sums * (SCALE / 2**level))
            out.append(
                [
                    jnp.concatenate([x[h * HEAD : (h + 1) * HEAD] for x in (hi, lo)], axis=0)
                    for h in range(2)
                ]
            )
        return out

    for index, level in enumerate(remote):
        (block,) = queries(level)
        for h in range(2):
            queries_out[index][h] = block[h]

    results = {}
    units = []
    for level in (2, 1):
        group, rows, blocks = level_shape(level, tokens)
        per_block = rows * group // LEAF
        level_queries = queries(level)
        for block, sums in enumerate(pooled_rows(level, masked, tokens)):
            start = first_leaf + block * per_block
            weight = mass(counts, start, per_block, group, (rows, LANES), 0)
            lanes = mass(counts, start, per_block, group, (16, rows), 1)
            keys = far_keys(
                sums[:, :LANES] / jnp.maximum(weight.astype(F32), 1.0), far_marks(weight == 0)
            )
            values = far_values(sums[:, LANES:], lanes.astype(F32).astype(BF16))
            for h in range(2):
                query = level_queries[block ^ 1][h]

                def second(scores, at=(level, block ^ 1, h), value=values[h]):
                    results[at] = far(scores, value)

                units.append((functools.partial(far_scores, keys[h], query), second))
    staggered(units)
    for block in range(level_shape(1, tokens)[2]):
        cols = slice(block * LEAF, (block + 1) * LEAF)
        for h in range(2):
            coarse = to_spread(results[2, block // 2, h])
            top, sums, totals = merge(
                [results[1, block, h], spread(coarse, 2, (block % 2) * LANES, LEAF)]
            )
            far_out[h, :, cols] = sums
            far_stat[h, 0:1, cols] = top
            far_stat[h, 1:2, cols] = totals

    for side, leaf in ((0, first_leaf - 1), (1, first_leaf + leaves)):
        there = jnp.logical_and(leaf >= 0, leaf < count * leaves)
        held = jnp.where(there, counts[jnp.clip(leaf, 0, count * leaves - 1)], 0)
        end_marks[side, :LEAF] = near_marks(iota((LEAF, LANES), 0) >= held)
        inner = side * (leaves - 2) * LEAF
        end_marks[side, LEAF:] = mark[inner : inner + 2 * LEAF, :]
    for index, level in enumerate(remote):
        group, rows, _ = level_shape(level, tokens)
        for i in range(2**index):
            start = (rank ^ (2**index + i)) * leaves
            at = slice(i * rows, (i + 1) * rows)
            weight = mass(counts, start, leaves, group, (rows, LANES), 0)
            marks_out[index][at, :] = far_marks(weight == 0)
            lanes = mass(counts, start, leaves, group, (16, rows), 1)
            mass_out[index][:, at] = lanes.astype(F32).astype(BF16)


def last_kernel(
    tokens, remote, near_in, near_stat, far_in, far_stat, q_ends, end_marks, kv_rows, v_cols, *rest
):
    levels = len(remote)
    queries, marks_in, mass_in = rest[:levels], rest[levels : 2 * levels], rest[2 * levels : 3 * levels]
    pair, step = rest[3 * levels : 3 * levels + 2]
    packs = rest[3 * levels + 2 : -3]
    out, stage, sems = rest[-3:]
    rank = lax.axis_index("seq")
    leaves = tokens // LEAF
    flag = jnp.where(rank % 2 == 1, 1, 0)
    ends = {}
    results = {}

    def near_unit(side):
        own = flag if side == 0 else 1 - flag
        inner = slice(side * (leaves - 2) * LEAF, (side * (leaves - 2) + 2) * LEAF)

        def chosen(at):
            here = pair[at, :].astype(F32)
            there = step[at, :].astype(F32)
            return jnp.where(own == 1, here, there).astype(BF16)

        def first():
            return near_scores(
                jnp.concatenate([chosen(slice(0, LEAF)), kv_rows[inner, :LANES]], axis=0),
                end_marks[side],
                q_ends[:, side * LEAF : (side + 1) * LEAF],
            )

        def second(scores):
            halves = [chosen(slice(LEAF + i * LANES, LEAF + (i + 1) * LANES)) for i in range(2)]
            window = jnp.concatenate(halves + [v_cols[:, inner]], axis=1)
            for h in range(2):
                ends[side * (leaves - 1), h] = near(scores, window, h)

        return first, second

    def far_units(index):
        level = remote[index]
        group, rows, _ = level_shape(level, tokens)
        fields = [[], []]
        for i in range(2**index):
            ref = pair if index == 0 else packs[2**index - 2 + i]
            at = halo_rows() if index == 0 else 0
            for field in fields:
                field.append(decode([ref[at + t * rows : at + (t + 1) * rows, :] for t in range(TERMS)]))
                at += TERMS * rows
        means, sums = [jnp.concatenate(field, axis=0) for field in fields]
        keys = far_keys(means, marks_in[index][...])
        values = far_values(sums * group, mass_in[index][...])
        units = []
        for h in range(2):

            def second(scores, h=h):
                results[index, h] = far(scores, values[h])

            units.append((functools.partial(far_scores, keys[h], queries[index][h]), second))
        return units

    units = [near_unit(0), near_unit(1)]
    for index in range(levels):
        units += far_units(index)
    staggered(units)

    coarse = []
    for h in range(2):
        merged = results[levels - 1, h]
        for index in reversed(range(levels - 1)):
            rows = level_shape(remote[index], tokens)[1]
            merged = merge([results[index, h], spread(to_spread(merged), 2, 0, rows)])
        coarse.append(to_spread(merged))
    step_rows = LEAF // 2 ** (remote[0] - 1)
    copies = []
    for block in range(leaves // 2):
        far_cols = slice(block * LEAF, (block + 1) * LEAF)
        for h in range(2):
            far_term = merge(
                [
                    (far_stat[h, 0:1, far_cols], far_in[h, :, far_cols], far_stat[h, 1:2, far_cols]),
                    spread(coarse[h], 2 ** (remote[0] - 1), block * step_rows, LEAF),
                ]
            )
            fine = to_spread(far_term)
            for part in range(2):
                n = 2 * block + part
                cols = slice(n * LEAF, (n + 1) * LEAF)
                if (n, h) in ends:
                    near_term = ends[n, h]
                else:
                    near_term = (near_stat[h, 0:1, cols], near_in[h, :, cols], near_stat[h, 1:2, cols])
                _, sums, totals = merge([near_term, spread(fine, 2, part * LANES, LEAF)])
                stage[h, :, cols] = (sums / totals).astype(BF16)
        cols = slice(2 * block * LEAF, 2 * (block + 1) * LEAF)
        copies.append(
            pltpu.make_async_copy(stage.at[:, :, cols], out.at[:, :, cols], sems.at[block])
        )
        copies[-1].start()
    for copy in copies:
        copy.wait()


VMEM = pl.BlockSpec(memory_space=pltpu.VMEM)
HBM = pl.BlockSpec(memory_space=pl.ANY)


def params():
    return pltpu.CompilerParams(vmem_limit_bytes=48 * 2**20)


def head_pair(q, k, v, order, counts):
    tokens = q.shape[2]
    leaves = tokens // LEAF
    count = lax.axis_size("seq")
    depth = (tokens * count // LEAF).bit_length() - 1
    remote = tuple(range(leaves.bit_length() - 1, depth))
    flat = (2 * HEAD, tokens)
    shape = jax.ShapeDtypeStruct
    outs = [
        shape((tokens, 4 * HEAD), BF16),
        shape(flat, BF16),
        shape((1, tokens), jnp.int32),
        shape((pack_rows(0, tokens, remote[0]), LANES), SENT),
        shape((halo_rows(), LANES), SENT),
    ] + [shape((pack_rows(i, tokens, remote[i]), LANES), SENT) for i in range(1, len(remote))]
    made = pl.pallas_call(
        functools.partial(kv_kernel, tokens, remote),
        out_shape=outs,
        in_specs=[HBM] * 4,
        out_specs=[VMEM] * len(outs),
        scratch_shapes=[
            pltpu.SMEM(counts.shape, jnp.int32),
            pltpu.VMEM(flat, BF16),
            pltpu.VMEM(flat, BF16),
            pltpu.SemaphoreType.DMA((4,)),
        ],
        compiler_params=params(),
        cost_estimate=pl.CostEstimate(
            flops=2 * 256 * tokens * tokens, bytes_accessed=4 * 2**20, transcendentals=0
        ),
        name="gather_keys",
    )(*(pltpu.with_memory_space_constraint(x, pltpu.HBM) for x in (counts, order, k.reshape(flat), v.reshape(flat))))
    kv_rows, v_cols, order_here, pair, step = made[:5]
    packs = made[5:]

    got_pair = lax.ppermute(pair, "seq", [(i, i ^ 1) for i in range(count)])
    swaps = []
    for i in range(1, count - 1, 2):
        swaps += [(i, i + 1), (i + 1, i)]
    got_step = lax.ppermute(step, "seq", swaps) if swaps else jnp.zeros_like(step)
    got = []
    for index in range(1, len(remote)):
        for partner in range(2**index, 2 ** (index + 1)):
            got.append(
                lax.ppermute(packs[index - 1], "seq", [(i, i ^ partner) for i in range(count)])
            )

    widths = [level_shape(level, tokens)[1] for level in remote]
    local_outs = (
        [
            shape((2, HEAD, tokens), F32),
            shape((2, 2, tokens), F32),
            shape((2, HEAD, tokens // 2), F32),
            shape((2, 2, tokens // 2), F32),
            shape((2 * HEAD, 2 * LEAF), BF16),
            shape((2, 3 * LEAF, LANES), BF16),
        ]
        + [shape((2, 2 * HEAD, width), BF16) for width in widths]
        + [shape((2**i * width, LANES), F32) for i, width in enumerate(widths)]
        + [shape((16, 2**i * width), BF16) for i, width in enumerate(widths)]
    )
    local = pl.pallas_call(
        functools.partial(local_kernel, tokens, remote),
        out_shape=local_outs,
        in_specs=[HBM] + [VMEM] * 4,
        out_specs=[VMEM] * len(local_outs),
        scratch_shapes=[
            pltpu.SMEM(counts.shape, jnp.int32),
            pltpu.SemaphoreType.DMA(()),
            pltpu.VMEM((tokens, LANES), BF16),
        ],
        compiler_params=params(),
        cost_estimate=pl.CostEstimate(
            flops=2 * 128 * tokens * tokens + 2**31, bytes_accessed=8 * 2**20, transcendentals=2**22
        ),
        name="local_attention",
    )(counts, q.reshape(flat), order_here, kv_rows, v_cols)
    return pl.pallas_call(
        functools.partial(last_kernel, tokens, remote),
        out_shape=shape((2, HEAD, tokens), BF16),
        in_specs=[VMEM] * (len(local) + 4 + len(got)),
        out_specs=HBM,
        scratch_shapes=[
            pltpu.VMEM((2, HEAD, tokens), BF16),
            pltpu.SemaphoreType.DMA((leaves // 2,)),
        ],
        compiler_params=params(),
        cost_estimate=pl.CostEstimate(flops=2**30, bytes_accessed=4 * 2**20, transcendentals=2**20),
        name="remote_attention",
    )(*local[:6], kv_rows, v_cols, *local[6:], got_pair, got_step, *got)


def shards(q, k, v, order, counts):
    heads = q.shape[0]
    if heads % 2:
        q, k, v = (jnp.concatenate([x, jnp.zeros_like(x[:1])], axis=0) for x in (q, k, v))
    out = [
        head_pair(q[h : h + 2], k[h : h + 2], v[h : h + 2], order, counts)
        for h in range(0, q.shape[0], 2)
    ]
    out = out[0] if len(out) == 1 else jnp.concatenate(out, axis=0)
    return out[:heads] if heads % 2 else out


def solution(mesh):
    placed = (
        P("head", None, ("grp", "seq")),
        P("head", None, ("grp", "seq")),
        P("head", None, ("grp", "seq")),
        P(("grp", "seq"), None),
        P("grp"),
    )
    return jax.shard_map(
        shards,
        mesh=mesh,
        in_specs=placed,
        out_specs=P("head", None, ("grp", "seq")),
        check_vma=False,
    )
```

```python
import functools
import math

import jax
import jax.numpy as jnp
from jax import lax
from jax.experimental import pallas as pl
from jax.experimental.pallas import tpu as pltpu
from jax.sharding import PartitionSpec as P

LEAF = 256
HEAD = 64
LANES = 128
MASKED = -1e30
F32 = jnp.float32
BF16 = jnp.bfloat16
SCALE = math.log2(math.e) / math.sqrt(HEAD)
SENT = jnp.int16
CODE = 32000.0
PIECE = 4 * HEAD + 16


def dot(a, b):
    return lax.dot_general(a, b, (((1,), (0,)), ((), ())), preferred_element_type=F32)


def iota(shape, dim):
    return lax.broadcasted_iota(jnp.int32, shape, dim)


def bits(cond):
    return jnp.where(cond, 1.0, 0.0).astype(BF16)


def split(x, terms=2):
    out = []
    for _ in range(terms - 1):
        out.append(x.astype(BF16))
        x = x - out[-1].astype(F32)
    return out + [x.astype(BF16)]


def encode(keys, values):
    parts = []
    row = iota((16, keys.shape[1]), 0)
    exponents = jnp.zeros(row.shape, F32)
    for i, x in enumerate((keys, values)):
        largest = jnp.max(jnp.abs(x), axis=0, keepdims=True)
        exponent = jnp.floor(jnp.log2(jnp.maximum(largest, 2.0**-100))) + 1.0
        parts.append(jnp.round(x * (jnp.exp2(-exponent) * CODE)))
        exponents = jnp.where(row == i, exponent, exponents)
    codes = jnp.concatenate(parts + [exponents], axis=0).astype(jnp.int32).astype(SENT)
    return [codes[:, i : i + LANES] for i in range(0, codes.shape[1], LANES)]


def put(ref, at, pieces):
    for piece in pieces:
        ref[at : at + PIECE, :] = piece
        at += PIECE


def decode(ref, at, width):
    pieces = [ref[at + i * PIECE : at + (i + 1) * PIECE, :] for i in range(width // LANES)]
    x = jnp.concatenate(pieces, axis=1).astype(jnp.int32).astype(F32)
    scales = jnp.exp2(x[4 * HEAD :]) * (1.0 / CODE)
    return x[: 2 * HEAD] * scales[0:1], x[2 * HEAD : 4 * HEAD] * scales[1:2]


def one_hot(order_row, tokens):
    high = order_row // LEAF
    low = (order_row - high * LEAF).astype(F32).astype(BF16)
    slots = iota((LEAF, LEAF), 0).astype(F32).astype(BF16)
    base = jnp.where(slots == low, jnp.ones((), BF16), jnp.zeros((), BF16))
    return jnp.concatenate([base * bits(high == j) for j in range(tokens // LEAF)], axis=0)


def pool_rows(group, first_row, rows):
    return bits(iota((rows, LEAF), 1) // group + first_row == iota((rows, LEAF), 0))


def level_shape(level, tokens):
    group = 2**level
    rows = tokens // group
    return group, max(min(rows, LEAF), LANES), max(rows // LEAF, 1)


def place(level, leaf, tokens):
    group, rows, _ = level_shape(level, tokens)
    per_leaf = LEAF // group
    return (leaf * per_leaf) // rows, (leaf * per_leaf) % rows


def pooled(levels, leaf_values, tokens):
    sums = {}
    whole = [level for level in levels if LEAF // 2**level % 16 == 0]
    parts = [pool_rows(2**level, 0, LEAF // 2**level) for level in whole]
    for leaf, values in enumerate(leaf_values):
        both = dot(jnp.concatenate(parts, axis=0), values)
        at = 0
        for level in whole:
            count = LEAF // 2**level
            block, _ = place(level, leaf, tokens)
            sums.setdefault((level, block), []).append(both[at : at + count])
            at += count
    out = {at: jnp.concatenate(pieces, axis=0) for at, pieces in sums.items()}
    for level in levels:
        if level in whole:
            continue
        group, rows, _ = level_shape(level, tokens)
        for leaf, values in enumerate(leaf_values):
            block, first = place(level, leaf, tokens)
            piece = dot(pool_rows(group, first, rows), values)
            out[level, block] = out[level, block] + piece if leaf else piece
    return out


def mass(counts, first_leaf, leaves, group, rows):
    row = iota((16, rows), 1)
    per_leaf = LEAF // group
    leaf = row // per_leaf
    held = jnp.zeros(row.shape, jnp.int32)
    for n in range(leaves):
        held = jnp.where(leaf == n, counts[first_leaf + n], held)
    return jnp.clip(held - (row % per_leaf) * group, 0, group).astype(F32)


def valid_only(kv_rows, held):
    keep = bits(iota((LEAF, LANES), 0) < held)
    return kv_rows * jnp.concatenate([keep, keep], axis=1)


def near_marks(empty):
    return jnp.where((iota(empty.shape, 1) == 0) & empty, MASKED, 0.0).astype(BF16)


def far_keys(means, weight):
    hi, lo = split(means)
    mark = jnp.where((iota(weight.shape, 0) == 0) & (weight == 0.0), MASKED, 0.0).astype(BF16)
    rest = jnp.zeros((HEAD - 16, hi.shape[1]), BF16)
    out = []
    for h in range(2):
        here = slice(h * HEAD, (h + 1) * HEAD)
        out.append(
            jnp.concatenate([hi[here], lo[here], hi[here], mark, rest], axis=0).T
        )
    return out


def far_values(sums, mass_rows):
    hi, lo = split(sums)
    mass_rows = mass_rows.astype(BF16)
    return [
        jnp.concatenate([hi[h * HEAD : (h + 1) * HEAD], lo[h * HEAD : (h + 1) * HEAD], mass_rows], axis=0)
        for h in range(2)
    ]


def near_scores(k_window, mark, query):
    none = jnp.zeros((HEAD, LEAF), BF16)
    right = jnp.concatenate(
        [
            jnp.concatenate([query[:HEAD], none], axis=1),
            jnp.concatenate([none, query[HEAD:]], axis=1),
            bits(iota((LANES, 2 * LEAF), 0) == 0),
        ],
        axis=0,
    )
    left = jnp.concatenate([k_window, mark], axis=1)
    return [dot(left[i * LEAF : (i + 1) * LEAF], right) for i in range(3)]


def near(scores, v_window, h):
    scores = [piece[:, h * LEAF : (h + 1) * LEAF] for piece in scores]
    top = functools.reduce(jnp.maximum, [jnp.max(x, axis=0, keepdims=True) for x in scores])
    sums = totals = 0.0
    for i, piece in enumerate(scores):
        weights = jnp.exp2((piece - top) * SCALE)
        totals = totals + jnp.sum(weights, axis=0, keepdims=True)
        value = v_window[h * HEAD : (h + 1) * HEAD, i * LEAF : (i + 1) * LEAF]
        sums = sums + dot(value, weights.astype(BF16))
    return top * SCALE, sums, totals


def far_scores(keys, query):
    hi, lo = query[:HEAD], query[HEAD:]
    flag = bits(iota((HEAD, query.shape[1]), 0) == 0)
    return dot(keys, jnp.concatenate([hi, hi, lo, flag], axis=0))


def far(scores, value):
    top = jnp.max(scores, axis=0, keepdims=True).astype(BF16).astype(F32)
    w_hi, w_lo = split(jnp.exp2(scores - top))
    out = dot(jnp.concatenate([value, value], axis=1), jnp.concatenate([w_hi, w_lo], axis=0))
    return top, out[:HEAD] + out[HEAD : 2 * HEAD], out[2 * HEAD : 2 * HEAD + 1]


def staggered(units, ahead=1):
    held = []
    for first, second in units:
        held.append((second, first()))
        if len(held) > ahead:
            second, scores = held.pop(0)
            second(scores)
    for second, scores in held:
        second(scores)


def to_spread(term):
    top, sums, totals = term
    row = iota((16, sums.shape[1]), 0)
    t_hi, t_lo = split(totals)
    tail = jnp.where(row == 0, t_hi.astype(F32), jnp.where(row == 1, t_lo.astype(F32), top))
    hi, lo = split(sums)
    return jnp.concatenate([hi, lo, tail.astype(BF16)], axis=0)


def spread_matrix(times, first, width=LEAF):
    size = (LANES, width)
    return bits(iota(size, 0) == iota(size, 1) // times + first)


def spread(rows, matrix):
    x = dot(rows, matrix)
    tail = x[2 * HEAD :]
    return tail[2:3], x[:HEAD] + x[HEAD : 2 * HEAD], tail[0:1] + tail[1:2]


def merge(terms):
    top = functools.reduce(jnp.maximum, [t[0] for t in terms])
    sums = totals = 0.0
    for t in terms:
        factor = jnp.exp2(t[0] - top)
        sums = sums + t[1] * factor
        totals = totals + t[2] * factor
    return top, sums, totals


def halo_rows():
    return LEAF // LANES * PIECE


def joined(tokens, step):
    return step.shape[0] > halo_rows()


def pack_rows(index, tokens, level):
    rows = level_shape(level, tokens)[1] // LANES * PIECE
    return rows + (halo_rows() if index == 0 else 0)


def kv_kernel(
    tokens, remote, counts_in, order_in, k_in, v_in, q_in, kv_rows, v_cols, q_cols, pair, step, *rest
):
    packs, (counts, order, k, v, q, sems) = rest[: len(remote) - 1], rest[len(remote) - 1 :]
    copies = [
        pltpu.make_async_copy(source, target, sems.at[i])
        for i, (source, target) in enumerate(
            ((order_in, order), (k_in, k), (v_in, v), (q_in, q), (counts_in, counts))
        )
    ]
    for copy in copies:
        copy.start()
    for copy in copies:
        copy.wait()
    rank = lax.axis_index("seq")
    leaves = tokens // LEAF
    joint = jnp.concatenate([k[...], v[...], q[...]], axis=0)
    masked = []
    ends = {}
    for n in range(leaves):
        cols = slice(n * LEAF, (n + 1) * LEAF)
        got = dot(joint, one_hot(order[:, cols], tokens))
        got16 = got.astype(BF16)
        rows = got16[: 2 * LANES].T
        q_cols[:, cols] = got16[2 * LANES :]
        kv_rows[cols, :] = rows
        v_cols[:, cols] = got16[LANES : 2 * LANES]
        if n in (0, leaves - 1):
            ends[n] = got
        masked.append(valid_only(rows, counts[rank * leaves + n]))
    odd = rank % 2 == 1

    @pl.when(odd)
    def _():
        put(pair, 0, encode(ends[0][:LANES], ends[0][LANES : 2 * LANES]))
        put(step, 0, encode(ends[leaves - 1][:LANES], ends[leaves - 1][LANES : 2 * LANES]))

    @pl.when(jnp.logical_not(odd))
    def _():
        put(pair, 0, encode(ends[leaves - 1][:LANES], ends[leaves - 1][LANES : 2 * LANES]))
        put(step, 0, encode(ends[0][:LANES], ends[0][LANES : 2 * LANES]))

    sums = pooled(remote, masked, tokens)
    for index, level in enumerate(remote):
        codes = coarse_codes(counts, rank, level, sums[level, 0], tokens)
        if index == 0:
            put(pair, halo_rows(), codes)
        else:
            put(packs[index - 1], 0, codes)
        if index == 1 and joined(tokens, step):
            put(step, halo_rows(), codes)


def coarse_codes(counts, rank, level, sums, tokens):
    group, rows, _ = level_shape(level, tokens)
    leaves = tokens // LEAF
    weight = mass(counts, rank * leaves, leaves, group, rows)[:1]
    sums = sums.T
    return encode(sums[:LANES] / jnp.maximum(weight, 1.0), sums[LANES:])


def local_kernel(tokens, remote, counts_in, q_cols, kv_rows, v_cols, *rest):
    levels = len(remote)
    sums_out, stat_out, end_marks, matrices = rest[:4]
    queries_out, mass_out = rest[4 : 4 + levels], rest[4 + levels : 4 + 2 * levels]
    counts, sem, mark = rest[4 + 2 * levels :]
    copy = pltpu.make_async_copy(counts_in, counts, sem)
    copy.start()
    rank = lax.axis_index("seq")
    count = lax.axis_size("seq")
    leaves = tokens // LEAF
    first_leaf = rank * leaves
    copy.wait()
    near_terms = {}
    for n in range(leaves):
        rows = slice(n * LEAF, (n + 1) * LEAF)
        mark[rows, :] = near_marks(iota((LEAF, LANES), 0) >= counts[first_leaf + n])

    def near_unit(n):
        cols = slice(n * LEAF, (n + 1) * LEAF)
        window = slice((n - 1) * LEAF, (n + 2) * LEAF)

        def first():
            return near_scores(kv_rows[window, :LANES], mark[window, :], q_cols[:, cols])

        def second(scores):
            for h in range(2):
                near_terms[n, h] = near(scores, v_cols[:, window], h)

        return first, second

    staggered([near_unit(n) for n in range(1, leaves - 1)])
    leaf_q = [q_cols[:, n * LEAF : (n + 1) * LEAF].T for n in range(leaves)]
    q_sums = pooled((1, 2) + tuple(remote), leaf_q, tokens)

    def queries(level, block):
        hi, lo = split(q_sums[level, block].T * (SCALE / 2**level))
        return [
            jnp.concatenate([x[h * HEAD : (h + 1) * HEAD] for x in (hi, lo)], axis=0)
            for h in range(2)
        ]

    masked = [
        valid_only(kv_rows[n * LEAF : (n + 1) * LEAF, :], counts[first_leaf + n])
        for n in range(leaves)
    ]
    kv_sums = pooled((1, 2), masked, tokens)
    results = {}
    units = []
    for level in (2, 1):
        group, rows, blocks = level_shape(level, tokens)
        per_block = rows * group // LEAF
        for block in range(blocks):
            weight = mass(counts, first_leaf + block * per_block, per_block, group, rows)
            sums = kv_sums[level, block].T
            keys = far_keys(sums[:LANES] / jnp.maximum(weight[:1], 1.0), weight)
            values = far_values(sums[LANES:], weight)
            query = queries(level, block ^ 1)
            for h in range(2):

                def second(scores, at=(level, block ^ 1, h), value=values[h]):
                    results[at] = far(scores, value)

                units.append((functools.partial(far_scores, keys[h], query[h]), second))
    staggered(units, 4)
    for index, level in enumerate(remote):
        block = queries(level, 0)
        for h in range(2):
            queries_out[index][h] = block[h]
    twice = spread_matrix(2, 0)
    matrices[0] = twice
    for j in range(4):
        matrices[j + 1] = spread_matrix(8, j * 32)
    for block in range(leaves // 2):
        for h in range(2):
            coarse = to_spread(results[2, block // 2, h])
            half = slice((block % 2) * LANES, (block % 2 + 1) * LANES)
            fine = to_spread(merge([results[1, block, h], spread(coarse[:, half], twice)]))
            for part in range(2):
                n = 2 * block + part
                cols = slice(n * LEAF, (n + 1) * LEAF)
                term = spread(fine[:, part * LANES : (part + 1) * LANES], twice)
                if 0 < n < leaves - 1:
                    term = merge([near_terms[n, h], term])
                stat_out[h, 0:1, cols], sums_out[h, :, cols], stat_out[h, 1:2, cols] = term

    row = iota((LEAF, LANES), 0)
    for side, leaf in ((0, first_leaf - 1), (1, first_leaf + leaves)):
        there = jnp.logical_and(leaf >= 0, leaf < count * leaves)
        held = jnp.where(there, counts[jnp.clip(leaf, 0, count * leaves - 1)], 0)
        end_marks[side, :LEAF] = near_marks(row >= held)
        for i in range(2):
            inner = first_leaf + side * (leaves - 2) + i
            end_marks[side, (i + 1) * LEAF : (i + 2) * LEAF] = near_marks(row >= counts[inner])
    for index, level in enumerate(remote):
        group, rows, _ = level_shape(level, tokens)
        for i in range(2**index):
            start = (rank ^ (2**index + i)) * leaves
            mass_out[index][:, i * rows : (i + 1) * rows] = mass(counts, start, leaves, group, rows)


def last_kernel(
    tokens, remote, q_cols, kv_rows, v_cols, sums_in, stat_in, end_marks, matrices, *rest
):
    levels = len(remote)
    queries, mass_in = rest[:levels], rest[levels : 2 * levels]
    pair, step = rest[2 * levels : 2 * levels + 2]
    packs = rest[2 * levels + 2 : -3]
    out, stage, sems = rest[-3:]
    rank = lax.axis_index("seq")
    leaves = tokens // LEAF
    flag = jnp.where(rank % 2 == 1, 1, 0)
    ends = {}
    results = {}

    halo_pair = decode(pair, 0, LEAF)
    halo_step = decode(step, 0, LEAF)

    def near_unit(side):
        own = flag if side == 0 else 1 - flag
        inner = slice(side * (leaves - 2) * LEAF, (side * (leaves - 2) + 2) * LEAF)
        keys, values = [
            jnp.where(own == 1, here, there).astype(BF16)
            for here, there in zip(halo_pair, halo_step)
        ]

        def first():
            return near_scores(
                jnp.concatenate([keys.T, kv_rows[inner, :LANES]], axis=0),
                end_marks[side],
                q_cols[:, side * (leaves - 1) * LEAF : (side * (leaves - 1) + 1) * LEAF],
            )

        def second(scores):
            window = jnp.concatenate([values, v_cols[:, inner]], axis=1)
            for h in range(2):
                ends[side * (leaves - 1), h] = near(scores, window, h)

        return first, second

    def far_units(index):
        level = remote[index]
        group, rows, _ = level_shape(level, tokens)
        if index == 0:
            fields = [decode(pair, halo_rows(), rows)]
        else:
            refs = [(packs[2**index - 2 + i], 0) for i in range(2**index - (index == 1 and joined(tokens, step)))]
            if index == 1 and joined(tokens, step):
                refs.append((step, halo_rows()))
            fields = [decode(ref, at, rows) for ref, at in refs]
        means, sums = [jnp.concatenate(field, axis=1) for field in zip(*fields)]
        keys = far_keys(means, mass_in[index][...])
        values = far_values(sums, mass_in[index][...])
        units = []
        for h in range(2):

            def second(scores, h=h):
                results[index, h] = far(scores, values[h])

            units.append((functools.partial(far_scores, keys[h], queries[index][h]), second))
        return units

    units = [near_unit(0), near_unit(1)]
    for index in range(levels):
        units += far_units(index)
    staggered(units, 2)

    coarse = []
    for h in range(2):
        merged = results[levels - 1, h]
        for index in reversed(range(levels - 1)):
            rows = level_shape(remote[index], tokens)[1]
            merged = merge(
                [results[index, h], spread(to_spread(merged)[:, :LANES], matrices[0, :, :rows])]
            )
        coarse.append(to_spread(merged))
    copies = []
    for n in range(leaves):
        cols = slice(n * LEAF, (n + 1) * LEAF)
        half = slice(n // 4 * LANES, (n // 4 + 1) * LANES)
        for h in range(2):
            terms = [
                (stat_in[h, 0:1, cols], sums_in[h, :, cols], stat_in[h, 1:2, cols]),
                spread(coarse[h][:, half], matrices[n % 4 + 1]),
            ]
            if (n, h) in ends:
                terms.append(ends[n, h])
            _, sums, totals = merge(terms)
            stage[h, :, cols] = (sums * (1.0 / totals)).astype(BF16)
        if n % 2:
            both = slice((n - 1) * LEAF, (n + 1) * LEAF)
            copies.append(
                pltpu.make_async_copy(stage.at[:, :, both], out.at[:, :, both], sems.at[n // 2])
            )
            copies[-1].start()
    for copy in copies:
        copy.wait()


VMEM = pl.BlockSpec(memory_space=pltpu.VMEM)
ANY = pl.BlockSpec(memory_space=pl.ANY)


def params():
    return pltpu.CompilerParams(vmem_limit_bytes=48 * 2**20)


def head_pair(q, k, v, order, counts):
    tokens = q.shape[2]
    leaves = tokens // LEAF
    count = lax.axis_size("seq")
    depth = (tokens * count // LEAF).bit_length() - 1
    remote = tuple(range(leaves.bit_length() - 1, depth))
    four = False
    flat = (2 * HEAD, tokens)
    shape = jax.ShapeDtypeStruct
    outs = [
        shape((tokens, 4 * HEAD), BF16),
        shape(flat, BF16),
        shape(flat, BF16),
        shape((pack_rows(0, tokens, remote[0]), LANES), SENT),
        shape((halo_rows() + (pack_rows(1, tokens, remote[1]) if four else 0), LANES), SENT),
    ] + [shape((pack_rows(i, tokens, remote[i]), LANES), SENT) for i in range(1, len(remote))]
    counts, order, k, v, q = (
        pltpu.with_memory_space_constraint(x, pltpu.HBM)
        for x in (counts, order, k.reshape(flat), v.reshape(flat), q.reshape(flat))
    )
    kv_rows, v_cols, q_cols, pair, step, *packs = pl.pallas_call(
        functools.partial(kv_kernel, tokens, remote),
        out_shape=outs,
        in_specs=[ANY] * 5,
        out_specs=[VMEM] * len(outs),
        scratch_shapes=[
            pltpu.SMEM(counts.shape, jnp.int32),
            pltpu.VMEM((1, tokens), jnp.int32),
            pltpu.VMEM(flat, BF16),
            pltpu.VMEM(flat, BF16),
            pltpu.VMEM(flat, BF16),
            pltpu.SemaphoreType.DMA((5,)),
        ],
        compiler_params=params(),
        cost_estimate=pl.CostEstimate(
            flops=2 * 256 * tokens * tokens, bytes_accessed=4 * 2**20, transcendentals=0
        ),
        name="gather_keys",
    )(counts, order, k, v, q)

    got_pair = lax.ppermute(pair, "seq", [(i, i ^ 1) for i in range(count)])
    got = []
    for index in range(1, len(remote)):
        for partner in range(2**index, 2 ** (index + 1)):
            if four and partner == 3:
                continue
            got.append(
                lax.ppermute(packs[index - 1], "seq", [(i, i ^ partner) for i in range(count)])
            )
    swaps = [(i, count - 1 - i) for i in range(count)] if four else []
    for i in range(1, count - 1, 2):
        swaps += [] if four else [(i, i + 1), (i + 1, i)]
    got_step = lax.ppermute(step, "seq", swaps) if swaps else jnp.zeros_like(step)

    widths = [level_shape(level, tokens)[1] for level in remote]
    outs = (
        [shape((2, HEAD, tokens), F32), shape((2, 2, tokens), F32)]
        + [shape((2, 3 * LEAF, LANES), BF16), shape((5, LANES, LEAF), BF16)]
        + [shape((2, 2 * HEAD, width), BF16) for width in widths]
        + [shape((16, 2**i * width), F32) for i, width in enumerate(widths)]
    )
    local = pl.pallas_call(
        functools.partial(local_kernel, tokens, remote),
        out_shape=outs,
        in_specs=[ANY] + [VMEM] * 3,
        out_specs=[VMEM] * len(outs),
        scratch_shapes=[
            pltpu.SMEM(counts.shape, jnp.int32),
            pltpu.SemaphoreType.DMA(()),
            pltpu.VMEM((tokens, LANES), BF16),
        ],
        compiler_params=params(),
        cost_estimate=pl.CostEstimate(flops=2**33, bytes_accessed=8 * 2**20, transcendentals=2**22),
        name="local_attention",
    )(counts, q_cols, kv_rows, v_cols)
    return pl.pallas_call(
        functools.partial(last_kernel, tokens, remote),
        out_shape=shape((2, HEAD, tokens), BF16),
        in_specs=[VMEM] * (5 + len(local) + len(got)),
        out_specs=ANY,
        scratch_shapes=[
            pltpu.VMEM((2, HEAD, tokens), BF16),
            pltpu.SemaphoreType.DMA((leaves // 2,)),
        ],
        compiler_params=params(),
        cost_estimate=pl.CostEstimate(flops=2**30, bytes_accessed=4 * 2**20, transcendentals=2**20),
        name="remote_attention",
    )(q_cols, kv_rows, v_cols, *local, got_pair, got_step, *got)


def shards(q, k, v, order, counts):
    heads = q.shape[0]
    if heads % 2:
        q, k, v = (jnp.concatenate([x, jnp.zeros_like(x[:1])], axis=0) for x in (q, k, v))
    out = [
        head_pair(q[h : h + 2], k[h : h + 2], v[h : h + 2], order, counts)
        for h in range(0, q.shape[0], 2)
    ]
    out = out[0] if len(out) == 1 else jnp.concatenate(out, axis=0)
    return out[:heads] if heads % 2 else out


def solution(mesh):
    placed = (
        P("head", None, ("grp", "seq")),
        P("head", None, ("grp", "seq")),
        P("head", None, ("grp", "seq")),
        P(("grp", "seq"), None),
        P("grp"),
    )
    return jax.shard_map(
        shards,
        mesh=mesh,
        in_specs=placed,
        out_specs=P("head", None, ("grp", "seq")),
        check_vma=False,
    )
```

```python
import functools
import math

import jax
import jax.numpy as jnp
from jax import lax
from jax.experimental import pallas as pl
from jax.experimental.pallas import tpu as pltpu
from jax.sharding import PartitionSpec as P

LEAF = 256
HEAD = 64
LANES = 128
MASKED = -1e30
F32 = jnp.float32
BF16 = jnp.bfloat16
SCALE = math.log2(math.e) / math.sqrt(HEAD)
SENT = jnp.int16
CODE = 32000.0
PIECE = 4 * HEAD + 16


def dot(a, b):
    return lax.dot_general(a, b, (((1,), (0,)), ((), ())), preferred_element_type=F32)


def iota(shape, dim):
    return lax.broadcasted_iota(jnp.int32, shape, dim)


def bits(cond):
    return jnp.where(cond, 1.0, 0.0).astype(BF16)


def split(x, terms=2):
    out = []
    for _ in range(terms - 1):
        out.append(x.astype(BF16))
        x = x - out[-1].astype(F32)
    return out + [x.astype(BF16)]


def encode(keys, values):
    parts = []
    row = iota((16, keys.shape[1]), 0)
    exponents = jnp.zeros(row.shape, F32)
    for i, x in enumerate((keys, values)):
        largest = jnp.max(jnp.abs(x), axis=0, keepdims=True)
        exponent = jnp.floor(jnp.log2(jnp.maximum(largest, 2.0**-100))) + 1.0
        parts.append(jnp.round(x * (jnp.exp2(-exponent) * CODE)))
        exponents = jnp.where(row == i, exponent, exponents)
    codes = jnp.concatenate(parts + [exponents], axis=0).astype(jnp.int32).astype(SENT)
    return [codes[:, i : i + LANES] for i in range(0, codes.shape[1], LANES)]


def put(ref, at, pieces):
    for piece in pieces:
        ref[at : at + PIECE, :] = piece
        at += PIECE


def decode(ref, at, width):
    pieces = [ref[at + i * PIECE : at + (i + 1) * PIECE, :] for i in range(width // LANES)]
    x = jnp.concatenate(pieces, axis=1).astype(jnp.int32).astype(F32)
    scales = jnp.exp2(x[4 * HEAD :]) * (1.0 / CODE)
    return x[: 2 * HEAD] * scales[0:1], x[2 * HEAD : 4 * HEAD] * scales[1:2]


def one_hot(order_row, tokens):
    high = order_row // LEAF
    low = (order_row - high * LEAF).astype(F32).astype(BF16)
    slots = iota((LEAF, LEAF), 0).astype(F32).astype(BF16)
    base = jnp.where(slots == low, jnp.ones((), BF16), jnp.zeros((), BF16))
    return jnp.concatenate([base * bits(high == j) for j in range(tokens // LEAF)], axis=0)


def pool_rows(group, first_row, rows):
    return bits(iota((rows, LEAF), 1) // group + first_row == iota((rows, LEAF), 0))


def level_shape(level, tokens):
    group = 2**level
    rows = tokens // group
    return group, max(min(rows, LEAF), LANES), max(rows // LEAF, 1)


def place(level, leaf, tokens):
    group, rows, _ = level_shape(level, tokens)
    per_leaf = LEAF // group
    return (leaf * per_leaf) // rows, (leaf * per_leaf) % rows


def pooled(levels, leaf_values, tokens):
    sums = {}
    whole = [level for level in levels if LEAF // 2**level % 16 == 0]
    parts = [pool_rows(2**level, 0, LEAF // 2**level) for level in whole]
    for leaf, values in enumerate(leaf_values):
        both = dot(jnp.concatenate(parts, axis=0), values)
        at = 0
        for level in whole:
            count = LEAF // 2**level
            block, _ = place(level, leaf, tokens)
            sums.setdefault((level, block), []).append(both[at : at + count])
            at += count
    out = {at: jnp.concatenate(pieces, axis=0) for at, pieces in sums.items()}
    for level in levels:
        if level in whole:
            continue
        group, rows, _ = level_shape(level, tokens)
        for leaf, values in enumerate(leaf_values):
            block, first = place(level, leaf, tokens)
            piece = dot(pool_rows(group, first, rows), values)
            out[level, block] = out[level, block] + piece if leaf else piece
    return out


def mass(counts, first_leaf, leaves, group, rows):
    row = iota((16, rows), 1)
    per_leaf = LEAF // group
    leaf = row // per_leaf
    held = jnp.zeros(row.shape, jnp.int32)
    for n in range(leaves):
        held = jnp.where(leaf == n, counts[first_leaf + n], held)
    return jnp.clip(held - (row % per_leaf) * group, 0, group).astype(F32)


def valid_only(kv_rows, held):
    keep = bits(iota((LEAF, LANES), 0) < held)
    return kv_rows * jnp.concatenate([keep, keep], axis=1)


def near_marks(empty):
    return jnp.where((iota(empty.shape, 1) == 0) & empty, MASKED, 0.0).astype(BF16)


def far_keys(means, weight):
    hi, lo = split(means)
    mark = jnp.where((iota(weight.shape, 0) == 0) & (weight == 0.0), MASKED, 0.0).astype(BF16)
    rest = jnp.zeros((HEAD - 16, hi.shape[1]), BF16)
    out = []
    for h in range(2):
        here = slice(h * HEAD, (h + 1) * HEAD)
        out.append(
            jnp.concatenate([hi[here], lo[here], hi[here], mark, rest], axis=0).T
        )
    return out


def far_values(sums, mass_rows):
    hi, lo = split(sums)
    mass_rows = mass_rows.astype(BF16)
    return [
        jnp.concatenate([hi[h * HEAD : (h + 1) * HEAD], lo[h * HEAD : (h + 1) * HEAD], mass_rows], axis=0)
        for h in range(2)
    ]


def near_scores(k_window, mark, query):
    none = jnp.zeros((HEAD, LEAF), BF16)
    right = jnp.concatenate(
        [
            jnp.concatenate([query[:HEAD], none], axis=1),
            jnp.concatenate([none, query[HEAD:]], axis=1),
            bits(iota((LANES, 2 * LEAF), 0) == 0),
        ],
        axis=0,
    )
    left = jnp.concatenate([k_window, mark], axis=1)
    return [dot(left[i * LEAF : (i + 1) * LEAF], right) for i in range(3)]


def near(scores, v_window, h):
    scores = [piece[:, h * LEAF : (h + 1) * LEAF] for piece in scores]
    top = functools.reduce(jnp.maximum, [jnp.max(x, axis=0, keepdims=True) for x in scores])
    sums = totals = 0.0
    for i, piece in enumerate(scores):
        weights = jnp.exp2((piece - top) * SCALE)
        totals = totals + jnp.sum(weights, axis=0, keepdims=True)
        value = v_window[h * HEAD : (h + 1) * HEAD, i * LEAF : (i + 1) * LEAF]
        sums = sums + dot(value, weights.astype(BF16))
    return top * SCALE, sums, totals


def far_scores(keys, query):
    hi, lo = query[:HEAD], query[HEAD:]
    flag = bits(iota((HEAD, query.shape[1]), 0) == 0)
    return dot(keys, jnp.concatenate([hi, hi, lo, flag], axis=0))


def far(scores, value):
    top = jnp.max(scores, axis=0, keepdims=True).astype(BF16).astype(F32)
    w_hi, w_lo = split(jnp.exp2(scores - top))
    out = dot(jnp.concatenate([value, value], axis=1), jnp.concatenate([w_hi, w_lo], axis=0))
    return top, out[:HEAD] + out[HEAD : 2 * HEAD], out[2 * HEAD : 2 * HEAD + 1]


def staggered(units, ahead=1):
    held = []
    for first, second in units:
        held.append((second, first()))
        if len(held) > ahead:
            second, scores = held.pop(0)
            second(scores)
    for second, scores in held:
        second(scores)


def to_spread(term):
    top, sums, totals = term
    row = iota((16, sums.shape[1]), 0)
    t_hi, t_lo = split(totals)
    tail = jnp.where(row == 0, t_hi.astype(F32), jnp.where(row == 1, t_lo.astype(F32), top))
    hi, lo = split(sums)
    return jnp.concatenate([hi, lo, tail.astype(BF16)], axis=0)


def spread_matrix(times, first, width=LEAF):
    size = (LANES, width)
    return bits(iota(size, 0) == iota(size, 1) // times + first)


def from_spread(x):
    tail = x[2 * HEAD :]
    return tail[2:3], x[:HEAD] + x[HEAD : 2 * HEAD], tail[0:1] + tail[1:2]


def merge(terms):
    top = functools.reduce(jnp.maximum, [t[0] for t in terms])
    sums = totals = 0.0
    for t in terms:
        factor = jnp.exp2(t[0] - top)
        sums = sums + t[1] * factor
        totals = totals + t[2] * factor
    return top, sums, totals


def halo_rows():
    return LEAF // LANES * PIECE


def pack_rows(index, tokens, level):
    rows = level_shape(level, tokens)[1] // LANES * PIECE
    return rows + (halo_rows() if index == 0 else 0)


def key_kernel(
    tokens, remote, counts_in, order_in, k_in, v_in, kv_rows, v_cols, order, other, pair, *rest
):
    sums_out, (counts, k, v, sems) = rest[: len(remote) - 1], rest[len(remote) - 1 :]
    copies = [
        pltpu.make_async_copy(source, target, sems.at[i])
        for i, (source, target) in enumerate(
            ((order_in, order), (k_in, k), (v_in, v), (counts_in, counts))
        )
    ]
    for copy in copies:
        copy.start()
    rank = lax.axis_index("seq")
    leaves = tokens // LEAF
    copies[0].wait()
    first = one_hot(order[:, :LEAF], tokens)
    for copy in copies[1:]:
        copy.wait()
    joint = jnp.concatenate([k[...], v[...]], axis=0)
    masked = []
    got = []
    for n in range(leaves):
        cols = slice(n * LEAF, (n + 1) * LEAF)
        got.append(dot(joint, one_hot(order[:, cols], tokens) if n else first).astype(BF16))
        rows = got[n].T
        kv_rows[cols, :] = rows
        v_cols[:, cols] = got[n][LANES:]
        masked.append(valid_only(rows, counts[rank * leaves + n]))
    odd = jnp.where(rank % 2 == 1, 1, 0)
    low, high = got[0].astype(F32), got[-1].astype(F32)
    halo = jnp.where(odd == 1, low, high)
    put(pair, 0, encode(halo[:LANES], halo[LANES:]))
    other[...] = jnp.where(odd == 1, high, low).astype(BF16)
    sums = pooled(remote, masked, tokens)
    put(pair, halo_rows(), coarse_codes(counts, rank, remote[0], sums[remote[0], 0], tokens))
    for ref, level in zip(sums_out, remote[1:]):
        ref[...] = sums[level, 0]


def pack_kernel(tokens, remote, counts_in, other, *rest):
    levels = len(remote) - 1
    sums, step, packs = rest[:levels], rest[levels], rest[levels + 1 : 2 * levels + 1]
    counts, sem = rest[2 * levels + 1 :]
    copy = pltpu.make_async_copy(counts_in, counts, sem)
    copy.start()
    rank = lax.axis_index("seq")
    halo = other[...].astype(F32)
    put(step, 0, encode(halo[:LANES], halo[LANES:]))
    copy.wait()
    for i, level in enumerate(remote[1:]):
        put(packs[i], 0, coarse_codes(counts, rank, level, sums[i][...], tokens))


def coarse_codes(counts, rank, level, sums, tokens):
    group, rows, _ = level_shape(level, tokens)
    leaves = tokens // LEAF
    weight = mass(counts, rank * leaves, leaves, group, rows)[:1]
    sums = sums.T
    return encode(sums[:LANES] / jnp.maximum(weight, 1.0), sums[LANES:])


def local_kernel(tokens, remote, counts_in, q, order, kv_rows, v_cols, q_cols, *rest):
    levels = len(remote)
    sums_out, stat_out, end_marks, matrices = rest[:4]
    queries_out, mass_out = rest[4 : 4 + levels], rest[4 + levels : 4 + 2 * levels]
    counts, sem, mark = rest[4 + 2 * levels :]
    copy = pltpu.make_async_copy(counts_in, counts, sem)
    copy.start()
    rank = lax.axis_index("seq")
    count = lax.axis_size("seq")
    leaves = tokens // LEAF
    first_leaf = rank * leaves
    for n in range(leaves):
        cols = slice(n * LEAF, (n + 1) * LEAF)
        q_cols[:, cols] = dot(q[...], one_hot(order[:, cols], tokens)).astype(BF16)
    copy.wait()
    near_terms = {}
    for n in range(leaves):
        rows = slice(n * LEAF, (n + 1) * LEAF)
        mark[rows, :] = near_marks(iota((LEAF, LANES), 0) >= counts[first_leaf + n])

    def near_unit(n):
        cols = slice(n * LEAF, (n + 1) * LEAF)
        window = slice((n - 1) * LEAF, (n + 2) * LEAF)

        def first():
            return near_scores(kv_rows[window, :LANES], mark[window, :], q_cols[:, cols])

        def second(scores):
            for h in range(2):
                near_terms[n, h] = near(scores, v_cols[:, window], h)

        return first, second

    staggered([near_unit(n) for n in range(1, leaves - 1)])
    leaf_q = [q_cols[:, n * LEAF : (n + 1) * LEAF].T for n in range(leaves)]
    q_sums = pooled((1, 2) + tuple(remote), leaf_q, tokens)

    def queries(level, block):
        hi, lo = split(q_sums[level, block].T * (SCALE / 2**level))
        return [
            jnp.concatenate([x[h * HEAD : (h + 1) * HEAD] for x in (hi, lo)], axis=0)
            for h in range(2)
        ]

    masked = [
        valid_only(kv_rows[n * LEAF : (n + 1) * LEAF, :], counts[first_leaf + n])
        for n in range(leaves)
    ]
    kv_sums = pooled((1, 2), masked, tokens)
    results = {}
    units = []
    for level in (2, 1):
        group, rows, blocks = level_shape(level, tokens)
        per_block = rows * group // LEAF
        for block in range(blocks):
            weight = mass(counts, first_leaf + block * per_block, per_block, group, rows)
            sums = kv_sums[level, block].T
            keys = far_keys(sums[:LANES] / jnp.maximum(weight[:1], 1.0), weight)
            values = far_values(sums[LANES:], weight)
            query = queries(level, block ^ 1)
            for h in range(2):

                def second(scores, at=(level, block ^ 1, h), value=values[h]):
                    results[at] = far(scores, value)

                units.append((functools.partial(far_scores, keys[h], query[h]), second))
    staggered(units, 4)
    for index, level in enumerate(remote):
        block = queries(level, 0)
        for h in range(2):
            queries_out[index][h] = block[h]
    twice = spread_matrix(2, 0)
    matrices[0] = twice
    for j in range(4):
        matrices[j + 1] = spread_matrix(8, j * 32)
    coarse = {at: to_spread(results[2, at[0], at[1]]) for at in ((b, h) for b in range(leaves // 4) for h in range(2))}
    fine = {}

    def join_unit(block, h):
        half = slice((block % 2) * LANES, (block % 2 + 1) * LANES)

        def second(x):
            fine[block, h] = to_spread(merge([results[1, block, h], from_spread(x)]))

        return functools.partial(dot, coarse[block // 2, h][:, half], twice), second

    def token_unit(n, h):
        cols = slice(n * LEAF, (n + 1) * LEAF)
        half = slice((n % 2) * LANES, (n % 2 + 1) * LANES)

        def second(x):
            term = from_spread(x)
            if 0 < n < leaves - 1:
                term = merge([near_terms[n, h], term])
            stat_out[h, 0:1, cols], sums_out[h, :, cols], stat_out[h, 1:2, cols] = term

        return (lambda: dot(fine[n // 2, h][:, half], twice)), second

    staggered([join_unit(block, h) for block in range(leaves // 2) for h in range(2)], 4)
    staggered([token_unit(n, h) for n in range(leaves) for h in range(2)], 4)

    row = iota((LEAF, LANES), 0)
    for side, leaf in ((0, first_leaf - 1), (1, first_leaf + leaves)):
        there = jnp.logical_and(leaf >= 0, leaf < count * leaves)
        held = jnp.where(there, counts[jnp.clip(leaf, 0, count * leaves - 1)], 0)
        end_marks[side, :LEAF] = near_marks(row >= held)
        for i in range(2):
            inner = first_leaf + side * (leaves - 2) + i
            end_marks[side, (i + 1) * LEAF : (i + 2) * LEAF] = near_marks(row >= counts[inner])
    for index, level in enumerate(remote):
        group, rows, _ = level_shape(level, tokens)
        for i in range(2**index):
            start = (rank ^ (2**index + i)) * leaves
            mass_out[index][:, i * rows : (i + 1) * rows] = mass(counts, start, leaves, group, rows)


def last_kernel(
    tokens, remote, q_cols, kv_rows, v_cols, sums_in, stat_in, end_marks, matrices, *rest
):
    levels = len(remote)
    queries, mass_in = rest[:levels], rest[levels : 2 * levels]
    pair, step = rest[2 * levels : 2 * levels + 2]
    packs = rest[2 * levels + 2 : -3]
    out, stage, sems = rest[-3:]
    rank = lax.axis_index("seq")
    leaves = tokens // LEAF
    flag = jnp.where(rank % 2 == 1, 1, 0)
    ends = {}
    results = {}

    halo_pair = decode(pair, 0, LEAF)
    halo_step = decode(step, 0, LEAF)

    def near_unit(side):
        own = flag if side == 0 else 1 - flag
        inner = slice(side * (leaves - 2) * LEAF, (side * (leaves - 2) + 2) * LEAF)
        keys, values = [
            jnp.where(own == 1, here, there).astype(BF16)
            for here, there in zip(halo_pair, halo_step)
        ]

        def first():
            return near_scores(
                jnp.concatenate([keys.T, kv_rows[inner, :LANES]], axis=0),
                end_marks[side],
                q_cols[:, side * (leaves - 1) * LEAF : (side * (leaves - 1) + 1) * LEAF],
            )

        def second(scores):
            window = jnp.concatenate([values, v_cols[:, inner]], axis=1)
            for h in range(2):
                ends[side * (leaves - 1), h] = near(scores, window, h)

        return first, second

    def far_units(index):
        level = remote[index]
        group, rows, _ = level_shape(level, tokens)
        if index == 0:
            fields = [decode(pair, halo_rows(), rows)]
        else:
            fields = [decode(packs[2**index - 2 + i], 0, rows) for i in range(2**index)]
        means, sums = [jnp.concatenate(field, axis=1) for field in zip(*fields)]
        keys = far_keys(means, mass_in[index][...])
        values = far_values(sums, mass_in[index][...])
        units = []
        for h in range(2):

            def second(scores, h=h):
                results[index, h] = far(scores, values[h])

            units.append((functools.partial(far_scores, keys[h], queries[index][h]), second))
        return units

    units = [near_unit(0), near_unit(1)]
    for index in range(levels):
        units += far_units(index)
    staggered(units, 2)

    coarse = []
    for h in range(2):
        merged = results[levels - 1, h]
        for index in reversed(range(levels - 1)):
            rows = level_shape(remote[index], tokens)[1]
            merged = merge(
                [results[index, h], from_spread(dot(to_spread(merged)[:, :LANES], matrices[0, :, :rows]))]
            )
        coarse.append(to_spread(merged))
    copies = []

    def token_unit(n, h):
        cols = slice(n * LEAF, (n + 1) * LEAF)
        half = slice(n // 4 * LANES, (n // 4 + 1) * LANES)

        def second(x):
            terms = [
                (stat_in[h, 0:1, cols], sums_in[h, :, cols], stat_in[h, 1:2, cols]),
                from_spread(x),
            ]
            if (n, h) in ends:
                terms.append(ends[n, h])
            _, sums, totals = merge(terms)
            stage[h, :, cols] = (sums * (1.0 / totals)).astype(BF16)
            if n % 2 and h:
                both = slice((n - 1) * LEAF, (n + 1) * LEAF)
                copies.append(
                    pltpu.make_async_copy(stage.at[:, :, both], out.at[:, :, both], sems.at[n // 2])
                )
                copies[-1].start()

        return functools.partial(dot, coarse[h][:, half], matrices[n % 4 + 1]), second

    staggered([token_unit(n, h) for n in range(leaves) for h in range(2)], 4)
    for copy in copies:
        copy.wait()


VMEM = pl.BlockSpec(memory_space=pltpu.VMEM)
ANY = pl.BlockSpec(memory_space=pl.ANY)


def params():
    return pltpu.CompilerParams(vmem_limit_bytes=48 * 2**20)


def step_pairs(count, heads):
    pairs = []
    for i in range(count):
        for h in range(heads):
            if 0 < i < count - 1:
                pairs.append((i * heads + h, (i + 1 if i % 2 else i - 1) * heads + h))
            else:
                pairs.append((i * heads + h, i * heads + (h ^ 1 if heads % 2 == 0 else h)))
    return pairs


def head_pair(q, k, v, order, counts):
    tokens = q.shape[2]
    leaves = tokens // LEAF
    count = lax.axis_size("seq")
    depth = (tokens * count // LEAF).bit_length() - 1
    remote = tuple(range(leaves.bit_length() - 1, depth))
    flat = (2 * HEAD, tokens)
    shape = jax.ShapeDtypeStruct
    widths = [level_shape(level, tokens)[1] for level in remote]
    sent = [shape((pack_rows(i, tokens, level), LANES), SENT) for i, level in enumerate(remote)]
    outs = [
        shape((tokens, 4 * HEAD), BF16),
        shape(flat, BF16),
        shape((1, tokens), jnp.int32),
        shape((2 * LANES, LEAF), BF16),
        sent[0],
    ] + [shape((width, 2 * LANES), F32) for width in widths[1:]]
    counts, order, k, v = (
        pltpu.with_memory_space_constraint(x, pltpu.HBM)
        for x in (counts, order, k.reshape(flat), v.reshape(flat))
    )
    kv_rows, v_cols, order_here, other, pair, *sums = pl.pallas_call(
        functools.partial(key_kernel, tokens, remote),
        out_shape=outs,
        in_specs=[ANY] * 4,
        out_specs=[VMEM] * len(outs),
        scratch_shapes=[
            pltpu.SMEM(counts.shape, jnp.int32),
            pltpu.VMEM(flat, BF16),
            pltpu.VMEM(flat, BF16),
            pltpu.SemaphoreType.DMA((4,)),
        ],
        compiler_params=params(),
        cost_estimate=pl.CostEstimate(
            flops=2 * 256 * tokens * tokens, bytes_accessed=4 * 2**20, transcendentals=0
        ),
        name="gather_keys",
    )(counts, order, k, v)
    got_pair = lax.ppermute(pair, "seq", [(i, i ^ 1) for i in range(count)])

    outs = [shape((halo_rows(), LANES), SENT)] + sent[1:]
    step, *packs = pl.pallas_call(
        functools.partial(pack_kernel, tokens, remote),
        out_shape=outs,
        in_specs=[ANY] + [VMEM] * len(remote),
        out_specs=[VMEM] * len(outs),
        scratch_shapes=[pltpu.SMEM(counts.shape, jnp.int32), pltpu.SemaphoreType.DMA(())],
        compiler_params=params(),
        cost_estimate=pl.CostEstimate(flops=2**20, bytes_accessed=2**18, transcendentals=0),
        name="pack_rest",
    )(counts, other, *sums)
    got = []
    for index in range(1, len(remote)):
        for partner in range(2**index, 2 ** (index + 1)):
            got.append(
                lax.ppermute(packs[index - 1], "seq", [(i, i ^ partner) for i in range(count)])
            )
    got_step = lax.ppermute(step, ("seq", "head"), step_pairs(count, lax.axis_size("head")))

    outs = (
        [shape(flat, BF16), shape((2, HEAD, tokens), F32), shape((2, 2, tokens), F32)]
        + [shape((2, 3 * LEAF, LANES), BF16), shape((5, LANES, LEAF), BF16)]
        + [shape((2, 2 * HEAD, width), BF16) for width in widths]
        + [shape((16, 2**i * width), F32) for i, width in enumerate(widths)]
    )
    q_cols, *local = pl.pallas_call(
        functools.partial(local_kernel, tokens, remote),
        out_shape=outs,
        in_specs=[ANY] + [VMEM] * 4,
        out_specs=[VMEM] * len(outs),
        scratch_shapes=[
            pltpu.SMEM(counts.shape, jnp.int32),
            pltpu.SemaphoreType.DMA(()),
            pltpu.VMEM((tokens, LANES), BF16),
        ],
        compiler_params=params(),
        cost_estimate=pl.CostEstimate(flops=2**20, bytes_accessed=2**16, transcendentals=0),
        name="local_attention",
    )(counts, q.reshape(flat), order_here, kv_rows, v_cols)
    return pl.pallas_call(
        functools.partial(last_kernel, tokens, remote),
        out_shape=shape((2, HEAD, tokens), BF16),
        in_specs=[VMEM] * (5 + len(local) + len(got)),
        out_specs=ANY,
        scratch_shapes=[
            pltpu.VMEM((2, HEAD, tokens), BF16),
            pltpu.SemaphoreType.DMA((leaves // 2,)),
        ],
        compiler_params=params(),
        cost_estimate=pl.CostEstimate(flops=2**30, bytes_accessed=4 * 2**20, transcendentals=2**20),
        name="remote_attention",
    )(q_cols, kv_rows, v_cols, *local, got_pair, got_step, *got)


def shards(q, k, v, order, counts):
    heads = q.shape[0]
    if heads % 2:
        q, k, v = (jnp.concatenate([x, jnp.zeros_like(x[:1])], axis=0) for x in (q, k, v))
    out = [
        head_pair(q[h : h + 2], k[h : h + 2], v[h : h + 2], order, counts)
        for h in range(0, q.shape[0], 2)
    ]
    out = out[0] if len(out) == 1 else jnp.concatenate(out, axis=0)
    return out[:heads] if heads % 2 else out


def solution(mesh):
    placed = (
        P("head", None, ("grp", "seq")),
        P("head", None, ("grp", "seq")),
        P("head", None, ("grp", "seq")),
        P(("grp", "seq"), None),
        P("grp"),
    )
    return jax.shard_map(
        shards,
        mesh=mesh,
        in_specs=placed,
        out_specs=P("head", None, ("grp", "seq")),
        check_vma=False,
    )
```

```python
import functools
import math

import jax
import jax.numpy as jnp
from jax import lax
from jax.experimental import pallas as pl
from jax.experimental.pallas import tpu as pltpu
from jax.sharding import PartitionSpec as P

LEAF = 256
HEAD = 64
LANES = 128
MASKED = -1e30
F32 = jnp.float32
BF16 = jnp.bfloat16
SCALE = math.log2(math.e) / math.sqrt(HEAD)
SENT = jnp.int16
CODE = 32000.0
PIECE = 4 * HEAD + 16


def dot(a, b):
    return lax.dot_general(a, b, (((1,), (0,)), ((), ())), preferred_element_type=F32)


def iota(shape, dim):
    return lax.broadcasted_iota(jnp.int32, shape, dim)


def bits(cond):
    return jnp.where(cond, 1.0, 0.0).astype(BF16)


def split(x, terms=2):
    out = []
    for _ in range(terms - 1):
        out.append(x.astype(BF16))
        x = x - out[-1].astype(F32)
    return out + [x.astype(BF16)]


def encode(keys, values):
    parts = []
    row = iota((16, keys.shape[1]), 0)
    exponents = jnp.zeros(row.shape, F32)
    for i, x in enumerate((keys, values)):
        largest = jnp.max(jnp.abs(x), axis=0, keepdims=True)
        exponent = jnp.floor(jnp.log2(jnp.maximum(largest, 2.0**-100))) + 1.0
        parts.append(jnp.round(x * (jnp.exp2(-exponent) * CODE)))
        exponents = jnp.where(row == i, exponent, exponents)
    codes = jnp.concatenate(parts + [exponents], axis=0).astype(jnp.int32).astype(SENT)
    return [codes[:, i : i + LANES] for i in range(0, codes.shape[1], LANES)]


def put(ref, at, pieces):
    for piece in pieces:
        ref[at : at + PIECE, :] = piece
        at += PIECE


def decode(ref, at, width):
    pieces = [ref[at + i * PIECE : at + (i + 1) * PIECE, :] for i in range(width // LANES)]
    x = jnp.concatenate(pieces, axis=1).astype(jnp.int32).astype(F32)
    scales = jnp.exp2(x[4 * HEAD :]) * (1.0 / CODE)
    return x[: 2 * HEAD] * scales[0:1], x[2 * HEAD : 4 * HEAD] * scales[1:2]


def one_hot(order_row, tokens):
    high = order_row // LEAF
    low = (order_row - high * LEAF).astype(F32).astype(BF16)
    slots = iota((LEAF, LEAF), 0).astype(F32).astype(BF16)
    base = jnp.where(slots == low, jnp.ones((), BF16), jnp.zeros((), BF16))
    return jnp.concatenate([base * bits(high == j) for j in range(tokens // LEAF)], axis=0)


def pool_rows(group, first_row, rows):
    return bits(iota((rows, LEAF), 1) // group + first_row == iota((rows, LEAF), 0))


def level_shape(level, tokens):
    group = 2**level
    rows = tokens // group
    return group, max(min(rows, LEAF), LANES), max(rows // LEAF, 1)


def place(level, leaf, tokens):
    group, rows, _ = level_shape(level, tokens)
    per_leaf = LEAF // group
    return (leaf * per_leaf) // rows, (leaf * per_leaf) % rows


class Pool:
    def __init__(self, levels, tokens):
        self.levels, self.tokens = levels, tokens
        self.whole = [level for level in levels if LEAF // 2**level % 16 == 0]
        parts = [pool_rows(2**level, 0, LEAF // 2**level) for level in self.whole]
        self.matrix = jnp.concatenate(parts, axis=0) if parts else None
        self.pieces, self.sums = {}, {}

    def add(self, leaf, values):
        both = dot(self.matrix, values) if self.whole else None
        at = 0
        for level in self.levels:
            block, first = place(level, leaf, self.tokens)
            if level in self.whole:
                count = LEAF // 2**level
                self.pieces.setdefault((level, block), {})[leaf] = both[at : at + count]
                at += count
            else:
                group, rows, _ = level_shape(level, self.tokens)
                piece = dot(pool_rows(group, first, rows), values)
                old = self.sums.get((level, block))
                self.sums[level, block] = piece if old is None else old + piece

    def get(self, level, block):
        if level not in self.whole:
            return self.sums[level, block]
        pieces = self.pieces[level, block]
        return jnp.concatenate([pieces[leaf] for leaf in sorted(pieces)], axis=0)


def mass(counts, first_leaf, leaves, group, rows):
    row = iota((16, rows), 1)
    per_leaf = LEAF // group
    leaf = row // per_leaf
    held = jnp.zeros(row.shape, jnp.int32)
    for n in range(leaves):
        held = jnp.where(leaf == n, counts[first_leaf + n], held)
    return jnp.clip(held - (row % per_leaf) * group, 0, group).astype(F32)


def valid_only(kv_rows, held):
    keep = bits(iota((LEAF, LANES), 0) < held)
    return kv_rows * jnp.concatenate([keep, keep], axis=1)


def near_marks(empty):
    return jnp.where((iota(empty.shape, 1) == 0) & empty, MASKED, 0.0).astype(BF16)


def far_keys(means, weight):
    hi, lo = split(means)
    mark = jnp.where((iota(weight.shape, 0) == 0) & (weight == 0.0), MASKED, 0.0).astype(BF16)
    rest = jnp.zeros((HEAD - 16, hi.shape[1]), BF16)
    out = []
    for h in range(2):
        here = slice(h * HEAD, (h + 1) * HEAD)
        out.append(
            jnp.concatenate([hi[here], lo[here], hi[here], mark, rest], axis=0).T
        )
    return out


def far_values(sums, mass_rows):
    hi, lo = split(sums)
    mass_rows = mass_rows.astype(BF16)
    return [
        jnp.concatenate([hi[h * HEAD : (h + 1) * HEAD], lo[h * HEAD : (h + 1) * HEAD], mass_rows], axis=0)
        for h in range(2)
    ]


def near_scores(k_window, mark, query):
    none = jnp.zeros((HEAD, LEAF), BF16)
    right = jnp.concatenate(
        [
            jnp.concatenate([query[:HEAD], none], axis=1),
            jnp.concatenate([none, query[HEAD:]], axis=1),
            bits(iota((LANES, 2 * LEAF), 0) == 0),
        ],
        axis=0,
    )
    left = jnp.concatenate([k_window, mark], axis=1)
    return [dot(left[i * LEAF : (i + 1) * LEAF], right) for i in range(3)]


def near(scores, v_window, h):
    scores = [piece[:, h * LEAF : (h + 1) * LEAF] for piece in scores]
    top = functools.reduce(jnp.maximum, [jnp.max(x, axis=0, keepdims=True) for x in scores])
    sums = totals = 0.0
    for i, piece in enumerate(scores):
        weights = jnp.exp2((piece - top) * SCALE)
        totals = totals + jnp.sum(weights, axis=0, keepdims=True)
        value = v_window[h * HEAD : (h + 1) * HEAD, i * LEAF : (i + 1) * LEAF]
        sums = sums + dot(value, weights.astype(BF16))
    return top * SCALE, sums, totals


def far_scores(keys, query):
    hi, lo = query[:HEAD], query[HEAD:]
    flag = bits(iota((HEAD, query.shape[1]), 0) == 0)
    return dot(keys, jnp.concatenate([hi, hi, lo, flag], axis=0))


def far(scores, value):
    top = jnp.max(scores, axis=0, keepdims=True).astype(BF16).astype(F32)
    w_hi, w_lo = split(jnp.exp2(scores - top))
    out = dot(jnp.concatenate([value, value], axis=1), jnp.concatenate([w_hi, w_lo], axis=0))
    return top, out[:HEAD] + out[HEAD : 2 * HEAD], out[2 * HEAD : 2 * HEAD + 1]


def staggered(units, ahead=1):
    held = []
    for first, second in units:
        held.append((second, first()))
        if len(held) > ahead:
            second, scores = held.pop(0)
            second(scores)
    for second, scores in held:
        second(scores)


def to_spread(term):
    top, sums, totals = term
    row = iota((16, sums.shape[1]), 0)
    t_hi, t_lo = split(totals)
    tail = jnp.where(row == 0, t_hi.astype(F32), jnp.where(row == 1, t_lo.astype(F32), top))
    hi, lo = split(sums)
    return jnp.concatenate([hi, lo, tail.astype(BF16)], axis=0)


def spread_matrix(times, first, width=LEAF):
    size = (LANES, width)
    return bits(iota(size, 0) == iota(size, 1) // times + first)


def from_spread(x):
    tail = x[2 * HEAD :]
    return tail[2:3], x[:HEAD] + x[HEAD : 2 * HEAD], tail[0:1] + tail[1:2]


def merge(terms):
    top = functools.reduce(jnp.maximum, [t[0] for t in terms])
    sums = totals = 0.0
    for t in terms:
        factor = jnp.exp2(t[0] - top)
        sums = sums + t[1] * factor
        totals = totals + t[2] * factor
    return top, sums, totals


def halo_rows():
    return LEAF // LANES * PIECE


def pack_rows(index, tokens, level):
    rows = level_shape(level, tokens)[1] // LANES * PIECE
    return rows + (halo_rows() if index == 0 else 0)


def key_kernel(
    tokens, remote, counts_in, order_in, k_in, v_in, kv_rows, v_cols, order, other, pair, *rest
):
    sums_out, (counts, k, v, sems) = rest[: len(remote) - 1], rest[len(remote) - 1 :]
    copies = [
        pltpu.make_async_copy(source, target, sems.at[i])
        for i, (source, target) in enumerate(
            ((order_in, order), (k_in, k), (v_in, v), (counts_in, counts))
        )
    ]
    for copy in copies:
        copy.start()
    rank = lax.axis_index("seq")
    leaves = tokens // LEAF
    copies[0].wait()
    first = one_hot(order[:, :LEAF], tokens)
    for copy in copies[1:]:
        copy.wait()
    joint = jnp.concatenate([k[...], v[...]], axis=0)
    odd = jnp.where(rank % 2 == 1, 1, 0)
    pool = Pool(remote, tokens)
    got = {}
    masked = {}

    def after(n):
        cols = slice(n * LEAF, (n + 1) * LEAF)
        rows = got[n].T
        kv_rows[cols, :] = rows
        v_cols[:, cols] = got[n][LANES:]
        masked[n] = valid_only(rows, counts[rank * leaves + n])

    def halos():
        low, high = got[0].astype(F32), got[leaves - 1].astype(F32)
        halo = jnp.where(odd == 1, low, high)
        put(pair, 0, encode(halo[:LANES], halo[LANES:]))
        other[...] = jnp.where(odd == 1, high, low).astype(BF16)

    for n in range(leaves):
        cols = slice(n * LEAF, (n + 1) * LEAF)
        got[n] = dot(joint, one_hot(order[:, cols], tokens) if n else first).astype(BF16)
        after(n)
    halos()
    for n in range(leaves):
        pool.add(n, masked[n])
    put(pair, halo_rows(), encode(*coarse_parts(counts, rank, remote[0], pool, tokens)))
    for ref, level in zip(sums_out, remote[1:]):
        means, sums = coarse_parts(counts, rank, level, pool, tokens)
        ref[:LANES, :] = means
        ref[LANES:, :] = sums


def pack_kernel(other, *rest):
    levels = len(rest) // 2
    sums, step, packs = rest[:levels], rest[levels], rest[levels + 1 :]
    halo = other[...].astype(F32)
    put(step, 0, encode(halo[:LANES], halo[LANES:]))
    for ref, x in zip(packs, sums):
        put(ref, 0, encode(x[:LANES, :], x[LANES:, :]))


def coarse_parts(counts, rank, level, pool, tokens):
    group, rows, _ = level_shape(level, tokens)
    leaves = tokens // LEAF
    weight = mass(counts, rank * leaves, leaves, group, rows)[:1]
    sums = pool.get(level, 0).T
    return sums[:LANES] / jnp.maximum(weight, 1.0), sums[LANES:]


def local_kernel(tokens, remote, counts_in, q, order, kv_rows, v_cols, q_cols, *rest):
    levels = len(remote)
    sums_out, stat_out, end_marks, matrices = rest[:4]
    queries_out, mass_out = rest[4 : 4 + levels], rest[4 + levels : 4 + 2 * levels]
    counts, sem, mark = rest[4 + 2 * levels :]
    copy = pltpu.make_async_copy(counts_in, counts, sem)
    copy.start()
    rank = lax.axis_index("seq")
    count = lax.axis_size("seq")
    leaves = tokens // LEAF
    first_leaf = rank * leaves
    near_terms = {}
    q_pool = Pool((1, 2) + tuple(remote), tokens)
    kv_pool = Pool((1, 2), tokens)
    for n in range(leaves):
        cols = slice(n * LEAF, (n + 1) * LEAF)
        got = dot(q[...], one_hot(order[:, cols], tokens)).astype(BF16)
        q_cols[:, cols] = got
    copy.wait()
    for n in range(leaves):
        rows = slice(n * LEAF, (n + 1) * LEAF)
        mark[rows, :] = near_marks(iota((LEAF, LANES), 0) >= counts[first_leaf + n])

    def near_unit(n):
        cols = slice(n * LEAF, (n + 1) * LEAF)
        window = slice((n - 1) * LEAF, (n + 2) * LEAF)

        def first():
            return near_scores(kv_rows[window, :LANES], mark[window, :], q_cols[:, cols])

        def second(scores):
            for h in range(2):
                near_terms[n, h] = near(scores, v_cols[:, window], h)

        return first, second

    staggered([near_unit(n) for n in range(1, leaves - 1)])
    for n in range(leaves):
        cols = slice(n * LEAF, (n + 1) * LEAF)
        q_pool.add(n, q_cols[:, cols].T)
    for n in range(leaves):
        cols = slice(n * LEAF, (n + 1) * LEAF)
        kv_pool.add(n, valid_only(kv_rows[cols, :], counts[first_leaf + n]))

    def queries(level, block):
        hi, lo = split(q_pool.get(level, block).T * (SCALE / 2**level))
        return [
            jnp.concatenate([x[h * HEAD : (h + 1) * HEAD] for x in (hi, lo)], axis=0)
            for h in range(2)
        ]

    results = {}
    units = []
    for level in (2, 1):
        group, rows, blocks = level_shape(level, tokens)
        per_block = rows * group // LEAF
        for block in range(blocks):
            weight = mass(counts, first_leaf + block * per_block, per_block, group, rows)
            sums = kv_pool.get(level, block).T
            keys = far_keys(sums[:LANES] / jnp.maximum(weight[:1], 1.0), weight)
            values = far_values(sums[LANES:], weight)
            query = queries(level, block ^ 1)
            for h in range(2):

                def second(scores, at=(level, block ^ 1, h), value=values[h]):
                    results[at] = far(scores, value)

                units.append((functools.partial(far_scores, keys[h], query[h]), second))
    staggered(units, 4)
    for index, level in enumerate(remote):
        block = queries(level, 0)
        for h in range(2):
            queries_out[index][h] = block[h]
    twice = spread_matrix(2, 0)
    matrices[0] = twice
    for j in range(4):
        matrices[j + 1] = spread_matrix(8, j * 32)
    coarse = {at: to_spread(results[2, at[0], at[1]]) for at in ((b, h) for b in range(leaves // 4) for h in range(2))}
    fine = {}

    def join_unit(block, h):
        half = slice((block % 2) * LANES, (block % 2 + 1) * LANES)

        def second(x):
            fine[block, h] = to_spread(merge([results[1, block, h], from_spread(x)]))

        return functools.partial(dot, coarse[block // 2, h][:, half], twice), second

    def token_unit(n, h):
        cols = slice(n * LEAF, (n + 1) * LEAF)
        half = slice((n % 2) * LANES, (n % 2 + 1) * LANES)

        def second(x):
            term = from_spread(x)
            if 0 < n < leaves - 1:
                term = merge([near_terms[n, h], term])
            stat_out[h, 0:1, cols], sums_out[h, :, cols], stat_out[h, 1:2, cols] = term

        return (lambda: dot(fine[n // 2, h][:, half], twice)), second

    staggered([join_unit(block, h) for block in range(leaves // 2) for h in range(2)], 4)
    staggered([token_unit(n, h) for n in range(leaves) for h in range(2)], 4)

    row = iota((LEAF, LANES), 0)
    for side, leaf in ((0, first_leaf - 1), (1, first_leaf + leaves)):
        there = jnp.logical_and(leaf >= 0, leaf < count * leaves)
        held = jnp.where(there, counts[jnp.clip(leaf, 0, count * leaves - 1)], 0)
        end_marks[side, :LEAF] = near_marks(row >= held)
        for i in range(2):
            inner = first_leaf + side * (leaves - 2) + i
            end_marks[side, (i + 1) * LEAF : (i + 2) * LEAF] = near_marks(row >= counts[inner])
    for index, level in enumerate(remote):
        group, rows, _ = level_shape(level, tokens)
        for i in range(2**index):
            start = (rank ^ (2**index + i)) * leaves
            mass_out[index][:, i * rows : (i + 1) * rows] = mass(counts, start, leaves, group, rows)


def last_kernel(
    tokens, remote, q_cols, kv_rows, v_cols, sums_in, stat_in, end_marks, matrices, *rest
):
    levels = len(remote)
    queries, mass_in = rest[:levels], rest[levels : 2 * levels]
    pair, step = rest[2 * levels : 2 * levels + 2]
    packs = rest[2 * levels + 2 : -3]
    out, stage, sems = rest[-3:]
    rank = lax.axis_index("seq")
    leaves = tokens // LEAF
    flag = jnp.where(rank % 2 == 1, 1, 0)
    ends = {}
    results = {}

    halo_pair = decode(pair, 0, LEAF)
    halo_step = decode(step, 0, LEAF)

    def near_unit(side):
        own = flag if side == 0 else 1 - flag
        inner = slice(side * (leaves - 2) * LEAF, (side * (leaves - 2) + 2) * LEAF)
        keys, values = [
            jnp.where(own == 1, here, there).astype(BF16)
            for here, there in zip(halo_pair, halo_step)
        ]

        def first():
            return near_scores(
                jnp.concatenate([keys.T, kv_rows[inner, :LANES]], axis=0),
                end_marks[side],
                q_cols[:, side * (leaves - 1) * LEAF : (side * (leaves - 1) + 1) * LEAF],
            )

        def second(scores):
            window = jnp.concatenate([values, v_cols[:, inner]], axis=1)
            for h in range(2):
                ends[side * (leaves - 1), h] = near(scores, window, h)

        return first, second

    def far_units(index):
        level = remote[index]
        group, rows, _ = level_shape(level, tokens)
        if index == 0:
            fields = [decode(pair, halo_rows(), rows)]
        else:
            fields = [decode(packs[2**index - 2 + i], 0, rows) for i in range(2**index)]
        means, sums = [jnp.concatenate(field, axis=1) for field in zip(*fields)]
        keys = far_keys(means, mass_in[index][...])
        values = far_values(sums, mass_in[index][...])
        units = []
        for h in range(2):

            def second(scores, h=h):
                results[index, h] = far(scores, values[h])

            units.append((functools.partial(far_scores, keys[h], queries[index][h]), second))
        return units

    units = [near_unit(0), near_unit(1)]
    for index in range(levels):
        units += far_units(index)
    staggered(units, 2)

    coarse = []
    for h in range(2):
        merged = results[levels - 1, h]
        for index in reversed(range(levels - 1)):
            rows = level_shape(remote[index], tokens)[1]
            merged = merge(
                [results[index, h], from_spread(dot(to_spread(merged)[:, :LANES], matrices[0, :, :rows]))]
            )
        coarse.append(to_spread(merged))
    copies = []

    def token_unit(n, h):
        cols = slice(n * LEAF, (n + 1) * LEAF)
        half = slice(n // 4 * LANES, (n // 4 + 1) * LANES)

        def second(x):
            terms = [
                (stat_in[h, 0:1, cols], sums_in[h, :, cols], stat_in[h, 1:2, cols]),
                from_spread(x),
            ]
            if (n, h) in ends:
                terms.append(ends[n, h])
            _, sums, totals = merge(terms)
            stage[h, :, cols] = (sums * (1.0 / totals)).astype(BF16)
            if n % 2 and h:
                both = slice((n - 1) * LEAF, (n + 1) * LEAF)
                copies.append(
                    pltpu.make_async_copy(stage.at[:, :, both], out.at[:, :, both], sems.at[n // 2])
                )
                copies[-1].start()

        return functools.partial(dot, coarse[h][:, half], matrices[n % 4 + 1]), second

    staggered([token_unit(n, h) for n in range(leaves) for h in range(2)], 4)
    for copy in copies:
        copy.wait()


VMEM = pl.BlockSpec(memory_space=pltpu.VMEM)
ANY = pl.BlockSpec(memory_space=pl.ANY)


def params():
    return pltpu.CompilerParams(vmem_limit_bytes=48 * 2**20)


def step_pairs(count, heads):
    pairs = []
    for i in range(count):
        for h in range(heads):
            if 0 < i < count - 1:
                pairs.append((i * heads + h, (i + 1 if i % 2 else i - 1) * heads + h))
            else:
                pairs.append((i * heads + h, i * heads + (h ^ 1 if heads % 2 == 0 else h)))
    return pairs


def head_pair(q, k, v, order, counts):
    tokens = q.shape[2]
    leaves = tokens // LEAF
    count = lax.axis_size("seq")
    depth = (tokens * count // LEAF).bit_length() - 1
    remote = tuple(range(leaves.bit_length() - 1, depth))
    flat = (2 * HEAD, tokens)
    shape = jax.ShapeDtypeStruct
    widths = [level_shape(level, tokens)[1] for level in remote]
    sent = [shape((pack_rows(i, tokens, level), LANES), SENT) for i, level in enumerate(remote)]
    outs = [
        shape((tokens, 4 * HEAD), BF16),
        shape(flat, BF16),
        shape((1, tokens), jnp.int32),
        shape((2 * LANES, LEAF), BF16),
        sent[0],
    ] + [shape((2 * LANES, width), F32) for width in widths[1:]]
    counts, order, k, v = (
        pltpu.with_memory_space_constraint(x, pltpu.HBM)
        for x in (counts, order, k.reshape(flat), v.reshape(flat))
    )
    kv_rows, v_cols, order_here, other, pair, *sums = pl.pallas_call(
        functools.partial(key_kernel, tokens, remote),
        out_shape=outs,
        in_specs=[ANY] * 4,
        out_specs=[VMEM] * len(outs),
        scratch_shapes=[
            pltpu.SMEM(counts.shape, jnp.int32),
            pltpu.VMEM(flat, BF16),
            pltpu.VMEM(flat, BF16),
            pltpu.SemaphoreType.DMA((4,)),
        ],
        compiler_params=params(),
        cost_estimate=pl.CostEstimate(
            flops=2 * 256 * tokens * tokens, bytes_accessed=4 * 2**20, transcendentals=0
        ),
        name="gather_keys",
    )(counts, order, k, v)
    got_pair = lax.ppermute(pair, "seq", [(i, i ^ 1) for i in range(count)])

    outs = [shape((halo_rows(), LANES), SENT)] + sent[1:]
    step, *packs = pl.pallas_call(
        pack_kernel,
        out_shape=outs,
        in_specs=[VMEM] * len(remote),
        out_specs=[VMEM] * len(outs),
        compiler_params=params(),
        cost_estimate=pl.CostEstimate(flops=2**20, bytes_accessed=2**18, transcendentals=0),
        name="pack_rest",
    )(other, *sums)
    got = []
    for index in range(1, len(remote)):
        for partner in range(2**index, 2 ** (index + 1)):
            got.append(
                lax.ppermute(packs[index - 1], "seq", [(i, i ^ partner) for i in range(count)])
            )
    got_step = lax.ppermute(step, ("seq", "head"), step_pairs(count, lax.axis_size("head")))

    outs = (
        [shape(flat, BF16), shape((2, HEAD, tokens), F32), shape((2, 2, tokens), F32)]
        + [shape((2, 3 * LEAF, LANES), BF16), shape((5, LANES, LEAF), BF16)]
        + [shape((2, 2 * HEAD, width), BF16) for width in widths]
        + [shape((16, 2**i * width), F32) for i, width in enumerate(widths)]
    )
    q_cols, *local = pl.pallas_call(
        functools.partial(local_kernel, tokens, remote),
        out_shape=outs,
        in_specs=[ANY] + [VMEM] * 4,
        out_specs=[VMEM] * len(outs),
        scratch_shapes=[
            pltpu.SMEM(counts.shape, jnp.int32),
            pltpu.SemaphoreType.DMA(()),
            pltpu.VMEM((tokens, LANES), BF16),
        ],
        compiler_params=params(),
        cost_estimate=pl.CostEstimate(flops=2**20, bytes_accessed=2**16, transcendentals=0),
        name="local_attention",
    )(counts, q.reshape(flat), order_here, kv_rows, v_cols)
    return pl.pallas_call(
        functools.partial(last_kernel, tokens, remote),
        out_shape=shape((2, HEAD, tokens), BF16),
        in_specs=[VMEM] * (5 + len(local) + len(got)),
        out_specs=ANY,
        scratch_shapes=[
            pltpu.VMEM((2, HEAD, tokens), BF16),
            pltpu.SemaphoreType.DMA((leaves // 2,)),
        ],
        compiler_params=params(),
        cost_estimate=pl.CostEstimate(flops=2**30, bytes_accessed=4 * 2**20, transcendentals=2**20),
        name="remote_attention",
    )(q_cols, kv_rows, v_cols, *local, got_pair, got_step, *got)


def shards(q, k, v, order, counts):
    heads = q.shape[0]
    if heads % 2:
        q, k, v = (jnp.concatenate([x, jnp.zeros_like(x[:1])], axis=0) for x in (q, k, v))
    out = [
        head_pair(q[h : h + 2], k[h : h + 2], v[h : h + 2], order, counts)
        for h in range(0, q.shape[0], 2)
    ]
    out = out[0] if len(out) == 1 else jnp.concatenate(out, axis=0)
    return out[:heads] if heads % 2 else out


def solution(mesh):
    placed = (
        P("head", None, ("grp", "seq")),
        P("head", None, ("grp", "seq")),
        P("head", None, ("grp", "seq")),
        P(("grp", "seq"), None),
        P("grp"),
    )
    return jax.shard_map(
        shards,
        mesh=mesh,
        in_specs=placed,
        out_specs=P("head", None, ("grp", "seq")),
        check_vma=False,
    )
```

```python
import functools
import math

import jax
import jax.numpy as jnp
from jax import lax
from jax.experimental import pallas as pl
from jax.experimental.pallas import tpu as pltpu
from jax.sharding import PartitionSpec as P

LEAF = 256
HEAD = 64
LANES = 128
MASKED = -1e30
F32 = jnp.float32
BF16 = jnp.bfloat16
SCALE = math.log2(math.e) / math.sqrt(HEAD)
SENT = jnp.int16
CODE = 32000.0
PIECE = 4 * HEAD + 16


def dot(a, b):
    return lax.dot_general(a, b, (((1,), (0,)), ((), ())), preferred_element_type=F32)


def iota(shape, dim):
    return lax.broadcasted_iota(jnp.int32, shape, dim)


def bits(cond):
    return jnp.where(cond, 1.0, 0.0).astype(BF16)


def split(x, terms=2):
    out = []
    for _ in range(terms - 1):
        out.append(x.astype(BF16))
        x = x - out[-1].astype(F32)
    return out + [x.astype(BF16)]


def encode(keys, values):
    parts = []
    row = iota((16, keys.shape[1]), 0)
    exponents = jnp.zeros(row.shape, F32)
    for i, x in enumerate((keys, values)):
        largest = jnp.max(jnp.abs(x), axis=0, keepdims=True)
        exponent = jnp.floor(jnp.log2(jnp.maximum(largest, 2.0**-100))) + 1.0
        parts.append(jnp.round(x * (jnp.exp2(-exponent) * CODE)))
        exponents = jnp.where(row == i, exponent, exponents)
    codes = jnp.concatenate(parts + [exponents], axis=0).astype(jnp.int32).astype(SENT)
    return [codes[:, i : i + LANES] for i in range(0, codes.shape[1], LANES)]


def put(ref, at, pieces):
    for piece in pieces:
        ref[at : at + PIECE, :] = piece
        at += PIECE


def decode(ref, at, width):
    pieces = [ref[at + i * PIECE : at + (i + 1) * PIECE, :] for i in range(width // LANES)]
    x = jnp.concatenate(pieces, axis=1).astype(jnp.int32).astype(F32)
    scales = jnp.exp2(x[4 * HEAD :]) * (1.0 / CODE)
    return x[: 2 * HEAD] * scales[0:1], x[2 * HEAD : 4 * HEAD] * scales[1:2]


def one_hot(order_row, tokens):
    high = order_row // LEAF
    low = (order_row - high * LEAF).astype(F32).astype(BF16)
    slots = iota((LEAF, LEAF), 0).astype(F32).astype(BF16)
    base = jnp.where(slots == low, jnp.ones((), BF16), jnp.zeros((), BF16))
    return jnp.concatenate([base * bits(high == j) for j in range(tokens // LEAF)], axis=0)


def pool_rows(group, first_row, rows):
    return bits(iota((rows, LEAF), 1) // group + first_row == iota((rows, LEAF), 0))


def level_shape(level, tokens):
    group = 2**level
    rows = tokens // group
    return group, max(min(rows, LEAF), LANES), max(rows // LEAF, 1)


def place(level, leaf, tokens):
    group, rows, _ = level_shape(level, tokens)
    per_leaf = LEAF // group
    return (leaf * per_leaf) // rows, (leaf * per_leaf) % rows


class Pool:
    def __init__(self, levels, tokens):
        self.levels, self.tokens = levels, tokens
        self.whole = [level for level in levels if LEAF // 2**level % 16 == 0]
        parts = [pool_rows(2**level, 0, LEAF // 2**level) for level in self.whole]
        self.matrix = jnp.concatenate(parts, axis=0) if parts else None
        self.pieces, self.sums = {}, {}

    def add(self, leaf, values):
        both = dot(self.matrix, values) if self.whole else None
        at = 0
        for level in self.levels:
            block, first = place(level, leaf, self.tokens)
            if level in self.whole:
                count = LEAF // 2**level
                self.pieces.setdefault((level, block), {})[leaf] = both[at : at + count]
                at += count
            else:
                group, rows, _ = level_shape(level, self.tokens)
                piece = dot(pool_rows(group, first, rows), values)
                old = self.sums.get((level, block))
                self.sums[level, block] = piece if old is None else old + piece

    def get(self, level, block):
        if level not in self.whole:
            return self.sums[level, block]
        pieces = self.pieces[level, block]
        return jnp.concatenate([pieces[leaf] for leaf in sorted(pieces)], axis=0)


def mass(counts, first_leaf, leaves, group, rows):
    row = iota((16, rows), 1)
    per_leaf = LEAF // group
    leaf = row // per_leaf
    held = jnp.zeros(row.shape, jnp.int32)
    for n in range(leaves):
        held = jnp.where(leaf == n, counts[first_leaf + n], held)
    return jnp.clip(held - (row % per_leaf) * group, 0, group).astype(F32)


def valid_only(kv_rows, held):
    keep = bits(iota((LEAF, LANES), 0) < held)
    return kv_rows * jnp.concatenate([keep, keep], axis=1)


def near_marks(empty):
    return jnp.where((iota(empty.shape, 1) == 0) & empty, MASKED, 0.0).astype(BF16)


def far_keys(means, weight):
    hi, lo = split(means)
    mark = jnp.where((iota(weight.shape, 0) == 0) & (weight == 0.0), MASKED, 0.0).astype(BF16)
    rest = jnp.zeros((HEAD - 16, hi.shape[1]), BF16)
    out = []
    for h in range(2):
        here = slice(h * HEAD, (h + 1) * HEAD)
        out.append(
            jnp.concatenate([hi[here], lo[here], hi[here], mark, rest], axis=0).T
        )
    return out


def far_values(sums, mass_rows):
    hi, lo = split(sums)
    mass_rows = mass_rows.astype(BF16)
    return [
        jnp.concatenate([hi[h * HEAD : (h + 1) * HEAD], lo[h * HEAD : (h + 1) * HEAD], mass_rows], axis=0)
        for h in range(2)
    ]


def near_scores(k_window, mark, query):
    none = jnp.zeros((HEAD, LEAF), BF16)
    right = jnp.concatenate(
        [
            jnp.concatenate([query[:HEAD], none], axis=1),
            jnp.concatenate([none, query[HEAD:]], axis=1),
            bits(iota((LANES, 2 * LEAF), 0) == 0),
        ],
        axis=0,
    )
    left = jnp.concatenate([k_window, mark], axis=1)
    return [dot(left[i * LEAF : (i + 1) * LEAF], right) for i in range(3)]


def near(scores, v_window, h):
    scores = [piece[:, h * LEAF : (h + 1) * LEAF] for piece in scores]
    top = functools.reduce(jnp.maximum, [jnp.max(x, axis=0, keepdims=True) for x in scores])
    sums = totals = 0.0
    for i, piece in enumerate(scores):
        weights = jnp.exp2((piece - top) * SCALE)
        totals = totals + jnp.sum(weights, axis=0, keepdims=True)
        value = v_window[h * HEAD : (h + 1) * HEAD, i * LEAF : (i + 1) * LEAF]
        sums = sums + dot(value, weights.astype(BF16))
    return top * SCALE, sums, totals


def far_scores(keys, query):
    hi, lo = query[:HEAD], query[HEAD:]
    flag = bits(iota((HEAD, query.shape[1]), 0) == 0)
    return dot(keys, jnp.concatenate([hi, hi, lo, flag], axis=0))


def far(scores, value):
    top = jnp.max(scores, axis=0, keepdims=True).astype(BF16).astype(F32)
    w_hi, w_lo = split(jnp.exp2(scores - top))
    out = dot(jnp.concatenate([value, value], axis=1), jnp.concatenate([w_hi, w_lo], axis=0))
    return top, out[:HEAD] + out[HEAD : 2 * HEAD], out[2 * HEAD : 2 * HEAD + 1]


def staggered(units, ahead=1):
    held = []
    for first, second in units:
        held.append((second, first()))
        if len(held) > ahead:
            second, scores = held.pop(0)
            second(scores)
    for second, scores in held:
        second(scores)


def to_spread(term):
    top, sums, totals = term
    row = iota((16, sums.shape[1]), 0)
    t_hi, t_lo = split(totals)
    tail = jnp.where(row == 0, t_hi.astype(F32), jnp.where(row == 1, t_lo.astype(F32), top))
    hi, lo = split(sums)
    return jnp.concatenate([hi, lo, tail.astype(BF16)], axis=0)


def spread_matrix(times, first, width=LEAF):
    size = (LANES, width)
    return bits(iota(size, 0) == iota(size, 1) // times + first)


def from_spread(x):
    tail = x[2 * HEAD :]
    return tail[2:3], x[:HEAD] + x[HEAD : 2 * HEAD], tail[0:1] + tail[1:2]


def merge(terms):
    top = functools.reduce(jnp.maximum, [t[0] for t in terms])
    sums = totals = 0.0
    for t in terms:
        factor = jnp.exp2(t[0] - top)
        sums = sums + t[1] * factor
        totals = totals + t[2] * factor
    return top, sums, totals


def halo_rows():
    return LEAF // LANES * PIECE


def pack_rows(index, tokens, level):
    rows = level_shape(level, tokens)[1] // LANES * PIECE
    return rows + (halo_rows() if index == 0 else 0)


def key_kernel(
    tokens, remote, counts_in, order_in, k_in, v_in, kv_rows, v_cols, order, other, pair, *rest
):
    sums_out, (counts, k, v, sems) = rest[: len(remote) - 1], rest[len(remote) - 1 :]
    copies = [
        pltpu.make_async_copy(source, target, sems.at[i])
        for i, (source, target) in enumerate(
            ((order_in, order), (k_in, k), (v_in, v), (counts_in, counts))
        )
    ]
    for copy in copies:
        copy.start()
    rank = lax.axis_index("seq")
    leaves = tokens // LEAF
    copies[0].wait()
    first = one_hot(order[:, :LEAF], tokens)
    for copy in copies[1:]:
        copy.wait()
    joint = jnp.concatenate([k[...], v[...]], axis=0)
    odd = jnp.where(rank % 2 == 1, 1, 0)
    pool = Pool(remote, tokens)
    got = {}
    masked = {}

    def after(n):
        cols = slice(n * LEAF, (n + 1) * LEAF)
        rows = got[n].T
        kv_rows[cols, :] = rows
        v_cols[:, cols] = got[n][LANES:]
        masked[n] = valid_only(rows, counts[rank * leaves + n])

    def halos():
        low, high = got[0].astype(F32), got[leaves - 1].astype(F32)
        halo = jnp.where(odd == 1, low, high)
        put(pair, 0, encode(halo[:LANES], halo[LANES:]))
        other[...] = jnp.where(odd == 1, high, low).astype(BF16)

    for n in range(leaves):
        cols = slice(n * LEAF, (n + 1) * LEAF)
        got[n] = dot(joint, one_hot(order[:, cols], tokens) if n else first).astype(BF16)
        after(n)
    halos()
    for n in range(leaves):
        pool.add(n, masked[n])
    put(pair, halo_rows(), encode(*coarse_parts(counts, rank, remote[0], pool, tokens)))
    for ref, level in zip(sums_out, remote[1:]):
        means, sums = coarse_parts(counts, rank, level, pool, tokens)
        ref[:LANES, :] = means
        ref[LANES:, :] = sums


def pack_kernel(other, *rest):
    levels = len(rest) // 2
    sums, step, packs = rest[:levels], rest[levels], rest[levels + 1 :]
    halo = other[...].astype(F32)
    put(step, 0, encode(halo[:LANES], halo[LANES:]))
    for ref, x in zip(packs, sums):
        put(ref, 0, encode(x[:LANES, :], x[LANES:, :]))


def coarse_parts(counts, rank, level, pool, tokens):
    group, rows, _ = level_shape(level, tokens)
    leaves = tokens // LEAF
    weight = mass(counts, rank * leaves, leaves, group, rows)[:1]
    sums = pool.get(level, 0).T
    return sums[:LANES] / jnp.maximum(weight, 1.0), sums[LANES:]


def local_kernel(tokens, remote, counts_in, q, order, kv_rows, v_cols, q_cols, *rest):
    levels = len(remote)
    sums_out, stat_out, end_marks, matrices = rest[:4]
    queries_out, mass_out = rest[4 : 4 + levels], rest[4 + levels : 4 + 2 * levels]
    counts, sem, mark = rest[4 + 2 * levels :]
    copy = pltpu.make_async_copy(counts_in, counts, sem)
    copy.start()
    rank = lax.axis_index("seq")
    count = lax.axis_size("seq")
    leaves = tokens // LEAF
    first_leaf = rank * leaves
    near_terms = {}
    q_pool = Pool((1, 2) + tuple(remote), tokens)
    kv_pool = Pool((1, 2), tokens)
    for n in range(leaves):
        cols = slice(n * LEAF, (n + 1) * LEAF)
        got = dot(q[...], one_hot(order[:, cols], tokens)).astype(BF16)
        q_cols[:, cols] = got
    copy.wait()
    for n in range(leaves):
        rows = slice(n * LEAF, (n + 1) * LEAF)
        mark[rows, :] = near_marks(iota((LEAF, LANES), 0) >= counts[first_leaf + n])

    def near_unit(n):
        cols = slice(n * LEAF, (n + 1) * LEAF)
        window = slice((n - 1) * LEAF, (n + 2) * LEAF)

        def first():
            return near_scores(kv_rows[window, :LANES], mark[window, :], q_cols[:, cols])

        def second(scores):
            for h in range(2):
                near_terms[n, h] = near(scores, v_cols[:, window], h)

        return first, second

    staggered([near_unit(n) for n in range(1, leaves - 1)])
    for n in range(leaves):
        cols = slice(n * LEAF, (n + 1) * LEAF)
        q_pool.add(n, q_cols[:, cols].T)
    for n in range(leaves):
        cols = slice(n * LEAF, (n + 1) * LEAF)
        kv_pool.add(n, valid_only(kv_rows[cols, :], counts[first_leaf + n]))

    def queries(level, block):
        hi, lo = split(q_pool.get(level, block).T * (SCALE / 2**level))
        return [
            jnp.concatenate([x[h * HEAD : (h + 1) * HEAD] for x in (hi, lo)], axis=0)
            for h in range(2)
        ]

    results = {}
    units = []
    for level in (2, 1):
        group, rows, blocks = level_shape(level, tokens)
        per_block = rows * group // LEAF
        for block in range(blocks):
            weight = mass(counts, first_leaf + block * per_block, per_block, group, rows)
            sums = kv_pool.get(level, block).T
            keys = far_keys(sums[:LANES] / jnp.maximum(weight[:1], 1.0), weight)
            values = far_values(sums[LANES:], weight)
            query = queries(level, block ^ 1)
            for h in range(2):

                def second(scores, at=(level, block ^ 1, h), value=values[h]):
                    results[at] = far(scores, value)

                units.append((functools.partial(far_scores, keys[h], query[h]), second))
    staggered(units, 4)
    for index, level in enumerate(remote):
        block = queries(level, 0)
        for h in range(2):
            queries_out[index][h] = block[h]
    twice = spread_matrix(2, 0)
    matrices[0] = twice
    for j in range(4):
        matrices[j + 1] = spread_matrix(8, j * 32)
    coarse = {at: to_spread(results[2, at[0], at[1]]) for at in ((b, h) for b in range(leaves // 4) for h in range(2))}
    fine = {}

    def join_unit(block, h):
        half = slice((block % 2) * LANES, (block % 2 + 1) * LANES)

        def second(x):
            fine[block, h] = to_spread(merge([results[1, block, h], from_spread(x)]))

        return functools.partial(dot, coarse[block // 2, h][:, half], twice), second

    def token_unit(n, h):
        cols = slice(n * LEAF, (n + 1) * LEAF)
        half = slice((n % 2) * LANES, (n % 2 + 1) * LANES)

        def second(x):
            term = from_spread(x)
            if 0 < n < leaves - 1:
                term = merge([near_terms[n, h], term])
            stat_out[h, 0:1, cols], sums_out[h, :, cols], stat_out[h, 1:2, cols] = term

        return (lambda: dot(fine[n // 2, h][:, half], twice)), second

    staggered([join_unit(block, h) for block in range(leaves // 2) for h in range(2)], 4)
    staggered([token_unit(n, h) for n in range(leaves) for h in range(2)], 4)

    row = iota((LEAF, LANES), 0)
    for side, leaf in ((0, first_leaf - 1), (1, first_leaf + leaves)):
        there = jnp.logical_and(leaf >= 0, leaf < count * leaves)
        held = jnp.where(there, counts[jnp.clip(leaf, 0, count * leaves - 1)], 0)
        end_marks[side, :LEAF] = near_marks(row >= held)
        for i in range(2):
            inner = first_leaf + side * (leaves - 2) + i
            end_marks[side, (i + 1) * LEAF : (i + 2) * LEAF] = near_marks(row >= counts[inner])
    for index, level in enumerate(remote):
        group, rows, _ = level_shape(level, tokens)
        for i in range(2**index):
            start = (rank ^ (2**index + i)) * leaves
            mass_out[index][:, i * rows : (i + 1) * rows] = mass(counts, start, leaves, group, rows)


def last_kernel(
    tokens, remote, q_cols, kv_rows, v_cols, sums_in, stat_in, end_marks, matrices, *rest
):
    levels = len(remote)
    queries, mass_in = rest[:levels], rest[levels : 2 * levels]
    pair, step = rest[2 * levels : 2 * levels + 2]
    packs = rest[2 * levels + 2 : -3]
    out, stage, sems = rest[-3:]
    rank = lax.axis_index("seq")
    leaves = tokens // LEAF
    flag = jnp.where(rank % 2 == 1, 1, 0)
    ends = {}
    results = {}

    halo_pair = decode(pair, 0, LEAF)
    halo_step = decode(step, 0, LEAF)

    def near_unit(side):
        own = flag if side == 0 else 1 - flag
        inner = slice(side * (leaves - 2) * LEAF, (side * (leaves - 2) + 2) * LEAF)
        keys, values = [
            jnp.where(own == 1, here, there).astype(BF16)
            for here, there in zip(halo_pair, halo_step)
        ]

        def first():
            return near_scores(
                jnp.concatenate([keys.T, kv_rows[inner, :LANES]], axis=0),
                end_marks[side],
                q_cols[:, side * (leaves - 1) * LEAF : (side * (leaves - 1) + 1) * LEAF],
            )

        def second(scores):
            window = jnp.concatenate([values, v_cols[:, inner]], axis=1)
            for h in range(2):
                ends[side * (leaves - 1), h] = near(scores, window, h)

        return first, second

    def far_units(index):
        level = remote[index]
        group, rows, _ = level_shape(level, tokens)
        if index == 0:
            fields = [decode(pair, halo_rows(), rows)]
        else:
            fields = [decode(packs[2**index - 2 + i], 0, rows) for i in range(2**index)]
        means, sums = [jnp.concatenate(field, axis=1) for field in zip(*fields)]
        keys = far_keys(means, mass_in[index][...])
        values = far_values(sums, mass_in[index][...])
        units = []
        for h in range(2):

            def second(scores, h=h):
                results[index, h] = far(scores, values[h])

            units.append((functools.partial(far_scores, keys[h], queries[index][h]), second))
        return units

    units = []
    for index in reversed(range(levels)):
        units += far_units(index)
    staggered(units + [near_unit(0), near_unit(1)], 2)

    coarse = []
    for h in range(2):
        merged = results[levels - 1, h]
        for index in reversed(range(levels - 1)):
            rows = level_shape(remote[index], tokens)[1]
            merged = merge(
                [results[index, h], from_spread(dot(to_spread(merged)[:, :LANES], matrices[0, :, :rows]))]
            )
        coarse.append(to_spread(merged))
    copies = []

    def token_unit(n, h):
        cols = slice(n * LEAF, (n + 1) * LEAF)
        half = slice(n // 4 * LANES, (n // 4 + 1) * LANES)

        def second(x):
            terms = [
                (stat_in[h, 0:1, cols], sums_in[h, :, cols], stat_in[h, 1:2, cols]),
                from_spread(x),
            ]
            if (n, h) in ends:
                terms.append(ends[n, h])
            _, sums, totals = merge(terms)
            stage[h, :, cols] = (sums * (1.0 / totals)).astype(BF16)
            if n % 2 and h:
                both = slice((n - 1) * LEAF, (n + 1) * LEAF)
                copies.append(
                    pltpu.make_async_copy(stage.at[:, :, both], out.at[:, :, both], sems.at[n // 2])
                )
                copies[-1].start()

        return functools.partial(dot, coarse[h][:, half], matrices[n % 4 + 1]), second

    staggered([token_unit(n, h) for n in range(leaves) for h in range(2)], 4)
    for copy in copies:
        copy.wait()


VMEM = pl.BlockSpec(memory_space=pltpu.VMEM)
ANY = pl.BlockSpec(memory_space=pl.ANY)


def params():
    return pltpu.CompilerParams(vmem_limit_bytes=48 * 2**20)


def step_pairs(count, heads):
    pairs = []
    for i in range(count):
        for h in range(heads):
            if 0 < i < count - 1:
                pairs.append((i * heads + h, (i + 1 if i % 2 else i - 1) * heads + h))
            else:
                pairs.append((i * heads + h, i * heads + (h ^ 1 if heads % 2 == 0 else h)))
    return pairs


def head_pair(q, k, v, order, counts):
    tokens = q.shape[2]
    leaves = tokens // LEAF
    count = lax.axis_size("seq")
    depth = (tokens * count // LEAF).bit_length() - 1
    remote = tuple(range(leaves.bit_length() - 1, depth))
    flat = (2 * HEAD, tokens)
    shape = jax.ShapeDtypeStruct
    widths = [level_shape(level, tokens)[1] for level in remote]
    sent = [shape((pack_rows(i, tokens, level), LANES), SENT) for i, level in enumerate(remote)]
    outs = [
        shape((tokens, 4 * HEAD), BF16),
        shape(flat, BF16),
        shape((1, tokens), jnp.int32),
        shape((2 * LANES, LEAF), BF16),
        sent[0],
    ] + [shape((2 * LANES, width), F32) for width in widths[1:]]
    counts, order, k, v = (
        pltpu.with_memory_space_constraint(x, pltpu.HBM)
        for x in (counts, order, k.reshape(flat), v.reshape(flat))
    )
    kv_rows, v_cols, order_here, other, pair, *sums = pl.pallas_call(
        functools.partial(key_kernel, tokens, remote),
        out_shape=outs,
        in_specs=[ANY] * 4,
        out_specs=[VMEM] * len(outs),
        scratch_shapes=[
            pltpu.SMEM(counts.shape, jnp.int32),
            pltpu.VMEM(flat, BF16),
            pltpu.VMEM(flat, BF16),
            pltpu.SemaphoreType.DMA((4,)),
        ],
        compiler_params=params(),
        cost_estimate=pl.CostEstimate(
            flops=2 * 256 * tokens * tokens, bytes_accessed=4 * 2**20, transcendentals=0
        ),
        name="gather_keys",
    )(counts, order, k, v)
    got_pair = lax.ppermute(pair, "seq", [(i, i ^ 1) for i in range(count)])

    outs = [shape((halo_rows(), LANES), SENT)] + sent[1:]
    step, *packs = pl.pallas_call(
        pack_kernel,
        out_shape=outs,
        in_specs=[VMEM] * len(remote),
        out_specs=[VMEM] * len(outs),
        compiler_params=params(),
        cost_estimate=pl.CostEstimate(flops=2**20, bytes_accessed=2**18, transcendentals=0),
        name="pack_rest",
    )(other, *sums)
    got = []
    for index in range(1, len(remote)):
        for partner in range(2**index, 2 ** (index + 1)):
            got.append(
                lax.ppermute(packs[index - 1], "seq", [(i, i ^ partner) for i in range(count)])
            )
    got_step = lax.ppermute(step, ("seq", "head"), step_pairs(count, lax.axis_size("head")))

    outs = (
        [shape(flat, BF16), shape((2, HEAD, tokens), F32), shape((2, 2, tokens), F32)]
        + [shape((2, 3 * LEAF, LANES), BF16), shape((5, LANES, LEAF), BF16)]
        + [shape((2, 2 * HEAD, width), BF16) for width in widths]
        + [shape((16, 2**i * width), F32) for i, width in enumerate(widths)]
    )
    q_cols, *local = pl.pallas_call(
        functools.partial(local_kernel, tokens, remote),
        out_shape=outs,
        in_specs=[ANY] + [VMEM] * 4,
        out_specs=[VMEM] * len(outs),
        scratch_shapes=[
            pltpu.SMEM(counts.shape, jnp.int32),
            pltpu.SemaphoreType.DMA(()),
            pltpu.VMEM((tokens, LANES), BF16),
        ],
        compiler_params=params(),
        cost_estimate=pl.CostEstimate(flops=2**20, bytes_accessed=2**16, transcendentals=0),
        name="local_attention",
    )(counts, q.reshape(flat), order_here, kv_rows, v_cols)
    return pl.pallas_call(
        functools.partial(last_kernel, tokens, remote),
        out_shape=shape((2, HEAD, tokens), BF16),
        in_specs=[VMEM] * (5 + len(local) + len(got)),
        out_specs=ANY,
        scratch_shapes=[
            pltpu.VMEM((2, HEAD, tokens), BF16),
            pltpu.SemaphoreType.DMA((leaves // 2,)),
        ],
        compiler_params=params(),
        cost_estimate=pl.CostEstimate(flops=2**30, bytes_accessed=4 * 2**20, transcendentals=2**20),
        name="remote_attention",
    )(q_cols, kv_rows, v_cols, *local, got_pair, got_step, *got)


def shards(q, k, v, order, counts):
    heads = q.shape[0]
    if heads % 2:
        q, k, v = (jnp.concatenate([x, jnp.zeros_like(x[:1])], axis=0) for x in (q, k, v))
    out = [
        head_pair(q[h : h + 2], k[h : h + 2], v[h : h + 2], order, counts)
        for h in range(0, q.shape[0], 2)
    ]
    out = out[0] if len(out) == 1 else jnp.concatenate(out, axis=0)
    return out[:heads] if heads % 2 else out


def solution(mesh):
    placed = (
        P("head", None, ("grp", "seq")),
        P("head", None, ("grp", "seq")),
        P("head", None, ("grp", "seq")),
        P(("grp", "seq"), None),
        P("grp"),
    )
    return jax.shard_map(
        shards,
        mesh=mesh,
        in_specs=placed,
        out_specs=P("head", None, ("grp", "seq")),
        check_vma=False,
    )
```

```python
import functools
import math

import jax
import jax.numpy as jnp
from jax import lax
from jax.experimental import pallas as pl
from jax.experimental.pallas import tpu as pltpu
from jax.sharding import PartitionSpec as P

LEAF = 256
HEAD = 64
LANES = 128
MASKED = -1e30
F32 = jnp.float32
BF16 = jnp.bfloat16
SCALE = math.log2(math.e) / math.sqrt(HEAD)
SENT = jnp.int16
CODE = 32000.0
PIECE = 4 * HEAD + 16


def dot(a, b):
    return lax.dot_general(a, b, (((1,), (0,)), ((), ())), preferred_element_type=F32)


def iota(shape, dim):
    return lax.broadcasted_iota(jnp.int32, shape, dim)


def bits(cond):
    return jnp.where(cond, 1.0, 0.0).astype(BF16)


def split(x, terms=2):
    out = []
    for _ in range(terms - 1):
        out.append(x.astype(BF16))
        x = x - out[-1].astype(F32)
    return out + [x.astype(BF16)]


def encode(keys, values):
    parts = []
    row = iota((16, keys.shape[1]), 0)
    exponents = jnp.zeros(row.shape, F32)
    for i, x in enumerate((keys, values)):
        largest = jnp.max(jnp.abs(x), axis=0, keepdims=True)
        exponent = jnp.floor(jnp.log2(jnp.maximum(largest, 2.0**-100))) + 1.0
        parts.append(jnp.round(x * (jnp.exp2(-exponent) * CODE)))
        exponents = jnp.where(row == i, exponent, exponents)
    codes = jnp.concatenate(parts + [exponents], axis=0).astype(jnp.int32).astype(SENT)
    return [codes[:, i : i + LANES] for i in range(0, codes.shape[1], LANES)]


def put(ref, at, pieces):
    for piece in pieces:
        ref[at : at + PIECE, :] = piece
        at += PIECE


def decode(ref, at, width):
    pieces = [ref[at + i * PIECE : at + (i + 1) * PIECE, :] for i in range(width // LANES)]
    x = jnp.concatenate(pieces, axis=1).astype(jnp.int32).astype(F32)
    scales = jnp.exp2(x[4 * HEAD :]) * (1.0 / CODE)
    return x[: 2 * HEAD] * scales[0:1], x[2 * HEAD : 4 * HEAD] * scales[1:2]


def one_hot(order_row, tokens):
    high = order_row // LEAF
    low = (order_row - high * LEAF).astype(F32).astype(BF16)
    slots = iota((LEAF, LEAF), 0).astype(F32).astype(BF16)
    base = jnp.where(slots == low, jnp.ones((), BF16), jnp.zeros((), BF16))
    return jnp.concatenate([base * bits(high == j) for j in range(tokens // LEAF)], axis=0)


def pool_rows(group, first_row, rows):
    return bits(iota((rows, LEAF), 1) // group + first_row == iota((rows, LEAF), 0))


def level_shape(level, tokens):
    group = 2**level
    rows = tokens // group
    return group, max(min(rows, LEAF), LANES), max(rows // LEAF, 1)


def place(level, leaf, tokens):
    group, rows, _ = level_shape(level, tokens)
    per_leaf = LEAF // group
    return (leaf * per_leaf) // rows, (leaf * per_leaf) % rows


class Pool:
    def __init__(self, levels, tokens, turned=False):
        self.levels, self.tokens, self.turned = levels, tokens, turned
        self.whole = [level for level in levels if LEAF // 2**level % 16 == 0]
        parts = [pool_rows(2**level, 0, LEAF // 2**level) for level in self.whole]
        self.matrix = jnp.concatenate(parts, axis=0) if parts else None
        self.pieces, self.sums = {}, {}

    def add(self, leaf, values):
        if self.turned:
            both = lax.dot_general(
                self.matrix, values, (((1,), (1,)), ((), ())), preferred_element_type=F32
            )
            values = values.T
        else:
            both = dot(self.matrix, values) if self.whole else None
        at = 0
        for level in self.levels:
            block, first = place(level, leaf, self.tokens)
            if level in self.whole:
                count = LEAF // 2**level
                self.pieces.setdefault((level, block), {})[leaf] = both[at : at + count]
                at += count
            else:
                group, rows, _ = level_shape(level, self.tokens)
                piece = dot(pool_rows(group, first, rows), values)
                old = self.sums.get((level, block))
                self.sums[level, block] = piece if old is None else old + piece

    def get(self, level, block):
        if level not in self.whole:
            return self.sums[level, block]
        pieces = self.pieces[level, block]
        return jnp.concatenate([pieces[leaf] for leaf in sorted(pieces)], axis=0)


def mass(counts, first_leaf, leaves, group, rows):
    row = iota((16, rows), 1)
    per_leaf = LEAF // group
    leaf = row // per_leaf
    held = jnp.zeros(row.shape, jnp.int32)
    for n in range(leaves):
        held = jnp.where(leaf == n, counts[first_leaf + n], held)
    return jnp.clip(held - (row % per_leaf) * group, 0, group).astype(F32)


def valid_only(kv_rows, held):
    keep = bits(iota((LEAF, LANES), 0) < held)
    return kv_rows * jnp.concatenate([keep, keep], axis=1)


def near_marks(empty):
    return jnp.where((iota(empty.shape, 1) == 0) & empty, MASKED, 0.0).astype(BF16)


def far_keys(means, weight):
    hi, lo = split(means)
    mark = jnp.where((iota(weight.shape, 0) == 0) & (weight == 0.0), MASKED, 0.0).astype(BF16)
    rest = jnp.zeros((HEAD - 16, hi.shape[1]), BF16)
    out = []
    for h in range(2):
        here = slice(h * HEAD, (h + 1) * HEAD)
        out.append(
            jnp.concatenate([hi[here], lo[here], hi[here], mark, rest], axis=0).T
        )
    return out


def far_values(sums, mass_rows):
    hi, lo = split(sums)
    mass_rows = mass_rows.astype(BF16)
    return [
        jnp.concatenate([hi[h * HEAD : (h + 1) * HEAD], lo[h * HEAD : (h + 1) * HEAD], mass_rows], axis=0)
        for h in range(2)
    ]


def near_scores(k_window, mark, query):
    none = jnp.zeros((HEAD, LEAF), BF16)
    right = jnp.concatenate(
        [
            jnp.concatenate([query[:HEAD], none], axis=1),
            jnp.concatenate([none, query[HEAD:]], axis=1),
            bits(iota((LANES, 2 * LEAF), 0) == 0),
        ],
        axis=0,
    )
    left = jnp.concatenate([k_window, mark], axis=1)
    return [dot(left[i * LEAF : (i + 1) * LEAF], right) for i in range(3)]


def near(scores, v_window, h):
    scores = [piece[:, h * LEAF : (h + 1) * LEAF] for piece in scores]
    top = functools.reduce(jnp.maximum, [jnp.max(x, axis=0, keepdims=True) for x in scores])
    sums = totals = 0.0
    for i, piece in enumerate(scores):
        weights = jnp.exp2((piece - top) * SCALE)
        totals = totals + jnp.sum(weights, axis=0, keepdims=True)
        value = v_window[h * HEAD : (h + 1) * HEAD, i * LEAF : (i + 1) * LEAF]
        sums = sums + dot(value, weights.astype(BF16))
    return top * SCALE, sums, totals


def far_scores(keys, query):
    hi, lo = query[:HEAD], query[HEAD:]
    flag = bits(iota((HEAD, query.shape[1]), 0) == 0)
    return dot(keys, jnp.concatenate([hi, hi, lo, flag], axis=0))


def far(scores, value):
    top = jnp.max(scores, axis=0, keepdims=True).astype(BF16).astype(F32)
    w_hi, w_lo = split(jnp.exp2(scores - top))
    out = dot(jnp.concatenate([value, value], axis=1), jnp.concatenate([w_hi, w_lo], axis=0))
    return top, out[:HEAD] + out[HEAD : 2 * HEAD], out[2 * HEAD : 2 * HEAD + 1]


def staggered(units, ahead=1):
    held = []
    for first, second in units:
        held.append((second, first()))
        if len(held) > ahead:
            second, scores = held.pop(0)
            second(scores)
    for second, scores in held:
        second(scores)


def to_spread(term):
    top, sums, totals = term
    row = iota((16, sums.shape[1]), 0)
    t_hi, t_lo = split(totals)
    tail = jnp.where(row == 0, t_hi.astype(F32), jnp.where(row == 1, t_lo.astype(F32), top))
    hi, lo = split(sums)
    return jnp.concatenate([hi, lo, tail.astype(BF16)], axis=0)


def spread_matrix(times, first, width=LEAF):
    size = (LANES, width)
    return bits(iota(size, 0) == iota(size, 1) // times + first)


def from_spread(x):
    tail = x[2 * HEAD :]
    return tail[2:3], x[:HEAD] + x[HEAD : 2 * HEAD], tail[0:1] + tail[1:2]


def merge(terms):
    top = functools.reduce(jnp.maximum, [t[0] for t in terms])
    sums = totals = 0.0
    for t in terms:
        factor = jnp.exp2(t[0] - top)
        sums = sums + t[1] * factor
        totals = totals + t[2] * factor
    return top, sums, totals


def halo_rows():
    return LEAF // LANES * PIECE


def pack_rows(index, tokens, level):
    rows = level_shape(level, tokens)[1] // LANES * PIECE
    return rows + (halo_rows() if index == 0 else 0)


def key_kernel(
    tokens, remote, counts_in, order_in, k_in, v_in, kv_rows, v_cols, order, other, pair, *rest
):
    sums_out, (counts, k, v, sems) = rest[: len(remote) - 1], rest[len(remote) - 1 :]
    copies = [
        pltpu.make_async_copy(source, target, sems.at[i])
        for i, (source, target) in enumerate(
            ((order_in, order), (k_in, k), (v_in, v), (counts_in, counts))
        )
    ]
    for copy in copies:
        copy.start()
    rank = lax.axis_index("seq")
    leaves = tokens // LEAF
    copies[0].wait()
    first = one_hot(order[:, :LEAF], tokens)
    for copy in copies[1:]:
        copy.wait()
    joint = jnp.concatenate([k[...], v[...]], axis=0)
    odd = jnp.where(rank % 2 == 1, 1, 0)
    pool = Pool(remote, tokens)
    got = {}
    masked = {}

    def after(n):
        cols = slice(n * LEAF, (n + 1) * LEAF)
        masked[n] = valid_only(got[n].T, counts[rank * leaves + n])
        kv_rows[cols, :] = masked[n]
        v_cols[:, cols] = got[n][LANES:]

    def halos():
        low, high = got[0].astype(F32), got[leaves - 1].astype(F32)
        halo = jnp.where(odd == 1, low, high)
        put(pair, 0, encode(halo[:LANES], halo[LANES:]))
        other[...] = jnp.where(odd == 1, high, low).astype(BF16)

    for n in range(leaves):
        cols = slice(n * LEAF, (n + 1) * LEAF)
        got[n] = dot(joint, one_hot(order[:, cols], tokens) if n else first).astype(BF16)
        after(n)
    halos()
    for n in range(leaves):
        pool.add(n, masked[n])
    put(pair, halo_rows(), encode(*coarse_parts(counts, rank, remote[0], pool, tokens)))
    for ref, level in zip(sums_out, remote[1:]):
        means, sums = coarse_parts(counts, rank, level, pool, tokens)
        ref[:LANES, :] = means
        ref[LANES:, :] = sums


def pack_kernel(other, *rest):
    levels = len(rest) // 2
    sums, step, packs = rest[:levels], rest[levels], rest[levels + 1 :]
    halo = other[...].astype(F32)
    put(step, 0, encode(halo[:LANES], halo[LANES:]))
    for ref, x in zip(packs, sums):
        put(ref, 0, encode(x[:LANES, :], x[LANES:, :]))


def coarse_parts(counts, rank, level, pool, tokens):
    group, rows, _ = level_shape(level, tokens)
    leaves = tokens // LEAF
    weight = mass(counts, rank * leaves, leaves, group, rows)[:1]
    sums = pool.get(level, 0).T
    return sums[:LANES] / jnp.maximum(weight, 1.0), sums[LANES:]


def local_kernel(tokens, remote, counts_in, q, order, kv_rows, v_cols, q_cols, *rest):
    levels = len(remote)
    sums_out, stat_out, end_marks, matrices = rest[:4]
    queries_out, mass_out = rest[4 : 4 + levels], rest[4 + levels : 4 + 2 * levels]
    counts, sem, mark = rest[4 + 2 * levels :]
    copy = pltpu.make_async_copy(counts_in, counts, sem)
    copy.start()
    rank = lax.axis_index("seq")
    count = lax.axis_size("seq")
    leaves = tokens // LEAF
    first_leaf = rank * leaves
    near_terms = {}
    q_pool = Pool((1, 2) + tuple(remote), tokens, True)
    kv_pool = Pool((1, 2), tokens)
    for n in range(leaves):
        cols = slice(n * LEAF, (n + 1) * LEAF)
        got = dot(q[...], one_hot(order[:, cols], tokens)).astype(BF16)
        q_cols[:, cols] = got
    copy.wait()
    for n in range(leaves):
        rows = slice(n * LEAF, (n + 1) * LEAF)
        mark[rows, :] = near_marks(iota((LEAF, LANES), 0) >= counts[first_leaf + n])

    def near_unit(n):
        cols = slice(n * LEAF, (n + 1) * LEAF)
        window = slice((n - 1) * LEAF, (n + 2) * LEAF)

        def first():
            return near_scores(kv_rows[window, :LANES], mark[window, :], q_cols[:, cols])

        def second(scores):
            for h in range(2):
                near_terms[n, h] = near(scores, v_cols[:, window], h)

        return first, second

    for n in range(leaves):
        cols = slice(n * LEAF, (n + 1) * LEAF)
        q_pool.add(n, q_cols[:, cols])
    for n in range(leaves):
        cols = slice(n * LEAF, (n + 1) * LEAF)
        kv_pool.add(n, kv_rows[cols, :])

    staggered([near_unit(n) for n in range(1, leaves - 1)])

    def queries(level, block):
        hi, lo = split(q_pool.get(level, block).T * (SCALE / 2**level))
        return [
            jnp.concatenate([x[h * HEAD : (h + 1) * HEAD] for x in (hi, lo)], axis=0)
            for h in range(2)
        ]

    results = {}
    units = []
    for level in (2, 1):
        group, rows, blocks = level_shape(level, tokens)
        per_block = rows * group // LEAF
        for block in range(blocks):
            weight = mass(counts, first_leaf + block * per_block, per_block, group, rows)
            sums = kv_pool.get(level, block).T
            keys = far_keys(sums[:LANES] / jnp.maximum(weight[:1], 1.0), weight)
            values = far_values(sums[LANES:], weight)
            query = queries(level, block ^ 1)
            for h in range(2):

                def second(scores, at=(level, block ^ 1, h), value=values[h]):
                    results[at] = far(scores, value)

                units.append((functools.partial(far_scores, keys[h], query[h]), second))
    staggered(units, 4)
    for index, level in enumerate(remote):
        block = queries(level, 0)
        for h in range(2):
            queries_out[index][h] = block[h]
    twice = spread_matrix(2, 0)
    matrices[0] = twice
    for j in range(4):
        matrices[j + 1] = spread_matrix(8, j * 32)
    coarse = {at: to_spread(results[2, at[0], at[1]]) for at in ((b, h) for b in range(leaves // 4) for h in range(2))}
    fine = {}

    def join_unit(block, h):
        half = slice((block % 2) * LANES, (block % 2 + 1) * LANES)

        def second(x):
            fine[block, h] = to_spread(merge([results[1, block, h], from_spread(x)]))

        return functools.partial(dot, coarse[block // 2, h][:, half], twice), second

    def token_unit(n, h):
        cols = slice(n * LEAF, (n + 1) * LEAF)
        half = slice((n % 2) * LANES, (n % 2 + 1) * LANES)

        def second(x):
            term = from_spread(x)
            if 0 < n < leaves - 1:
                term = merge([near_terms[n, h], term])
            stat_out[h, 0:1, cols], sums_out[h, :, cols], stat_out[h, 1:2, cols] = term

        return (lambda: dot(fine[n // 2, h][:, half], twice)), second

    staggered([join_unit(block, h) for block in range(leaves // 2) for h in range(2)], 4)
    staggered([token_unit(n, h) for n in range(leaves) for h in range(2)], 4)

    row = iota((LEAF, LANES), 0)
    for side, leaf in ((0, first_leaf - 1), (1, first_leaf + leaves)):
        there = jnp.logical_and(leaf >= 0, leaf < count * leaves)
        held = jnp.where(there, counts[jnp.clip(leaf, 0, count * leaves - 1)], 0)
        end_marks[side, :LEAF] = near_marks(row >= held)
        for i in range(2):
            inner = first_leaf + side * (leaves - 2) + i
            end_marks[side, (i + 1) * LEAF : (i + 2) * LEAF] = near_marks(row >= counts[inner])
    for index, level in enumerate(remote):
        group, rows, _ = level_shape(level, tokens)
        for i in range(2**index):
            start = (rank ^ (2**index + i)) * leaves
            mass_out[index][:, i * rows : (i + 1) * rows] = mass(counts, start, leaves, group, rows)


def end_unit(tokens, side, halo, q_cols, kv_rows, v_cols, end_marks, keep):
    leaves = tokens // LEAF
    keys, values = [x.astype(BF16) for x in halo]
    inner = pl.ds(pl.multiple_of(side * ((leaves - 2) * LEAF), LEAF), 2 * LEAF)
    own = pl.ds(pl.multiple_of(side * ((leaves - 1) * LEAF), LEAF), LEAF)

    def first():
        return near_scores(
            jnp.concatenate([keys.T, kv_rows[inner, :][:, :LANES]], axis=0),
            end_marks[side],
            q_cols[:, own],
        )

    def second(scores):
        window = jnp.concatenate([values, v_cols[:, inner]], axis=1)
        for h in range(2):
            keep(h, near(scores, window, h))

    return first, second


def far_units(tokens, level, fields, queries, mass_rows, keep):
    means, sums = [jnp.concatenate(field, axis=1) for field in zip(*fields)]
    keys = far_keys(means, mass_rows[...])
    values = far_values(sums, mass_rows[...])
    units = []
    for h in range(2):

        def second(scores, h=h):
            keep(h, far(scores, values[h]))

        units.append((functools.partial(far_scores, keys[h], queries[h]), second))
    return units


def pair_kernel(
    tokens, level, q_cols, kv_rows, v_cols, end_marks, queries, mass_rows, pair,
    far_out, far_stat, end_out, end_stat
):
    side = 1 - lax.axis_index("seq") % 2

    def keeper(sums_ref, stat_ref):
        def keep(h, term):
            stat_ref[h, 0:1, :], sums_ref[h], stat_ref[h, 1:2, :] = term

        return keep

    rows = level_shape(level, tokens)[1]
    units = far_units(
        tokens, level, [decode(pair, halo_rows(), rows)], queries, mass_rows, keeper(far_out, far_stat)
    )
    units.append(
        end_unit(
            tokens, side, decode(pair, 0, LEAF), q_cols, kv_rows, v_cols, end_marks,
            keeper(end_out, end_stat),
        )
    )
    staggered(units, 2)


def last_kernel(
    tokens, remote, q_cols, kv_rows, v_cols, sums_in, stat_in, end_marks, matrices, *rest
):
    levels = len(remote)
    queries, mass_in = rest[: levels - 1], rest[levels - 1 : 2 * levels - 2]
    far_in, far_stat, end_in, end_stat, step = rest[2 * levels - 2 : 2 * levels + 3]
    packs = rest[2 * levels + 3 : -3]
    out, stage, sems = rest[-3:]
    odd = lax.axis_index("seq") % 2
    leaves = tokens // LEAF
    results = {}
    steps = {}
    for h in range(2):
        results[0, h] = (far_stat[h, 0:1, :], far_in[h], far_stat[h, 1:2, :])
    units = []
    for index in reversed(range(1, levels)):
        rows = level_shape(remote[index], tokens)[1]
        fields = [decode(packs[2**index - 2 + i], 0, rows) for i in range(2**index)]

        def keep(h, term, index=index):
            results[index, h] = term

        units += far_units(
            tokens, remote[index], fields, queries[index - 1], mass_in[index - 1], keep
        )
    units.append(
        end_unit(
            tokens, odd, decode(step, 0, LEAF), q_cols, kv_rows, v_cols, end_marks, steps.__setitem__
        )
    )
    staggered(units, 2)
    first_is_pair = jnp.where(odd == 1, 1, 0)
    ends = {}
    for h in range(2):
        pair_term = (end_stat[h, 0:1, :], end_in[h], end_stat[h, 1:2, :])
        for n, flag in ((0, first_is_pair), (leaves - 1, 1 - first_is_pair)):
            ends[n, h] = tuple(
                jnp.where(flag == 1, x, y) for x, y in zip(pair_term, steps[h])
            )

    coarse = []
    for h in range(2):
        merged = results[levels - 1, h]
        for index in reversed(range(levels - 1)):
            rows = level_shape(remote[index], tokens)[1]
            merged = merge(
                [results[index, h], from_spread(dot(to_spread(merged)[:, :LANES], matrices[0, :, :rows]))]
            )
        coarse.append(to_spread(merged))
    copies = []

    def token_unit(n, h):
        cols = slice(n * LEAF, (n + 1) * LEAF)
        half = slice(n // 4 * LANES, (n // 4 + 1) * LANES)

        def second(x):
            terms = [
                (stat_in[h, 0:1, cols], sums_in[h, :, cols], stat_in[h, 1:2, cols]),
                from_spread(x),
            ]
            if (n, h) in ends:
                terms.append(ends[n, h])
            _, sums, totals = merge(terms)
            stage[h, :, cols] = (sums * (1.0 / totals)).astype(BF16)
            if n % 2 and h:
                both = slice((n - 1) * LEAF, (n + 1) * LEAF)
                copies.append(
                    pltpu.make_async_copy(stage.at[:, :, both], out.at[:, :, both], sems.at[n // 2])
                )
                copies[-1].start()

        return functools.partial(dot, coarse[h][:, half], matrices[n % 4 + 1]), second

    staggered([token_unit(n, h) for n in range(leaves) for h in range(2)], 4)
    for copy in copies:
        copy.wait()


VMEM = pl.BlockSpec(memory_space=pltpu.VMEM)
ANY = pl.BlockSpec(memory_space=pl.ANY)


def params():
    return pltpu.CompilerParams(vmem_limit_bytes=48 * 2**20)


def step_pairs(count, heads):
    pairs = []
    for i in range(count):
        for h in range(heads):
            if 0 < i < count - 1:
                pairs.append((i * heads + h, (i + 1 if i % 2 else i - 1) * heads + h))
            else:
                pairs.append((i * heads + h, i * heads + (h ^ 1 if heads % 2 == 0 else h)))
    return pairs


def head_pair(q, k, v, order, counts):
    tokens = q.shape[2]
    leaves = tokens // LEAF
    count = lax.axis_size("seq")
    depth = (tokens * count // LEAF).bit_length() - 1
    remote = tuple(range(leaves.bit_length() - 1, depth))
    flat = (2 * HEAD, tokens)
    shape = jax.ShapeDtypeStruct
    widths = [level_shape(level, tokens)[1] for level in remote]
    sent = [shape((pack_rows(i, tokens, level), LANES), SENT) for i, level in enumerate(remote)]
    outs = [
        shape((tokens, 4 * HEAD), BF16),
        shape(flat, BF16),
        shape((1, tokens), jnp.int32),
        shape((2 * LANES, LEAF), BF16),
        sent[0],
    ] + [shape((2 * LANES, width), F32) for width in widths[1:]]
    counts, order, k, v = (
        pltpu.with_memory_space_constraint(x, pltpu.HBM)
        for x in (counts, order, k.reshape(flat), v.reshape(flat))
    )
    kv_rows, v_cols, order_here, other, pair, *sums = pl.pallas_call(
        functools.partial(key_kernel, tokens, remote),
        out_shape=outs,
        in_specs=[ANY] * 4,
        out_specs=[VMEM] * len(outs),
        scratch_shapes=[
            pltpu.SMEM(counts.shape, jnp.int32),
            pltpu.VMEM(flat, BF16),
            pltpu.VMEM(flat, BF16),
            pltpu.SemaphoreType.DMA((4,)),
        ],
        compiler_params=params(),
        cost_estimate=pl.CostEstimate(
            flops=2 * 256 * tokens * tokens, bytes_accessed=4 * 2**20, transcendentals=0
        ),
        name="gather_keys",
    )(counts, order, k, v)
    got_pair = lax.ppermute(pair, "seq", [(i, i ^ 1) for i in range(count)])

    outs = [shape((halo_rows(), LANES), SENT)] + sent[1:]
    step, *packs = pl.pallas_call(
        pack_kernel,
        out_shape=outs,
        in_specs=[VMEM] * len(remote),
        out_specs=[VMEM] * len(outs),
        compiler_params=params(),
        cost_estimate=pl.CostEstimate(flops=2**20, bytes_accessed=2**18, transcendentals=0),
        name="pack_rest",
    )(other, *sums)
    got = []
    for index in range(1, len(remote)):
        for partner in range(2**index, 2 ** (index + 1)):
            got.append(
                lax.ppermute(packs[index - 1], "seq", [(i, i ^ partner) for i in range(count)])
            )
    got_step = lax.ppermute(step, ("seq", "head"), step_pairs(count, lax.axis_size("head")))

    outs = (
        [shape(flat, BF16), shape((2, HEAD, tokens), F32), shape((2, 2, tokens), F32)]
        + [shape((2, 3 * LEAF, LANES), BF16), shape((5, LANES, LEAF), BF16)]
        + [shape((2, 2 * HEAD, width), BF16) for width in widths]
        + [shape((16, 2**i * width), F32) for i, width in enumerate(widths)]
    )
    q_cols, *local = pl.pallas_call(
        functools.partial(local_kernel, tokens, remote),
        out_shape=outs,
        in_specs=[ANY] + [VMEM] * 4,
        out_specs=[VMEM] * len(outs),
        scratch_shapes=[
            pltpu.SMEM(counts.shape, jnp.int32),
            pltpu.SemaphoreType.DMA(()),
            pltpu.VMEM((tokens, LANES), BF16),
        ],
        compiler_params=params(),
        cost_estimate=pl.CostEstimate(flops=2**31, bytes_accessed=2**16, transcendentals=0),
        name="local_attention",
    )(counts, q.reshape(flat), order_here, kv_rows, v_cols)
    sums, stat, end_marks, matrices = local[:4]
    queries, masses = local[4 : 4 + len(remote)], local[4 + len(remote) :]
    term = [shape((2, HEAD, LEAF), F32), shape((2, 2, LEAF), F32)]
    paired = pl.pallas_call(
        functools.partial(pair_kernel, tokens, remote[0]),
        out_shape=term + term,
        in_specs=[VMEM] * 7,
        out_specs=[VMEM] * 4,
        compiler_params=params(),
        cost_estimate=pl.CostEstimate(flops=2**28, bytes_accessed=2**20, transcendentals=2**19),
        name="pair_attention",
    )(q_cols, kv_rows, v_cols, end_marks, queries[0], masses[0], got_pair)
    last_args = [q_cols, kv_rows, v_cols, sums, stat, end_marks, matrices]
    last_args += [*queries[1:], *masses[1:], *paired, got_step, *got]
    return pl.pallas_call(
        functools.partial(last_kernel, tokens, remote),
        out_shape=shape((2, HEAD, tokens), BF16),
        in_specs=[VMEM] * len(last_args),
        out_specs=ANY,
        scratch_shapes=[
            pltpu.VMEM((2, HEAD, tokens), BF16),
            pltpu.SemaphoreType.DMA((leaves // 2,)),
        ],
        compiler_params=params(),
        cost_estimate=pl.CostEstimate(flops=2**30, bytes_accessed=4 * 2**20, transcendentals=2**20),
        name="remote_attention",
    )(*last_args)


def shards(q, k, v, order, counts):
    heads = q.shape[0]
    if heads % 2:
        q, k, v = (jnp.concatenate([x, jnp.zeros_like(x[:1])], axis=0) for x in (q, k, v))
    out = [
        head_pair(q[h : h + 2], k[h : h + 2], v[h : h + 2], order, counts)
        for h in range(0, q.shape[0], 2)
    ]
    out = out[0] if len(out) == 1 else jnp.concatenate(out, axis=0)
    return out[:heads] if heads % 2 else out


def solution(mesh):
    placed = (
        P("head", None, ("grp", "seq")),
        P("head", None, ("grp", "seq")),
        P("head", None, ("grp", "seq")),
        P(("grp", "seq"), None),
        P("grp"),
    )
    return jax.shard_map(
        shards,
        mesh=mesh,
        in_specs=placed,
        out_specs=P("head", None, ("grp", "seq")),
        check_vma=False,
    )
```

```python
import functools
import math

import jax
import jax.numpy as jnp
from jax import lax
from jax.experimental import pallas as pl
from jax.experimental.pallas import tpu as pltpu
from jax.sharding import PartitionSpec as P

LEAF = 256
HEAD = 64
LANES = 128
MASKED = -1e30
F32 = jnp.float32
BF16 = jnp.bfloat16
SCALE = math.log2(math.e) / math.sqrt(HEAD)
SENT = jnp.int16
CODE = 32000.0
PIECE = 4 * HEAD + 16


def dot(a, b):
    return lax.dot_general(a, b, (((1,), (0,)), ((), ())), preferred_element_type=F32)


def iota(shape, dim):
    return lax.broadcasted_iota(jnp.int32, shape, dim)


def bits(cond):
    return jnp.where(cond, 1.0, 0.0).astype(BF16)


def split(x, terms=2):
    out = []
    for _ in range(terms - 1):
        out.append(x.astype(BF16))
        x = x - out[-1].astype(F32)
    return out + [x.astype(BF16)]


def encode(keys, values):
    parts = []
    row = iota((16, keys.shape[1]), 0)
    exponents = jnp.zeros(row.shape, F32)
    for i, x in enumerate((keys, values)):
        largest = jnp.max(jnp.abs(x), axis=0, keepdims=True)
        exponent = jnp.floor(jnp.log2(jnp.maximum(largest, 2.0**-100))) + 1.0
        parts.append(jnp.round(x * (jnp.exp2(-exponent) * CODE)))
        exponents = jnp.where(row == i, exponent, exponents)
    codes = jnp.concatenate(parts + [exponents], axis=0).astype(jnp.int32).astype(SENT)
    return [codes[:, i : i + LANES] for i in range(0, codes.shape[1], LANES)]


def put(ref, at, pieces):
    for piece in pieces:
        ref[at : at + PIECE, :] = piece
        at += PIECE


def decode(ref, at, width):
    pieces = [ref[at + i * PIECE : at + (i + 1) * PIECE, :] for i in range(width // LANES)]
    x = jnp.concatenate(pieces, axis=1).astype(jnp.int32).astype(F32)
    scales = jnp.exp2(x[4 * HEAD :]) * (1.0 / CODE)
    return x[: 2 * HEAD] * scales[0:1], x[2 * HEAD : 4 * HEAD] * scales[1:2]


def one_hot(order_row, tokens):
    high = order_row // LEAF
    low = (order_row - high * LEAF).astype(F32).astype(BF16)
    slots = iota((LEAF, LEAF), 0).astype(F32).astype(BF16)
    base = jnp.where(slots == low, jnp.ones((), BF16), jnp.zeros((), BF16))
    return jnp.concatenate([base * bits(high == j) for j in range(tokens // LEAF)], axis=0)


def pool_rows(group, first_row, rows):
    return bits(iota((rows, LEAF), 1) // group + first_row == iota((rows, LEAF), 0))


def level_shape(level, tokens):
    group = 2**level
    rows = tokens // group
    return group, max(min(rows, LEAF), LANES), max(rows // LEAF, 1)


def place(level, leaf, tokens):
    group, rows, _ = level_shape(level, tokens)
    per_leaf = LEAF // group
    return (leaf * per_leaf) // rows, (leaf * per_leaf) % rows


class Pool:
    def __init__(self, levels, tokens, turned=False):
        self.levels, self.tokens, self.turned = levels, tokens, turned
        self.whole = [level for level in levels if LEAF // 2**level % 16 == 0]
        parts = [pool_rows(2**level, 0, LEAF // 2**level) for level in self.whole]
        self.matrix = jnp.concatenate(parts, axis=0) if parts else None
        self.pieces, self.sums = {}, {}

    def add(self, leaf, values):
        if self.turned:
            both = lax.dot_general(
                self.matrix, values, (((1,), (1,)), ((), ())), preferred_element_type=F32
            )
            values = values.T
        else:
            both = dot(self.matrix, values) if self.whole else None
        at = 0
        for level in self.levels:
            block, first = place(level, leaf, self.tokens)
            if level in self.whole:
                count = LEAF // 2**level
                self.pieces.setdefault((level, block), {})[leaf] = both[at : at + count]
                at += count
            else:
                group, rows, _ = level_shape(level, self.tokens)
                piece = dot(pool_rows(group, first, rows), values)
                old = self.sums.get((level, block))
                self.sums[level, block] = piece if old is None else old + piece

    def get(self, level, block):
        if level not in self.whole:
            return self.sums[level, block]
        pieces = self.pieces[level, block]
        return jnp.concatenate([pieces[leaf] for leaf in sorted(pieces)], axis=0)


def mass(counts, first_leaf, leaves, group, rows):
    row = iota((16, rows), 1)
    per_leaf = LEAF // group
    leaf = row // per_leaf
    held = jnp.zeros(row.shape, jnp.int32)
    for n in range(leaves):
        held = jnp.where(leaf == n, counts[first_leaf + n], held)
    return jnp.clip(held - (row % per_leaf) * group, 0, group).astype(F32)


def valid_only(kv_rows, held):
    keep = bits(iota((LEAF, LANES), 0) < held)
    return kv_rows * jnp.concatenate([keep, keep], axis=1)


def near_marks(empty):
    return jnp.where((iota(empty.shape, 1) == 0) & empty, MASKED, 0.0).astype(BF16)


def far_keys(means, weight):
    hi, lo = split(means)
    mark = jnp.where((iota(weight.shape, 0) == 0) & (weight == 0.0), MASKED, 0.0).astype(BF16)
    rest = jnp.zeros((HEAD - 16, hi.shape[1]), BF16)
    out = []
    for h in range(2):
        here = slice(h * HEAD, (h + 1) * HEAD)
        out.append(
            jnp.concatenate([hi[here], lo[here], hi[here], mark, rest], axis=0).T
        )
    return out


def far_values(sums, mass_rows):
    hi, lo = split(sums)
    mass_rows = mass_rows.astype(BF16)
    return [
        jnp.concatenate([hi[h * HEAD : (h + 1) * HEAD], lo[h * HEAD : (h + 1) * HEAD], mass_rows], axis=0)
        for h in range(2)
    ]


def near_scores(k_window, mark, query):
    none = jnp.zeros((HEAD, LEAF), BF16)
    right = jnp.concatenate(
        [
            jnp.concatenate([query[:HEAD], none], axis=1),
            jnp.concatenate([none, query[HEAD:]], axis=1),
            bits(iota((LANES, 2 * LEAF), 0) == 0),
        ],
        axis=0,
    )
    left = jnp.concatenate([k_window, mark], axis=1)
    return [dot(left[i * LEAF : (i + 1) * LEAF], right) for i in range(3)]


def near(scores, v_window, h):
    scores = [piece[:, h * LEAF : (h + 1) * LEAF] for piece in scores]
    top = functools.reduce(jnp.maximum, [jnp.max(x, axis=0, keepdims=True) for x in scores])
    sums = totals = 0.0
    for i, piece in enumerate(scores):
        weights = jnp.exp2((piece - top) * SCALE)
        totals = totals + jnp.sum(weights, axis=0, keepdims=True)
        value = v_window[h * HEAD : (h + 1) * HEAD, i * LEAF : (i + 1) * LEAF]
        sums = sums + dot(value, weights.astype(BF16))
    return top * SCALE, sums, totals


def far_scores(keys, query):
    hi, lo = query[:HEAD], query[HEAD:]
    flag = bits(iota((HEAD, query.shape[1]), 0) == 0)
    return dot(keys, jnp.concatenate([hi, hi, lo, flag], axis=0))


def far(scores, value):
    top = jnp.max(scores, axis=0, keepdims=True).astype(BF16).astype(F32)
    w_hi, w_lo = split(jnp.exp2(scores - top))
    out = dot(jnp.concatenate([value, value], axis=1), jnp.concatenate([w_hi, w_lo], axis=0))
    return top, out[:HEAD] + out[HEAD : 2 * HEAD], out[2 * HEAD : 2 * HEAD + 1]


def staggered(units, ahead=1):
    held = []
    for first, second in units:
        held.append((second, first()))
        if len(held) > ahead:
            second, scores = held.pop(0)
            second(scores)
    for second, scores in held:
        second(scores)


def to_spread(term):
    top, sums, totals = term
    row = iota((16, sums.shape[1]), 0)
    t_hi, t_lo = split(totals)
    tail = jnp.where(row == 0, t_hi.astype(F32), jnp.where(row == 1, t_lo.astype(F32), top))
    hi, lo = split(sums)
    return jnp.concatenate([hi, lo, tail.astype(BF16)], axis=0)


def spread_matrix(times, first, width=LEAF):
    size = (LANES, width)
    return bits(iota(size, 0) == iota(size, 1) // times + first)


def from_spread(x):
    tail = x[2 * HEAD :]
    return tail[2:3], x[:HEAD] + x[HEAD : 2 * HEAD], tail[0:1] + tail[1:2]


def merge(terms):
    top = functools.reduce(jnp.maximum, [t[0] for t in terms])
    sums = totals = 0.0
    for t in terms:
        factor = jnp.exp2(t[0] - top)
        sums = sums + t[1] * factor
        totals = totals + t[2] * factor
    return top, sums, totals


def halo_rows():
    return LEAF // LANES * PIECE


def pack_rows(index, tokens, level):
    rows = level_shape(level, tokens)[1] // LANES * PIECE
    return rows + (halo_rows() if index == 0 else 0)


def key_kernel(
    tokens, remote, counts_in, order_in, k_in, v_in, kv_rows, v_cols, order, other, pair, *rest
):
    sums_out, (counts, k, v, sems) = rest[: len(remote) - 1], rest[len(remote) - 1 :]
    copies = [
        pltpu.make_async_copy(source, target, sems.at[i])
        for i, (source, target) in enumerate(
            ((order_in, order), (k_in, k), (v_in, v), (counts_in, counts))
        )
    ]
    for copy in copies:
        copy.start()
    rank = lax.axis_index("seq")
    leaves = tokens // LEAF
    copies[0].wait()
    first = one_hot(order[:, :LEAF], tokens)
    for copy in copies[1:]:
        copy.wait()
    joint = jnp.concatenate([k[...], v[...]], axis=0)
    odd = jnp.where(rank % 2 == 1, 1, 0)
    pool = Pool(remote, tokens)
    got = {}
    masked = {}

    def after(n):
        cols = slice(n * LEAF, (n + 1) * LEAF)
        masked[n] = valid_only(got[n].T, counts[rank * leaves + n])
        kv_rows[cols, :] = masked[n]
        v_cols[:, cols] = got[n][LANES:]

    def halos():
        low, high = got[0].astype(F32), got[leaves - 1].astype(F32)
        halo = jnp.where(odd == 1, low, high)
        put(pair, 0, encode(halo[:LANES], halo[LANES:]))
        other[...] = jnp.where(odd == 1, high, low).astype(BF16)

    for n in range(leaves):
        cols = slice(n * LEAF, (n + 1) * LEAF)
        got[n] = dot(joint, one_hot(order[:, cols], tokens) if n else first).astype(BF16)
        after(n)
    halos()
    for n in range(leaves):
        pool.add(n, masked[n])
    put(pair, halo_rows(), encode(*coarse_parts(counts, rank, remote[0], pool, tokens)))
    for ref, level in zip(sums_out, remote[1:]):
        means, sums = coarse_parts(counts, rank, level, pool, tokens)
        ref[:LANES, :] = means
        ref[LANES:, :] = sums


def pack_kernel(other, *rest):
    levels = len(rest) // 2
    sums, step, packs = rest[:levels], rest[levels], rest[levels + 1 :]
    halo = other[...].astype(F32)
    put(step, 0, encode(halo[:LANES], halo[LANES:]))
    for ref, x in zip(packs, sums):
        put(ref, 0, encode(x[:LANES, :], x[LANES:, :]))


def coarse_parts(counts, rank, level, pool, tokens):
    group, rows, _ = level_shape(level, tokens)
    leaves = tokens // LEAF
    weight = mass(counts, rank * leaves, leaves, group, rows)[:1]
    sums = pool.get(level, 0).T
    return sums[:LANES] / jnp.maximum(weight, 1.0), sums[LANES:]


def local_kernel(tokens, remote, counts_in, q, order, kv_rows, v_cols, q_cols, *rest):
    levels = len(remote)
    sums_out, stat_out, end_marks, matrices = rest[:4]
    queries_out, mass_out = rest[4 : 4 + levels], rest[4 + levels : 4 + 2 * levels]
    counts, sem, mark = rest[4 + 2 * levels :]
    copy = pltpu.make_async_copy(counts_in, counts, sem)
    copy.start()
    rank = lax.axis_index("seq")
    count = lax.axis_size("seq")
    leaves = tokens // LEAF
    first_leaf = rank * leaves
    near_terms = {}
    q_pool = Pool((1, 2) + tuple(remote), tokens, True)
    kv_pool = Pool((1, 2), tokens)
    for n in range(leaves):
        cols = slice(n * LEAF, (n + 1) * LEAF)
        got = dot(q[...], one_hot(order[:, cols], tokens)).astype(BF16)
        q_cols[:, cols] = got
    copy.wait()
    for n in range(leaves):
        rows = slice(n * LEAF, (n + 1) * LEAF)
        mark[rows, :] = near_marks(iota((LEAF, LANES), 0) >= counts[first_leaf + n])

    def near_unit(n):
        cols = slice(n * LEAF, (n + 1) * LEAF)
        window = slice((n - 1) * LEAF, (n + 2) * LEAF)

        def first():
            return near_scores(kv_rows[window, :LANES], mark[window, :], q_cols[:, cols])

        def second(scores):
            for h in range(2):
                near_terms[n, h] = near(scores, v_cols[:, window], h)

        return first, second

    for n in range(leaves):
        cols = slice(n * LEAF, (n + 1) * LEAF)
        q_pool.add(n, q_cols[:, cols])
    for n in range(leaves):
        cols = slice(n * LEAF, (n + 1) * LEAF)
        kv_pool.add(n, kv_rows[cols, :])


    def queries(level, block):
        hi, lo = split(q_pool.get(level, block).T * (SCALE / 2**level))
        return [
            jnp.concatenate([x[h * HEAD : (h + 1) * HEAD] for x in (hi, lo)], axis=0)
            for h in range(2)
        ]

    results = {}
    units = []
    for level in (2, 1):
        group, rows, blocks = level_shape(level, tokens)
        per_block = rows * group // LEAF
        for block in range(blocks):
            weight = mass(counts, first_leaf + block * per_block, per_block, group, rows)
            sums = kv_pool.get(level, block).T
            keys = far_keys(sums[:LANES] / jnp.maximum(weight[:1], 1.0), weight)
            values = far_values(sums[LANES:], weight)
            query = queries(level, block ^ 1)
            for h in range(2):

                def second(scores, at=(level, block ^ 1, h), value=values[h]):
                    results[at] = far(scores, value)

                units.append((functools.partial(far_scores, keys[h], query[h]), second))
    staggered([near_unit(n) for n in range(1, leaves - 1)])
    staggered(units, 4)
    for index, level in enumerate(remote):
        block = queries(level, 0)
        for h in range(2):
            queries_out[index][h] = block[h]
    twice = spread_matrix(2, 0)
    matrices[0] = twice
    for j in range(4):
        matrices[j + 1] = spread_matrix(8, j * 32)
    coarse = {at: to_spread(results[2, at[0], at[1]]) for at in ((b, h) for b in range(leaves // 4) for h in range(2))}
    fine = {}

    def join_unit(block, h):
        half = slice((block % 2) * LANES, (block % 2 + 1) * LANES)

        def second(x):
            fine[block, h] = to_spread(merge([results[1, block, h], from_spread(x)]))

        return functools.partial(dot, coarse[block // 2, h][:, half], twice), second

    def token_unit(n, h):
        cols = slice(n * LEAF, (n + 1) * LEAF)
        half = slice((n % 2) * LANES, (n % 2 + 1) * LANES)

        def second(x):
            term = from_spread(x)
            if 0 < n < leaves - 1:
                term = merge([near_terms[n, h], term])
            stat_out[h, 0:1, cols], sums_out[h, :, cols], stat_out[h, 1:2, cols] = term

        return (lambda: dot(fine[n // 2, h][:, half], twice)), second

    staggered([join_unit(block, h) for block in range(leaves // 2) for h in range(2)], 4)
    staggered([token_unit(n, h) for n in range(leaves) for h in range(2)], 4)

    row = iota((LEAF, LANES), 0)
    for side, leaf in ((0, first_leaf - 1), (1, first_leaf + leaves)):
        there = jnp.logical_and(leaf >= 0, leaf < count * leaves)
        held = jnp.where(there, counts[jnp.clip(leaf, 0, count * leaves - 1)], 0)
        end_marks[side, :LEAF] = near_marks(row >= held)
        for i in range(2):
            inner = first_leaf + side * (leaves - 2) + i
            end_marks[side, (i + 1) * LEAF : (i + 2) * LEAF] = near_marks(row >= counts[inner])
    for index, level in enumerate(remote):
        group, rows, _ = level_shape(level, tokens)
        for i in range(2**index):
            start = (rank ^ (2**index + i)) * leaves
            mass_out[index][:, i * rows : (i + 1) * rows] = mass(counts, start, leaves, group, rows)


def end_unit(tokens, side, halo, q_cols, kv_rows, v_cols, end_marks, keep):
    leaves = tokens // LEAF
    keys, values = [x.astype(BF16) for x in halo]
    inner = pl.ds(pl.multiple_of(side * ((leaves - 2) * LEAF), LEAF), 2 * LEAF)
    own = pl.ds(pl.multiple_of(side * ((leaves - 1) * LEAF), LEAF), LEAF)

    def first():
        return near_scores(
            jnp.concatenate([keys.T, kv_rows[inner, :][:, :LANES]], axis=0),
            end_marks[side],
            q_cols[:, own],
        )

    def second(scores):
        window = jnp.concatenate([values, v_cols[:, inner]], axis=1)
        for h in range(2):
            keep(h, near(scores, window, h))

    return first, second


def far_units(tokens, level, fields, queries, mass_rows, keep):
    means, sums = [jnp.concatenate(field, axis=1) for field in zip(*fields)]
    keys = far_keys(means, mass_rows[...])
    values = far_values(sums, mass_rows[...])
    units = []
    for h in range(2):

        def second(scores, h=h):
            keep(h, far(scores, values[h]))

        units.append((functools.partial(far_scores, keys[h], queries[h]), second))
    return units


def pair_kernel(
    tokens, level, q_cols, kv_rows, v_cols, end_marks, queries, mass_rows, pair,
    far_out, far_stat, end_out, end_stat
):
    side = 1 - lax.axis_index("seq") % 2

    def keeper(sums_ref, stat_ref):
        def keep(h, term):
            stat_ref[h, 0:1, :], sums_ref[h], stat_ref[h, 1:2, :] = term

        return keep

    rows = level_shape(level, tokens)[1]
    units = far_units(
        tokens, level, [decode(pair, halo_rows(), rows)], queries, mass_rows, keeper(far_out, far_stat)
    )
    units.append(
        end_unit(
            tokens, side, decode(pair, 0, LEAF), q_cols, kv_rows, v_cols, end_marks,
            keeper(end_out, end_stat),
        )
    )
    staggered(units, 2)


def last_kernel(
    tokens, remote, q_cols, kv_rows, v_cols, sums_in, stat_in, end_marks, matrices, *rest
):
    levels = len(remote)
    queries, mass_in = rest[: levels - 1], rest[levels - 1 : 2 * levels - 2]
    far_in, far_stat, end_in, end_stat, step = rest[2 * levels - 2 : 2 * levels + 3]
    packs = rest[2 * levels + 3 : -3]
    out, stage, sems = rest[-3:]
    odd = lax.axis_index("seq") % 2
    leaves = tokens // LEAF
    results = {}
    steps = {}
    for h in range(2):
        results[0, h] = (far_stat[h, 0:1, :], far_in[h], far_stat[h, 1:2, :])
    units = []
    for index in reversed(range(1, levels)):
        rows = level_shape(remote[index], tokens)[1]
        fields = [decode(packs[2**index - 2 + i], 0, rows) for i in range(2**index)]

        def keep(h, term, index=index):
            results[index, h] = term

        units += far_units(
            tokens, remote[index], fields, queries[index - 1], mass_in[index - 1], keep
        )
    units.append(
        end_unit(
            tokens, odd, decode(step, 0, LEAF), q_cols, kv_rows, v_cols, end_marks, steps.__setitem__
        )
    )
    staggered(units, 2)
    first_is_pair = jnp.where(odd == 1, 1, 0)
    ends = {}
    for h in range(2):
        pair_term = (end_stat[h, 0:1, :], end_in[h], end_stat[h, 1:2, :])
        for n, flag in ((0, first_is_pair), (leaves - 1, 1 - first_is_pair)):
            ends[n, h] = tuple(
                jnp.where(flag == 1, x, y) for x, y in zip(pair_term, steps[h])
            )

    coarse = []
    for h in range(2):
        merged = results[levels - 1, h]
        for index in reversed(range(levels - 1)):
            rows = level_shape(remote[index], tokens)[1]
            merged = merge(
                [results[index, h], from_spread(dot(to_spread(merged)[:, :LANES], matrices[0, :, :rows]))]
            )
        coarse.append(to_spread(merged))
    copies = []

    def token_unit(n, h):
        cols = slice(n * LEAF, (n + 1) * LEAF)
        half = slice(n // 4 * LANES, (n // 4 + 1) * LANES)

        def second(x):
            terms = [
                (stat_in[h, 0:1, cols], sums_in[h, :, cols], stat_in[h, 1:2, cols]),
                from_spread(x),
            ]
            if (n, h) in ends:
                terms.append(ends[n, h])
            _, sums, totals = merge(terms)
            stage[h, :, cols] = (sums * (1.0 / totals)).astype(BF16)
            if n % 2 and h:
                both = slice((n - 1) * LEAF, (n + 1) * LEAF)
                copies.append(
                    pltpu.make_async_copy(stage.at[:, :, both], out.at[:, :, both], sems.at[n // 2])
                )
                copies[-1].start()

        return functools.partial(dot, coarse[h][:, half], matrices[n % 4 + 1]), second

    staggered([token_unit(n, h) for n in range(leaves) for h in range(2)], 4)
    for copy in copies:
        copy.wait()


VMEM = pl.BlockSpec(memory_space=pltpu.VMEM)
ANY = pl.BlockSpec(memory_space=pl.ANY)


def params():
    return pltpu.CompilerParams(vmem_limit_bytes=48 * 2**20)


def step_pairs(count, heads):
    pairs = []
    for i in range(count):
        for h in range(heads):
            if 0 < i < count - 1:
                pairs.append((i * heads + h, (i + 1 if i % 2 else i - 1) * heads + h))
            else:
                pairs.append((i * heads + h, i * heads + (h ^ 1 if heads % 2 == 0 else h)))
    return pairs


def head_pair(q, k, v, order, counts):
    tokens = q.shape[2]
    leaves = tokens // LEAF
    count = lax.axis_size("seq")
    depth = (tokens * count // LEAF).bit_length() - 1
    remote = tuple(range(leaves.bit_length() - 1, depth))
    flat = (2 * HEAD, tokens)
    shape = jax.ShapeDtypeStruct
    widths = [level_shape(level, tokens)[1] for level in remote]
    sent = [shape((pack_rows(i, tokens, level), LANES), SENT) for i, level in enumerate(remote)]
    outs = [
        shape((tokens, 4 * HEAD), BF16),
        shape(flat, BF16),
        shape((1, tokens), jnp.int32),
        shape((2 * LANES, LEAF), BF16),
        sent[0],
    ] + [shape((2 * LANES, width), F32) for width in widths[1:]]
    counts, order, k, v = (
        pltpu.with_memory_space_constraint(x, pltpu.HBM)
        for x in (counts, order, k.reshape(flat), v.reshape(flat))
    )
    kv_rows, v_cols, order_here, other, pair, *sums = pl.pallas_call(
        functools.partial(key_kernel, tokens, remote),
        out_shape=outs,
        in_specs=[ANY] * 4,
        out_specs=[VMEM] * len(outs),
        scratch_shapes=[
            pltpu.SMEM(counts.shape, jnp.int32),
            pltpu.VMEM(flat, BF16),
            pltpu.VMEM(flat, BF16),
            pltpu.SemaphoreType.DMA((4,)),
        ],
        compiler_params=params(),
        cost_estimate=pl.CostEstimate(
            flops=2 * 256 * tokens * tokens, bytes_accessed=4 * 2**20, transcendentals=0
        ),
        name="gather_keys",
    )(counts, order, k, v)
    got_pair = lax.ppermute(pair, "seq", [(i, i ^ 1) for i in range(count)])

    outs = [shape((halo_rows(), LANES), SENT)] + sent[1:]
    step, *packs = pl.pallas_call(
        pack_kernel,
        out_shape=outs,
        in_specs=[VMEM] * len(remote),
        out_specs=[VMEM] * len(outs),
        compiler_params=params(),
        cost_estimate=pl.CostEstimate(flops=2**20, bytes_accessed=2**18, transcendentals=0),
        name="pack_rest",
    )(other, *sums)
    got = []
    for index in range(1, len(remote)):
        for partner in range(2**index, 2 ** (index + 1)):
            got.append(
                lax.ppermute(packs[index - 1], "seq", [(i, i ^ partner) for i in range(count)])
            )
    got_step = lax.ppermute(step, ("seq", "head"), step_pairs(count, lax.axis_size("head")))

    outs = (
        [shape(flat, BF16), shape((2, HEAD, tokens), F32), shape((2, 2, tokens), F32)]
        + [shape((2, 3 * LEAF, LANES), BF16), shape((5, LANES, LEAF), BF16)]
        + [shape((2, 2 * HEAD, width), BF16) for width in widths]
        + [shape((16, 2**i * width), F32) for i, width in enumerate(widths)]
    )
    q_cols, *local = pl.pallas_call(
        functools.partial(local_kernel, tokens, remote),
        out_shape=outs,
        in_specs=[ANY] + [VMEM] * 4,
        out_specs=[VMEM] * len(outs),
        scratch_shapes=[
            pltpu.SMEM(counts.shape, jnp.int32),
            pltpu.SemaphoreType.DMA(()),
            pltpu.VMEM((tokens, LANES), BF16),
        ],
        compiler_params=params(),
        cost_estimate=pl.CostEstimate(flops=2**31, bytes_accessed=2**16, transcendentals=0),
        name="local_attention",
    )(counts, q.reshape(flat), order_here, kv_rows, v_cols)
    sums, stat, end_marks, matrices = local[:4]
    queries, masses = local[4 : 4 + len(remote)], local[4 + len(remote) :]
    term = [shape((2, HEAD, LEAF), F32), shape((2, 2, LEAF), F32)]
    paired = pl.pallas_call(
        functools.partial(pair_kernel, tokens, remote[0]),
        out_shape=term + term,
        in_specs=[VMEM] * 7,
        out_specs=[VMEM] * 4,
        compiler_params=params(),
        cost_estimate=pl.CostEstimate(flops=2**28, bytes_accessed=2**20, transcendentals=2**19),
        name="pair_attention",
    )(q_cols, kv_rows, v_cols, end_marks, queries[0], masses[0], got_pair)
    last_args = [q_cols, kv_rows, v_cols, sums, stat, end_marks, matrices]
    last_args += [*queries[1:], *masses[1:], *paired, got_step, *got]
    return pl.pallas_call(
        functools.partial(last_kernel, tokens, remote),
        out_shape=shape((2, HEAD, tokens), BF16),
        in_specs=[VMEM] * len(last_args),
        out_specs=ANY,
        scratch_shapes=[
            pltpu.VMEM((2, HEAD, tokens), BF16),
            pltpu.SemaphoreType.DMA((leaves // 2,)),
        ],
        compiler_params=params(),
        cost_estimate=pl.CostEstimate(flops=2**30, bytes_accessed=4 * 2**20, transcendentals=2**20),
        name="remote_attention",
    )(*last_args)


def shards(q, k, v, order, counts):
    heads = q.shape[0]
    if heads % 2:
        q, k, v = (jnp.concatenate([x, jnp.zeros_like(x[:1])], axis=0) for x in (q, k, v))
    out = [
        head_pair(q[h : h + 2], k[h : h + 2], v[h : h + 2], order, counts)
        for h in range(0, q.shape[0], 2)
    ]
    out = out[0] if len(out) == 1 else jnp.concatenate(out, axis=0)
    return out[:heads] if heads % 2 else out


def solution(mesh):
    placed = (
        P("head", None, ("grp", "seq")),
        P("head", None, ("grp", "seq")),
        P("head", None, ("grp", "seq")),
        P(("grp", "seq"), None),
        P("grp"),
    )
    return jax.shard_map(
        shards,
        mesh=mesh,
        in_specs=placed,
        out_specs=P("head", None, ("grp", "seq")),
        check_vma=False,
    )
```
